32 devices in a mesh: dp: 8 (over z, x), tensor: 4 (over y, core).
Axes of the slice: x: 2, y: 2, z: 4, core: 2. Of those that a mesh axis runs over, the one named last changes fastest.
Arguments:
- tokens: bfloat16 [7680, 1024], P('dp'), may hold values from -6 to 6
- lengths: int32 [512], P('dp'), may hold values from 2 to 15
- query_weight: bfloat16 [1024, 1024], P(None, 'tensor'), may hold values from -0.1875 to 0.1875
- key_weight: bfloat16 [1024, 1024], P(None, 'tensor'), may hold values from -0.1875 to 0.1875
- value_weight: bfloat16 [1024, 1024], P(None, 'tensor'), may hold values from -0.1875 to 0.1875
- output_weight: bfloat16 [1024, 1024], P('tensor'), may hold values from -0.375 to 0.375
- up_weight: bfloat16 [1024, 2048], P(None, 'tensor'), may hold values from -0.1875 to 0.1875
- up_bias: bfloat16 [2048], P('tensor'), may hold values from -3 to 3
- down_weight: bfloat16 [2048, 1024], P('tensor'), may hold values from -0.25 to 0.25
- first_gain: bfloat16 [1024], replicated, may hold values from 0.5 to 1.5
- first_shift: bfloat16 [1024], replicated, may hold values from -3 to 3
- second_gain: bfloat16 [1024], replicated, may hold values from 0.5 to 1.5
- second_shift: bfloat16 [1024], replicated, may hold values from -3 to 3
- output_bias: bfloat16 [1024], replicated, may hold values from -3 to 3
- down_bias: bfloat16 [1024], replicated, may hold values from -3 to 3
- cotangent: bfloat16 [7680, 1024], P('dp'), may hold values from -12 to 12
Outputs:
- block_out: bfloat16 [7680, 1024], P('dp')
- token_grad: bfloat16 [7680, 1024], P('dp')
- query_grad: float32 [1024, 1024], P(None, 'tensor')
- key_grad: float32 [1024, 1024], P(None, 'tensor')
- value_grad: float32 [1024, 1024], P(None, 'tensor')
- output_grad: float32 [1024, 1024], P('tensor')
- up_grad: float32 [1024, 2048], P(None, 'tensor')
- up_bias_grad: float32 [2048], P('tensor')
- down_grad: float32 [2048, 1024], P('tensor')
- first_gain_grad: float32 [1024], replicated
- first_shift_grad: float32 [1024], replicated
- second_gain_grad: float32 [1024], replicated
- second_shift_grad: float32 [1024], replicated
- output_bias_grad: float32 [1024], replicated
- down_bias_grad: float32 [1024], replicated
The draws below stay inside these ranges and needn't reach their ends.
All inputs are finite; a program needn't handle non-finite values.
Results may differ from the reference program's by a relative error of at most 0.017.
Values may be sent and summed in bfloat16 or wider, within the bound.
A program may use at most 128 MiB of HBM per device.

```python
import math
import jax
import jax.numpy as jnp
from jax import lax

D = 1024
H = 8
DH = 128
FF = 2048
PATCHES = 15
SER_DEV = 64
SERIES = 512
TOKENS = 7680
N_DP = 8


def draw_cotangent(key, part):
    key = jax.random.fold_in(key, 7)
    rows = jnp.arange(TOKENS).astype(jnp.float32)[:, None]
    rising = 1.0 + 2.0 * rows / (TOKENS - 1)
    values = jax.random.normal(key, (TOKENS, D), jnp.float32) * rising
    return jnp.clip(values, -12.0, 12.0).astype(jnp.bfloat16)


def with_ends(array, own_key, least, largest):
    index_at = [jax.random.randint(jax.random.fold_in(own_key, axis), (), 0, length) for axis, length in enumerate(array.shape)]
    widest = array.shape.index(max(array.shape))
    neighbour = index_at[:widest] + [(index_at[widest] + 1) % array.shape[widest]] + index_at[widest + 1:]
    return array.at[tuple(index_at)].set(least).at[tuple(neighbour)].set(largest)


def steps_of(rng, extent, pieces, smallest, top_value):
    loudness = 1.0
    for dim, shards_of in pieces:
        draws = jax.random.uniform(jax.random.fold_in(jax.random.fold_in(rng, 6), dim), (shards_of,), jnp.float32, smallest / len(pieces), top_value / len(pieces))
        loudness = loudness * jnp.repeat(jnp.exp(draws), extent[dim] // shards_of).reshape((-1,) + (1,) * (len(extent) - 1 - dim))
    return loudness


def scatter_about(key, extent, scale, reach, cuts=(), kind=jnp.bfloat16):
    array = jax.random.normal(key, extent, jnp.float32) * scale
    if len(cuts) > 0:
        array = steps_of(key, extent, cuts, -0.22, 0.18) * array
    return jnp.clip(array, min=-reach, max=reach).astype(kind)


def setup_inputs(seed: int = 0) -> dict:
    key_list = jax.random.split(jax.random.key(seed), 17)
    return {
        "tokens": scatter_about(key_list[0], (TOKENS, D), 1.0, 6.0, ((0, 8),)),
        "lengths": with_ends(jax.random.randint(key_list[1], (SERIES,), 2, PATCHES + 1), jax.random.fold_in(key_list[1], 1), 2, PATCHES).astype(jnp.int32),
        "query_weight": scatter_about(key_list[2], (D, D), D ** -0.5, 0.1875, ((1, 4),)),
        "key_weight": scatter_about(key_list[3], (D, D), D ** -0.5, 0.1875, ((1, 4),)),
        "value_weight": scatter_about(key_list[4], (D, D), D ** -0.5, 0.1875, ((1, 4),)),
        "output_weight": scatter_about(key_list[5], (D, D), (D // 4) ** -0.5, 0.375, ((0, 4),)),
        "up_weight": scatter_about(key_list[6], (D, FF), D ** -0.5, 0.1875, ((1, 4),)),
        "up_bias": scatter_about(key_list[7], (FF,), 0.5, 3.0, ((0, 4),)),
        "down_weight": scatter_about(key_list[8], (FF, D), (FF // 4) ** -0.5, 0.25, ((0, 4),)),
        "first_gain": jnp.clip(1.0 + 0.1 * jax.random.normal(key_list[9], (D,), jnp.float32), 0.5, 1.5).astype(jnp.bfloat16),
        "first_shift": scatter_about(key_list[10], (D,), 0.5, 3.0),
        "second_gain": jnp.clip(1.0 + 0.1 * jax.random.normal(key_list[11], (D,), jnp.float32), 0.5, 1.5).astype(jnp.bfloat16),
        "second_shift": scatter_about(key_list[12], (D,), 0.5, 3.0),
        "output_bias": scatter_about(key_list[13], (D,), 0.5, 3.0),
        "down_bias": scatter_about(key_list[14], (D,), 0.5, 3.0),
        "cotangent": draw_cotangent(jax.random.fold_in(key_list[16], 71), 0),
    }


@jax.custom_vjp
def low(v):
    return lax.optimization_barrier(v.astype(jnp.bfloat16)).astype(jnp.float32)

@jax.custom_vjp
def low_back(v):
    return v

def low_keep(v):
    return (low(v), None)

def low_pass(kept, grad):
    return (grad,)

def back_keep(v):
    return (v, None)

def back_low(kept, grad):
    return (low(grad),)
low.defvjp(low_keep, low_pass)
low_back.defvjp(back_keep, back_low)
EPS = 1e-05
HIGH = lax.Precision.HIGHEST

def norm_rows(rows, gain, shift):
    row_mean = lax.optimization_barrier(jnp.mean(rows, axis=-1, keepdims=True))
    centred = rows - row_mean
    variance = lax.optimization_barrier(jnp.mean(centred * centred, axis=-1, keepdims=True))
    return centred * lax.rsqrt(variance + EPS) * gain + shift

def allowed_mask(lengths):
    position = jnp.arange(PATCHES, dtype=jnp.int32)
    start = (PATCHES - lengths)[:, None, None]
    query_pos = position[None, :, None]
    key_pos = position[None, None, :]
    return (key_pos >= start) & (key_pos <= query_pos) | (key_pos == query_pos)

def attend(block):
    queries, key_rows, value_rows, allowed = block
    raw = jnp.einsum('sqhd,skhd->shqk', queries, key_rows, precision=HIGH) * (1.0 / math.sqrt(DH))
    scores = jnp.where(allowed[:, None], low_back(raw), -1e+30)
    row_max = lax.optimization_barrier(jnp.max(scores, axis=-1, keepdims=True))
    numerator = jnp.exp(scores - row_max)
    probs = low(numerator / lax.optimization_barrier(jnp.sum(numerator, axis=-1, keepdims=True)))
    heads_out = jnp.einsum('shqk,skhd->sqhd', probs, value_rows, precision=HIGH)
    return low_back(low(heads_out))

def forward(tokens, query_weight, key_weight, value_weight, output_weight, up_weight, up_bias, down_weight, first_gain, first_shift, second_gain, second_shift, output_bias, down_bias, allowed):
    first_normed = low(norm_rows(tokens, first_gain, first_shift))
    queries = low_back(low(jnp.dot(first_normed, query_weight, precision=HIGH)))
    key_rows = low_back(low(jnp.dot(first_normed, key_weight, precision=HIGH)))
    value_rows = low_back(low(jnp.dot(first_normed, value_weight, precision=HIGH)))
    shape = (N_DP, SER_DEV, PATCHES, H, DH)
    heads_out = lax.map(jax.checkpoint(attend), (queries.reshape(shape), key_rows.reshape(shape), value_rows.reshape(shape), allowed.reshape(N_DP, SER_DEV, PATCHES, PATCHES)))
    heads_out = heads_out.reshape(TOKENS, D)
    residual = tokens + low_back(jnp.dot(heads_out, output_weight, precision=HIGH)) + output_bias
    second_normed = low(norm_rows(residual, second_gain, second_shift))
    up_pre = low_back(jnp.dot(second_normed, up_weight, precision=HIGH) + up_bias)
    activated = low(jax.nn.gelu(up_pre, approximate=False))
    return residual + low_back(jnp.dot(activated, down_weight, precision=HIGH)) + down_bias

def reference(tokens, lengths, query_weight, key_weight, value_weight, output_weight, up_weight, up_bias, down_weight, first_gain, first_shift, second_gain, second_shift, output_bias, down_bias, cotangent):
    allowed = allowed_mask(lengths)
    floats = [arr.astype(jnp.float32) for arr in (tokens, query_weight, key_weight, value_weight, output_weight, up_weight, up_bias, down_weight, first_gain, first_shift, second_gain, second_shift, output_bias, down_bias)]

    def wrapped(*params):
        return forward(*params, allowed)
    outputs, pullback = jax.vjp(wrapped, *floats)
    gradients = pullback(cotangent.astype(jnp.float32))
    return (outputs.astype(jnp.bfloat16), gradients[0].astype(jnp.bfloat16), gradients[1], gradients[2], gradients[3], gradients[4], gradients[5], gradients[6], gradients[7], gradients[8], gradients[9], gradients[10], gradients[11], gradients[12], gradients[13])
```

```python
import functools
import math

import jax
import jax.numpy as jnp
from jax import lax
from jax.experimental import pallas as pl
from jax.experimental.pallas import tpu as pltpu
from jax.sharding import PartitionSpec as P

DH = 128


EPS = 1e-05


def norm_parts(rows, gain, shift):
    row_mean = jnp.mean(rows, axis=-1, keepdims=True)
    centred = rows - row_mean
    inverse = lax.rsqrt(jnp.mean(centred * centred, axis=-1, keepdims=True) + EPS)
    scaled = centred * inverse
    return (scaled * gain + shift, scaled, inverse)


def norm_back(incoming, scaled, inverse, gain):
    weighted = incoming * gain
    return inverse * (
        weighted
        - jnp.mean(weighted, axis=-1, keepdims=True)
        - scaled * jnp.mean(weighted * scaled, axis=-1, keepdims=True)
    )


def allowed_mask(lengths, count):
    position = jnp.arange(count, dtype=jnp.int32)
    start = (count - lengths)[:, None, None]
    query_pos = position[None, :, None]
    key_pos = position[None, None, :]
    return (key_pos >= start) & (key_pos <= query_pos) | (key_pos == query_pos)


def gelu_exact(values):
    return jax.nn.gelu(values, approximate=False)


def plain_shards(
    tokens,
    lengths,
    query_weight,
    key_weight,
    value_weight,
    output_weight,
    up_weight,
    up_bias,
    down_weight,
    first_gain,
    first_shift,
    second_gain,
    second_shift,
    output_bias,
    down_bias,
    cotangent,
):
    tok_rows = tokens.shape[0]
    series = lengths.shape[0]
    count = tok_rows // series
    heads_here = query_weight.shape[1] // DH
    groups = lax.axis_size("tensor")
    share = tok_rows // groups
    begin = lax.axis_index("tensor") * share
    scale_factor = 1.0 / math.sqrt(DH)
    allowed = allowed_mask(lengths, count)[:, None]

    def share_rows(array):
        return lax.dynamic_slice_in_dim(array, begin, share, 0)

    def to_heads(array):
        return array.reshape(series, count, heads_here, DH)

    def masked_scores(query_four, key_four):
        raw = (
            jnp.einsum("sqhd,skhd->shqk", query_four, key_four, preferred_element_type=jnp.float32)
            * scale_factor
        )
        return jnp.where(allowed, raw, -1e30)

    inputs = tokens.astype(jnp.float32)
    gain_one = first_gain.astype(jnp.float32)
    gain_two = second_gain.astype(jnp.float32)
    first_normed, first_scaled, first_inverse = norm_parts(
        inputs, gain_one, first_shift.astype(jnp.float32)
    )
    first_low = first_normed.astype(jnp.bfloat16)
    queries = jnp.dot(first_low, query_weight, preferred_element_type=jnp.float32).astype(
        jnp.bfloat16
    )
    key_rows = jnp.dot(first_low, key_weight, preferred_element_type=jnp.float32).astype(
        jnp.bfloat16
    )
    value_rows = jnp.dot(first_low, value_weight, preferred_element_type=jnp.float32).astype(
        jnp.bfloat16
    )
    query_four = to_heads(queries)
    key_four = to_heads(key_rows)
    value_four = to_heads(value_rows)
    scores = masked_scores(query_four, key_four)
    row_max = jnp.max(scores, axis=-1, keepdims=True)
    numerator = jnp.exp(scores - row_max)
    row_total = jnp.sum(numerator, axis=-1, keepdims=True)
    log_total = row_max + jnp.log(row_total)
    probs_low = (numerator / row_total).astype(jnp.bfloat16)
    heads_out = jnp.einsum(
        "shqk,skhd->sqhd", probs_low, value_four, preferred_element_type=jnp.float32
    )
    heads_low = heads_out.astype(jnp.bfloat16).reshape(tok_rows, heads_here * DH)
    attn_part = jnp.dot(heads_low, output_weight, preferred_element_type=jnp.float32)
    bias_attn = output_bias.astype(jnp.float32)
    bias_down = down_bias.astype(jnp.float32)
    grad_output = cotangent.astype(jnp.float32)
    attn_share = lax.psum_scatter(attn_part, "tensor", scatter_dimension=0, tiled=True)
    residual_share = share_rows(inputs) + attn_share + bias_attn
    second_share, second_scaled, second_inverse = norm_parts(
        residual_share, gain_two, second_shift.astype(jnp.float32)
    )
    second_low = lax.all_gather(second_share.astype(jnp.bfloat16), "tensor", axis=0, tiled=True)
    up_pre = jnp.dot(second_low, up_weight, preferred_element_type=jnp.float32) + up_bias.astype(
        jnp.float32
    )
    activated, gelu_pull = jax.vjp(gelu_exact, up_pre)
    activated = activated.astype(jnp.bfloat16)
    down_part = jnp.dot(activated, down_weight, preferred_element_type=jnp.float32)
    down_share = lax.psum_scatter(
        down_part.astype(jnp.bfloat16), "tensor", scatter_dimension=0, tiled=True
    ).astype(jnp.float32)
    out_share = (residual_share + down_share + bias_down).astype(jnp.bfloat16)
    block_out = lax.all_gather(out_share, "tensor", axis=0, tiled=True)
    down_bias_part = jnp.sum(share_rows(grad_output), axis=0)
    down_grad = jnp.einsum("tf,td->fd", activated, cotangent, preferred_element_type=jnp.float32)
    activated_grad = jnp.einsum(
        "td,fd->tf", cotangent, down_weight, preferred_element_type=jnp.float32
    )
    up_grad_pre = gelu_pull(activated_grad)[0].astype(jnp.bfloat16)
    up_bias_grad = jnp.sum(up_grad_pre.astype(jnp.float32), axis=0)
    up_grad = jnp.einsum("td,tf->df", second_low, up_grad_pre, preferred_element_type=jnp.float32)
    second_part = jnp.einsum(
        "tf,df->td", up_grad_pre, up_weight, preferred_element_type=jnp.float32
    )
    second_grad_share = lax.psum_scatter(second_part, "tensor", scatter_dimension=0, tiled=True)
    residual_share_grad = share_rows(grad_output) + norm_back(
        second_grad_share, second_scaled, second_inverse, gain_two
    )
    second_gain_part = jnp.sum(second_grad_share * second_scaled, axis=0)
    second_shift_part = jnp.sum(second_grad_share, axis=0)
    output_bias_part = jnp.sum(residual_share_grad, axis=0)
    residual_low = lax.all_gather(
        residual_share_grad.astype(jnp.bfloat16), "tensor", axis=0, tiled=True
    )
    output_grad = jnp.einsum(
        "tc,td->cd", heads_low, residual_low, preferred_element_type=jnp.float32
    )
    heads_grad = jnp.einsum(
        "td,cd->tc", residual_low, output_weight, preferred_element_type=jnp.float32
    )
    heads_grad_four = to_heads(heads_grad.astype(jnp.bfloat16))
    probs_again = jnp.exp(masked_scores(query_four, key_four) - log_total)
    value_rows_grad = jnp.einsum(
        "shqk,sqhd->skhd", probs_low, heads_grad_four, preferred_element_type=jnp.float32
    ).astype(jnp.bfloat16)
    probs_grad = jnp.einsum(
        "sqhd,skhd->shqk", heads_grad_four, value_four, preferred_element_type=jnp.float32
    )
    inner_sum = jnp.sum(probs_again * probs_grad, axis=-1, keepdims=True)
    scores_grad = (probs_again * (probs_grad - inner_sum)).astype(jnp.bfloat16)
    queries_grad = (
        (
            jnp.einsum("shqk,skhd->sqhd", scores_grad, key_four, preferred_element_type=jnp.float32)
            * scale_factor
        )
        .astype(jnp.bfloat16)
        .reshape(tok_rows, heads_here * DH)
    )
    key_rows_grad = (
        (
            jnp.einsum(
                "shqk,sqhd->skhd", scores_grad, query_four, preferred_element_type=jnp.float32
            )
            * scale_factor
        )
        .astype(jnp.bfloat16)
        .reshape(tok_rows, heads_here * DH)
    )
    value_rows_grad = value_rows_grad.reshape(tok_rows, heads_here * DH)
    query_grad = jnp.einsum(
        "td,tc->dc", first_low, queries_grad, preferred_element_type=jnp.float32
    )
    key_grad = jnp.einsum("td,tc->dc", first_low, key_rows_grad, preferred_element_type=jnp.float32)
    value_grad = jnp.einsum(
        "td,tc->dc", first_low, value_rows_grad, preferred_element_type=jnp.float32
    )
    first_part = (
        jnp.einsum("tc,dc->td", queries_grad, query_weight, preferred_element_type=jnp.float32)
        + jnp.einsum("tc,dc->td", key_rows_grad, key_weight, preferred_element_type=jnp.float32)
        + jnp.einsum("tc,dc->td", value_rows_grad, value_weight, preferred_element_type=jnp.float32)
    )
    first_grad_share = lax.psum_scatter(
        first_part.astype(jnp.bfloat16), "tensor", scatter_dimension=0, tiled=True
    ).astype(jnp.float32)
    scaled_share = share_rows(first_scaled)
    token_share = residual_share_grad + norm_back(
        first_grad_share, scaled_share, share_rows(first_inverse), gain_one
    )
    token_grad = lax.all_gather(token_share.astype(jnp.bfloat16), "tensor", axis=0, tiled=True)
    first_gain_part = jnp.sum(first_grad_share * scaled_share, axis=0)
    first_shift_part = jnp.sum(first_grad_share, axis=0)
    query_grad, key_grad, value_grad, output_grad, up_grad, up_bias_grad, down_grad = (
        lax.psum(query_grad.astype(jnp.bfloat16), "dp").astype(jnp.float32),
        lax.psum(key_grad.astype(jnp.bfloat16), "dp").astype(jnp.float32),
        lax.psum(value_grad.astype(jnp.bfloat16), "dp").astype(jnp.float32),
        lax.psum(output_grad.astype(jnp.bfloat16), "dp").astype(jnp.float32),
        lax.psum(up_grad.astype(jnp.bfloat16), "dp").astype(jnp.float32),
        lax.psum(up_bias_grad.astype(jnp.bfloat16), "dp").astype(jnp.float32),
        lax.psum(down_grad.astype(jnp.bfloat16), "dp").astype(jnp.float32),
    )
    (
        first_gain_grad,
        first_shift_grad,
        second_gain_grad,
        second_shift_grad,
        output_bias_grad,
        down_bias_grad,
    ) = lax.psum(
        (
            first_gain_part,
            first_shift_part,
            second_gain_part,
            second_shift_part,
            output_bias_part,
            down_bias_part,
        ),
        ("dp", "tensor"),
    )
    return (
        block_out,
        token_grad,
        query_grad,
        key_grad,
        value_grad,
        output_grad,
        up_grad,
        up_bias_grad,
        down_grad,
        first_gain_grad,
        first_shift_grad,
        second_gain_grad,
        second_shift_grad,
        output_bias_grad,
        down_bias_grad,
    )


F32 = jnp.float32
BF16 = jnp.bfloat16
MESH = pl.DeviceIdType.MESH
SUB = 80
N_SEMS = 128


def dot(a, b):
    return jnp.dot(a, b, preferred_element_type=F32)


def dot_nt(a, b):
    return lax.dot_general(a, b, (((1,), (1,)), ((), ())), preferred_element_type=F32)


def dot_tn(a, b):
    return lax.dot_general(a, b, (((0,), (0,)), ((), ())), preferred_element_type=F32)


def span(start, size):
    return pl.ds(pl.multiple_of(start, 16), size)


def lanes(start, size):
    return pl.ds(pl.multiple_of(start, 128), size)


class Links:
    def __init__(self, sends, recvs, anyone):
        self.sends, self.recvs, self.anyone = sends, recvs, anyone
        self.used = 0

    def take(self, count=1):
        first = self.used
        self.used += count
        assert self.used <= N_SEMS
        return first

    def copy(self, src, dst, index, device):
        return pltpu.make_async_remote_copy(
            src_ref=src,
            dst_ref=dst,
            send_sem=self.sends.at[index],
            recv_sem=self.recvs.at[index],
            device_id=device,
            device_id_type=MESH,
        )

    def got(self, dst, index):
        self.copy(dst, dst, index, self.anyone).wait_recv()

    def sent(self, src, index):
        self.copy(src, src, index, self.anyone).wait_send()


def layer_kernel(
    count,
    tokens,
    lengths,
    query_weight,
    key_weight,
    value_weight,
    output_weight,
    up_weight,
    up_bias,
    down_weight,
    first_gain,
    first_shift,
    second_gain,
    second_shift,
    output_bias,
    down_bias,
    cotangent,
    block_out,
    token_grad,
    down_out,
    up_out,
    output_out,
    qkv_out,
    vec_out,
    first_low,
    queries,
    key_rows,
    value_rows,
    probs,
    heads_own,
    heads_full,
    wo_all,
    residual,
    second_low,
    act,
    ugp,
    mail,
    residual_grad,
    residual_low,
    dqkv,
    g_down,
    g_up,
    g_output,
    g_qkv,
    rx_down,
    rx_up,
    rx_output,
    rx_qkv,
    rz_down,
    rz_up,
    rz_output,
    rz_qkv,
    rm_down,
    rm_up,
    rm_output,
    rm_qkv,
    t_down,
    t_up,
    t_output,
    t_qkv,
    vec,
    vec_sib,
    vec_parts,
    vec_sum,
    vec_all,
    sends,
    recvs,
    local_sems,
):
    n_rows, width = tokens.shape
    half = n_rows // 2
    tile = 16 * count
    n_tiles = n_rows // tile
    half_tiles = n_tiles // 2
    heads_here = query_weight.shape[1] // DH
    cols = heads_here * DH
    hidden = up_weight.shape[1]
    scale_factor = 1.0 / math.sqrt(DH)

    dp = lax.axis_index("dp")
    t = lax.axis_index("tensor")
    x = dp % 2
    z = dp // 2
    c = t % 2
    t_sib = t + 1 - 2 * c
    t_opp = (t + 2) % 4
    t_diag = (t_sib + 2) % 4
    sib = (dp, t_sib)
    opp = (dp, t_opp)
    diag = (dp, t_diag)
    xp = (dp + 1 - 2 * x, t)
    adj = (dp + 2 - 4 * (z % 2), t)
    mid = ((3 - z) * 2 + x, t)
    is_mid = jnp.logical_or(z == 1, z == 2)
    is_end = jnp.logical_or(z == 0, z == 3)
    dp_peers = [((dp + k) % 8, t) for k in range(1, 8)]
    links = Links(sends, recvs, sib)

    barrier = pltpu.get_barrier_semaphore()
    for peer in [sib, opp, diag] + dp_peers:
        pl.semaphore_signal(barrier, inc=1, device_id=peer, device_id_type=MESH)

    def row(ref):
        return ref[...].astype(F32).reshape(1, ref.shape[0])

    own_start = c * half
    sib_start = (1 - c) * half

    def first_norm(i, _):
        rows = span(i * SUB, SUB)
        v = tokens[rows, :].astype(F32)
        e = v - jnp.mean(v, axis=-1, keepdims=True)
        r = lax.rsqrt(jnp.mean(e * e, axis=-1, keepdims=True) + EPS)
        first_low[rows, :] = (e * r * row(first_gain) + row(first_shift)).astype(BF16)
        return 0

    lax.fori_loop(0, n_rows // SUB, first_norm, 0)

    pl.semaphore_wait(barrier, 10)

    wo_rows = [span(v * cols, cols) for v in (t, t_sib, t_opp, t_diag)]
    wo_all[wo_rows[0], :] = output_weight[...]
    i_wo = links.take(3)
    wo_sends = [
        links.copy(output_weight, wo_all.at[wo_rows[0], :], i_wo, opp),
        links.copy(output_weight, wo_all.at[wo_rows[0], :], i_wo + 1, sib),
        links.copy(wo_all.at[wo_rows[2], :], wo_all.at[wo_rows[2], :], i_wo + 2, sib),
    ]
    wo_sends[0].start()
    wo_sends[1].start()

    def allowed_of(number):
        def series_of(index):
            return jnp.floor((index + 0.5) * (1.0 / count))

        row_at = lax.broadcasted_iota(jnp.int32, (tile, 1), 0).astype(F32)
        col_at = lax.broadcasted_iota(jnp.int32, (1, tile), 1).astype(F32)
        row_series, col_series = series_of(row_at), series_of(col_at)
        n_series = lengths.shape[0]
        which = lax.broadcasted_iota(jnp.int32, (n_series, tile), 0).astype(F32)
        here = (which == col_series + (number * 16).astype(F32)).astype(BF16)
        all_lengths = jnp.broadcast_to(
            lengths[...].astype(F32).reshape(1, n_series), (8, n_series)
        ).astype(BF16)
        length = dot(all_lengths, here)[0:1, :]
        live = (col_at - count * col_series) >= (count - length)
        same = row_series == col_series
        seen = jnp.logical_and(live, col_at <= row_at)
        return jnp.logical_and(same, jnp.logical_or(seen, col_at == row_at))

    i_heads = links.take(3 * half_tiles)

    def head_slot(j):
        return span(j * tile, tile)

    def attend(i, _):
        h, j = i % 2, i // 2
        number = h * half_tiles + j
        rows = span(number * tile, tile)
        normed = first_low[rows, :]
        q = dot(normed, query_weight[...]).astype(BF16)
        k = dot(normed, key_weight[...]).astype(BF16)
        v = dot(normed, value_weight[...]).astype(BF16)
        queries[rows, :] = q
        key_rows[rows, :] = k
        value_rows[rows, :] = v
        allowed = allowed_of(number)
        for head in range(heads_here):
            at = slice(head * DH, (head + 1) * DH)
            scores = jnp.where(allowed, dot_nt(q[:, at], k[:, at]) * scale_factor, -1e30)
            numerator = jnp.exp(scores - jnp.max(scores, axis=-1, keepdims=True))
            share = numerator / jnp.sum(numerator, axis=-1, keepdims=True)
            probs[number * heads_here + head] = share
            heads_own[rows, at] = dot(share.astype(BF16), v[:, at]).astype(BF16)
        slot = heads_full.at[head_slot(j), lanes(t * cols, cols)]

        @pl.when(h == c)
        def _():
            heads_full[head_slot(j), lanes(t * cols, cols)] = heads_own[rows, :]
            links.copy(heads_own.at[rows, :], slot, i_heads + j, opp).start()

        @pl.when(h != c)
        def _():
            links.copy(heads_own.at[rows, :], slot, i_heads + half_tiles + j, sib).start()
            links.copy(heads_own.at[rows, :], slot, i_heads + 2 * half_tiles + j, diag).start()

        return 0

    lax.fori_loop(0, n_tiles, attend, 0)

    links.got(wo_all.at[wo_rows[2], :], i_wo)
    wo_sends[2].start()
    links.got(wo_all.at[wo_rows[1], :], i_wo + 1)
    links.got(wo_all.at[wo_rows[3], :], i_wo + 2)

    i_second = links.take(half_tiles)

    def residual_stats(rows):
        v = residual[rows, :]
        e = v - jnp.mean(v, axis=-1, keepdims=True)
        r = lax.rsqrt(jnp.mean(e * e, axis=-1, keepdims=True) + EPS)
        return e * r, r

    def project(j, _):
        here = head_slot(j)
        for n, who in enumerate((t_opp, t_sib, t_diag)):
            links.got(heads_full.at[here, lanes(who * cols, cols)], i_heads + n * half_tiles + j)
        rows = span(own_start + j * tile, tile)
        residual[here, :] = (
            tokens[rows, :].astype(F32) + dot(heads_full[here, :], wo_all[...]) + row(output_bias)
        )

        def second_norm(s, _):
            local = span(j * tile + s * SUB, SUB)
            xhat, _r = residual_stats(local)
            second_low[span(own_start + j * tile + s * SUB, SUB), :] = (
                xhat * row(second_gain) + row(second_shift)
            ).astype(BF16)
            return 0

        lax.fori_loop(0, tile // SUB, second_norm, 0)
        links.copy(second_low.at[rows, :], second_low.at[rows, :], i_second + j, sib).start()
        return 0

    lax.fori_loop(0, half_tiles, project, 0)

    vec[...] = jnp.zeros_like(vec)

    def in_turn(i):
        return jnp.where(i % 2 == 0, own_start, sib_start) + (i // 2) * tile

    def feed(i, _):
        rows = span(in_turn(i), tile)

        @pl.when(i % 2 == 1)
        def _():
            links.got(second_low.at[rows, :], i_second + i // 2)

        u = dot(second_low[rows, :], up_weight[...]) + row(up_bias)
        big = 0.5 * (1.0 + lax.erf(u * (1.0 / math.sqrt(2.0))))
        act[rows, :] = (u * big).astype(BF16)
        slope = big + u * (jnp.exp(-0.5 * u * u) * (1.0 / math.sqrt(2.0 * math.pi)))
        grad = (dot_nt(cotangent[rows, :], down_weight[...]) * slope).astype(BF16)
        ugp[rows, :] = grad
        vec[6:7, 0:hidden] += jnp.sum(grad.astype(F32), axis=0, keepdims=True)
        return 0

    lax.fori_loop(0, n_tiles, feed, 0)

    class Sum:
        def __init__(self, grads, rx, rz, rm, total, out):
            self.grads, self.rx, self.rz, self.rm, self.total, self.out = (
                grads, rx, rz, rm, total, out,
            )
            self.size = grads.shape[0] // 2
            self.mine = span(x * self.size, self.size)
            self.other = span((1 - x) * self.size, self.size)
            self.index = links.take(5)

        def add(self, into, take):
            step = 32

            def body(i, _):
                at = span(i * step, step)
                own = span(x * self.size + i * step, step)
                into[at if into is self.total else own, :] = (
                    self.grads[own, :].astype(F32) + take[at, :].astype(F32)
                ).astype(BF16)
                return 0

            lax.fori_loop(0, self.size // step, body, 0)

        def to_x(self):
            links.copy(self.grads.at[self.other, :], self.rx, self.index, xp).start()

        def add_x(self):
            links.got(self.rx, self.index)
            self.add(self.grads, self.rx)

            @pl.when(is_end)
            def _():
                links.copy(self.grads.at[self.mine, :], self.rz, self.index + 1, adj).start()

        def add_z(self):
            @pl.when(is_mid)
            def _():
                links.got(self.rz, self.index + 1)
                self.add(self.grads, self.rz)
                links.copy(self.grads.at[self.mine, :], self.rm, self.index + 2, mid).start()

        def finish_z(self):
            @pl.when(is_mid)
            def _():
                links.got(self.rm, self.index + 2)
                self.add(self.total, self.rm)
                links.copy(self.total, self.total, self.index + 3, adj).start()
                links.copy(self.total, self.out.at[self.mine, :], self.index + 4, xp).start()

        def back_x(self):
            @pl.when(is_end)
            def _():
                links.got(self.total, self.index + 3)
                links.copy(self.total, self.out.at[self.mine, :], self.index + 4, xp).start()

        def write(self, sem):
            return pltpu.make_async_copy(self.total, self.out.at[self.mine, :], sem)

        def end(self):
            links.got(self.out.at[self.other, :], self.index + 4)
            links.sent(self.grads.at[self.other, :], self.index)

            @pl.when(is_end)
            def _():
                links.sent(self.grads.at[self.mine, :], self.index + 1)

            @pl.when(is_mid)
            def _():
                links.sent(self.grads.at[self.mine, :], self.index + 2)
                links.sent(self.total, self.index + 3)

            links.sent(self.total, self.index + 4)

    sum_down = Sum(g_down, rx_down, rz_down, rm_down, t_down, down_out)
    sum_up = Sum(g_up, rx_up, rz_up, rm_up, t_up, up_out)
    sum_output = Sum(g_output, rx_output, rz_output, rm_output, t_output, output_out)
    sum_qkv = Sum(g_qkv, rx_qkv, rz_qkv, rm_qkv, t_qkv, qkv_out)

    def down_grads(i, _):
        at = lanes(i * 256, 256)
        g_down[span(i * 256, 256), :] = dot_tn(act[:, at], cotangent[...]).astype(BF16)
        return 0

    lax.fori_loop(0, hidden // 256, down_grads, 0)
    sum_down.to_x()

    class RowSum:
        def __init__(self, number, part):
            self.snd, self.r1, self.cs, self.r2 = (mail.at[4 * number + n] for n in range(4))
            self.part = part
            self.index = links.take(2 * half_tiles)

        def start(self):
            def far(j, _):
                here = head_slot(j)
                self.snd[here, :] = self.part(span(sib_start + j * tile, tile)).astype(BF16)
                links.copy(self.snd.at[here, :], self.r1.at[here, :], self.index + j, sib).start()
                return 0

            def near(j, _):
                here = head_slot(j)
                mine = self.part(span(own_start + j * tile, tile))
                links.got(self.r1.at[here, :], self.index + j)
                self.cs[here, :] = (mine + self.r1[here, :].astype(F32)).astype(BF16)
                links.copy(
                    self.cs.at[here, :], self.r2.at[here, :], self.index + half_tiles + j, opp
                ).start()
                return 0

            lax.fori_loop(0, half_tiles, far, 0)
            lax.fori_loop(0, half_tiles, near, 0)

        def wait(self, j):
            links.got(self.r2.at[head_slot(j), :], self.index + half_tiles + j)

        def rows(self, local):
            return self.cs[local, :].astype(F32) + self.r2[local, :].astype(F32)

        def end(self):
            def body(j, _):
                here = head_slot(j)
                links.sent(self.snd.at[here, :], self.index + j)
                links.sent(self.cs.at[here, :], self.index + half_tiles + j)
                return 0

            lax.fori_loop(0, half_tiles, body, 0)

    second_sum = RowSum(0, lambda rows: dot_nt(ugp[rows, :], up_weight[...]))
    second_sum.start()

    def up_grads(i, _):
        at = lanes(i * 256, 256)
        g_up[span(i * 256, 256), :] = dot_tn(second_low[:, at], ugp[...]).astype(BF16)
        return 0

    lax.fori_loop(0, width // 256, up_grads, 0)
    sum_up.to_x()

    out_sum = RowSum(1, lambda rows: dot(act[rows, :], down_weight[...]))
    out_sum.start()

    i_back = links.take(half_tiles)

    def add_to(at, value):
        vec[at : at + 1, :] += jnp.sum(value, axis=0, keepdims=True)

    def norm_back(incoming, xhat, r, gain):
        weighted = incoming * gain
        return r * (
            weighted
            - jnp.mean(weighted, axis=-1, keepdims=True)
            - xhat * jnp.mean(weighted * xhat, axis=-1, keepdims=True)
        )

    def second_back(j, _):
        second_sum.wait(j)

        def body(s, _):
            local = span(j * tile + s * SUB, SUB)
            rows = span(own_start + j * tile + s * SUB, SUB)
            incoming = second_sum.rows(local)
            xhat, r = residual_stats(local)
            given = cotangent[rows, :].astype(F32)
            grad = given + norm_back(incoming, xhat, r, row(second_gain))
            residual_grad[local, :] = grad
            residual_low[rows, :] = grad.astype(BF16)
            add_to(2, incoming * xhat)
            add_to(3, incoming)
            add_to(4, grad)
            add_to(5, given)
            return 0

        lax.fori_loop(0, tile // SUB, body, 0)
        rows = span(own_start + j * tile, tile)
        links.copy(residual_low.at[rows, :], residual_low.at[rows, :], i_back + j, sib).start()
        return 0

    lax.fori_loop(0, half_tiles, second_back, 0)

    sum_down.add_x()
    sum_up.add_x()

    def attend_back(i, _):
        start = in_turn(i)
        rows = span(start, tile)
        number = start // tile

        @pl.when(i % 2 == 1)
        def _():
            links.got(residual_low.at[rows, :], i_back + i // 2)

        grads = dot_nt(residual_low[rows, :], output_weight[...]).astype(BF16)
        for head in range(heads_here):
            at = slice(head * DH, (head + 1) * DH)
            share = probs[number * heads_here + head]
            q, k, v = queries[rows, at], key_rows[rows, at], value_rows[rows, at]
            share_grad = dot_nt(grads[:, at], v)
            inner = jnp.sum(share * share_grad, axis=-1, keepdims=True)
            scores_grad = (share * (share_grad - inner)).astype(BF16)
            dqkv[rows, head * DH : (head + 1) * DH] = (
                dot(scores_grad, k) * scale_factor
            ).astype(BF16)
            dqkv[rows, cols + head * DH : cols + (head + 1) * DH] = (
                dot_tn(scores_grad, q) * scale_factor
            ).astype(BF16)
            dqkv[rows, 2 * cols + head * DH : 2 * cols + (head + 1) * DH] = dot_tn(
                share.astype(BF16), grads[:, at]
            ).astype(BF16)
        return 0

    lax.fori_loop(0, n_tiles, attend_back, 0)

    sum_down.add_z()

    first_sum = RowSum(
        2,
        lambda rows: dot_nt(dqkv[rows, 0:cols], query_weight[...])
        + dot_nt(dqkv[rows, cols : 2 * cols], key_weight[...])
        + dot_nt(dqkv[rows, 2 * cols : 3 * cols], value_weight[...]),
    )
    first_sum.start()

    g_output[...] = dot_tn(heads_own[...], residual_low[...]).astype(BF16)
    sum_output.to_x()

    def qkv_grads(i, _):
        at = lanes(i * 256, 256)
        g_qkv[span(i * 256, 256), :] = dot_tn(first_low[:, at], dqkv[...]).astype(BF16)
        return 0

    lax.fori_loop(0, width // 256, qkv_grads, 0)
    sum_qkv.to_x()

    sum_up.add_z()
    sum_down.finish_z()
    sum_output.add_x()

    own_rows = span(own_start, half)
    other_rows = span(sib_start, half)
    i_out = links.take(2)
    out_rows = mail.at[4]
    token_rows = mail.at[8]

    def finish_out(j, _):
        out_sum.wait(j)

        def body(s, _):
            local = span(j * tile + s * SUB, SUB)
            out_rows[local, :] = (
                residual[local, :] + out_sum.rows(local) + row(down_bias)
            ).astype(BF16)
            return 0

        lax.fori_loop(0, tile // SUB, body, 0)
        return 0

    def wait_far(j, _):
        here = head_slot(j)
        links.sent(out_sum.snd.at[here, :], out_sum.index + j)
        links.sent(first_sum.snd.at[here, :], first_sum.index + j)
        return 0

    lax.fori_loop(0, half_tiles, wait_far, 0)
    lax.fori_loop(0, half_tiles, finish_out, 0)
    out_send = links.copy(out_rows, block_out.at[own_rows, :], i_out, sib)
    out_send.start()
    out_write = pltpu.make_async_copy(out_rows, block_out.at[own_rows, :], local_sems.at[0])
    out_write.start()

    sum_up.finish_z()
    sum_down.back_x()
    sum_output.add_z()
    sum_qkv.add_x()

    def first_back(j, _):
        first_sum.wait(j)

        def body(s, _):
            local = span(j * tile + s * SUB, SUB)
            rows = span(own_start + j * tile + s * SUB, SUB)
            incoming = first_sum.rows(local)
            v = tokens[rows, :].astype(F32)
            e = v - jnp.mean(v, axis=-1, keepdims=True)
            r = lax.rsqrt(jnp.mean(e * e, axis=-1, keepdims=True) + EPS)
            xhat = e * r
            token_rows[local, :] = (
                residual_grad[local, :] + norm_back(incoming, xhat, r, row(first_gain))
            ).astype(BF16)
            add_to(0, incoming * xhat)
            add_to(1, incoming)
            return 0

        lax.fori_loop(0, tile // SUB, body, 0)
        return 0

    lax.fori_loop(0, half_tiles, first_back, 0)
    token_send = links.copy(token_rows, token_grad.at[own_rows, :], i_out + 1, sib)
    token_send.start()
    token_write = pltpu.make_async_copy(token_rows, token_grad.at[own_rows, :], local_sems.at[1])
    token_write.start()

    i_vec = links.take(1 + 2 * 7)
    vec_send = links.copy(vec, vec_sib, i_vec, sib)
    vec_send.start()

    sum_qkv.add_z()
    sum_output.finish_z()
    sum_up.back_x()

    links.got(vec_sib, i_vec)
    vec_send.wait_send()
    at_row = lax.broadcasted_iota(jnp.int32, vec.shape, 0)
    vec[...] = vec[...] + jnp.where(at_row < 6, vec_sib[...], 0.0)
    part = width // 8
    vec_parts[dp] = vec[:, lanes(dp * part, part)]
    part_sends = []
    for k, peer in enumerate(dp_peers):
        send = links.copy(
            vec.at[:, lanes(peer[0] * part, part)], vec_parts.at[dp], i_vec + 1 + k, peer
        )
        send.start()
        part_sends.append(send)

    sum_qkv.finish_z()
    sum_output.back_x()

    for k in range(7):
        links.got(vec_parts.at[(dp + 7 - k) % 8], i_vec + 1 + k)
    total = vec_parts[0]
    for k in range(1, 8):
        total = total + vec_parts[k]
    vec_sum[...] = total
    vec_all[:, lanes(dp * part, part)] = total
    for k, peer in enumerate(dp_peers):
        send = links.copy(
            vec_sum, vec_all.at[:, lanes(dp * part, part)], i_vec + 8 + k, peer
        )
        send.start()
        part_sends.append(send)

    sum_qkv.back_x()

    writes = []
    for n, each in enumerate((sum_down, sum_up, sum_output, sum_qkv)):
        write = each.write(local_sems.at[2 + n])
        write.start()
        writes.append(write)

    for k in range(7):
        links.got(vec_all.at[:, lanes(((dp + 7 - k) % 8) * part, part)], i_vec + 8 + k)
    vec_out[...] = vec_all[...]

    for each in (sum_down, sum_up, sum_output, sum_qkv):
        each.end()
    for write in writes + [out_write, token_write]:
        write.wait()
    for send in wo_sends + part_sends + [out_send, token_send]:
        send.wait_send()
    links.got(block_out.at[other_rows, :], i_out)
    links.got(token_grad.at[other_rows, :], i_out + 1)

    def last_waits(j, _):
        here = head_slot(j)
        rows = span(own_start + j * tile, tile)
        far_rows = span(sib_start + j * tile, tile)
        links.sent(heads_own.at[rows, :], i_heads + j)
        links.sent(heads_own.at[far_rows, :], i_heads + half_tiles + j)
        links.sent(heads_own.at[far_rows, :], i_heads + 2 * half_tiles + j)
        links.sent(second_low.at[rows, :], i_second + j)
        links.sent(residual_low.at[rows, :], i_back + j)
        links.sent(second_sum.snd.at[here, :], second_sum.index + j)
        for each in (second_sum, out_sum, first_sum):
            links.sent(each.cs.at[here, :], each.index + half_tiles + j)
        return 0

    lax.fori_loop(0, half_tiles, last_waits, 0)


def kernel_shards(*args):
    tokens, lengths = args[0], args[1]
    n_rows, width = tokens.shape
    count = n_rows // lengths.shape[0]
    tile = 16 * count
    half = n_rows // 2
    cols = args[2].shape[1]
    hidden = args[6].shape[1]
    vmem = pltpu.VMEM
    grads = ((hidden, width), (width, hidden), (cols, width), (width, 3 * cols))
    halves = [(r // 2, n) for r, n in grads]
    any_space = pl.BlockSpec(memory_space=pl.ANY)
    in_vmem = pl.BlockSpec(memory_space=pltpu.VMEM)
    scratch = [
        vmem((n_rows, width), BF16),
        vmem((n_rows, cols), BF16),
        vmem((n_rows, cols), BF16),
        vmem((n_rows, cols), BF16),
        vmem((n_rows // tile * (cols // DH), tile, tile), F32),
        vmem((n_rows, cols), BF16),
        vmem((half, width), BF16),
        vmem((width, width), BF16),
        vmem((half, width), F32),
        vmem((n_rows, width), BF16),
        vmem((n_rows, hidden), BF16),
        vmem((n_rows, hidden), BF16),
        vmem((12, half, width), BF16),
        vmem((half, width), F32),
        vmem((n_rows, width), BF16),
        vmem((n_rows, 3 * cols), BF16),
    ]
    scratch += [vmem(s, BF16) for s in grads]
    for _ in range(4):
        scratch += [vmem(s, BF16) for s in halves]
    scratch += [
        vmem((8, width), F32),
        vmem((8, width), F32),
        vmem((8, 8, width // 8), F32),
        vmem((8, width // 8), F32),
        vmem((8, width), F32),
        pltpu.SemaphoreType.DMA((N_SEMS,)),
        pltpu.SemaphoreType.DMA((N_SEMS,)),
        pltpu.SemaphoreType.DMA((8,)),
    ]
    block_out, token_grad, down, up, output, qkv, vec = pl.pallas_call(
        functools.partial(layer_kernel, count),
        out_shape=[
            jax.ShapeDtypeStruct((n_rows, width), BF16),
            jax.ShapeDtypeStruct((n_rows, width), BF16),
            *[jax.ShapeDtypeStruct(s, BF16) for s in grads],
            jax.ShapeDtypeStruct((8, width), F32),
        ],
        in_specs=[in_vmem] * len(args),
        out_specs=[any_space] * 6 + [in_vmem],
        scratch_shapes=scratch,
        compiler_params=pltpu.CompilerParams(
            collective_id=0, has_side_effects=True, vmem_limit_bytes=63 * 2**20
        ),
        name="layer",
    )(*args)
    return (
        block_out,
        token_grad,
        qkv[:, 0:cols].astype(F32),
        qkv[:, cols : 2 * cols].astype(F32),
        qkv[:, 2 * cols :].astype(F32),
        output.astype(F32),
        up.astype(F32),
        vec[6, 0:hidden],
        down.astype(F32),
        vec[0],
        vec[1],
        vec[2],
        vec[3],
        vec[4],
        vec[5],
    )


def solution(mesh):
    fits = mesh.shape["dp"] == 8 and mesh.shape["tensor"] == 4
    return jax.shard_map(
        kernel_shards if fits else plain_shards,
        mesh=mesh,
        in_specs=(
            P("dp", None),
            P("dp"),
            P(None, "tensor"),
            P(None, "tensor"),
            P(None, "tensor"),
            P("tensor", None),
            P(None, "tensor"),
            P("tensor"),
            P("tensor", None),
            P(),
            P(),
            P(),
            P(),
            P(),
            P(),
            P("dp", None),
        ),
        out_specs=(
            P("dp", None),
            P("dp", None),
            P(None, "tensor"),
            P(None, "tensor"),
            P(None, "tensor"),
            P("tensor", None),
            P(None, "tensor"),
            P("tensor"),
            P("tensor", None),
            P(),
            P(),
            P(),
            P(),
            P(),
            P(),
        ),
        check_vma=False,
    )
```

```python
import functools
import math

import jax
import jax.numpy as jnp
from jax import lax
from jax.experimental import pallas as pl
from jax.experimental.pallas import tpu as pltpu
from jax.sharding import PartitionSpec as P

DH = 128


EPS = 1e-05


def norm_parts(rows, gain, shift):
    row_mean = jnp.mean(rows, axis=-1, keepdims=True)
    centred = rows - row_mean
    inverse = lax.rsqrt(jnp.mean(centred * centred, axis=-1, keepdims=True) + EPS)
    scaled = centred * inverse
    return (scaled * gain + shift, scaled, inverse)


def norm_back(incoming, scaled, inverse, gain):
    weighted = incoming * gain
    return inverse * (
        weighted
        - jnp.mean(weighted, axis=-1, keepdims=True)
        - scaled * jnp.mean(weighted * scaled, axis=-1, keepdims=True)
    )


def allowed_mask(lengths, count):
    position = jnp.arange(count, dtype=jnp.int32)
    start = (count - lengths)[:, None, None]
    query_pos = position[None, :, None]
    key_pos = position[None, None, :]
    return (key_pos >= start) & (key_pos <= query_pos) | (key_pos == query_pos)


def gelu_exact(values):
    return jax.nn.gelu(values, approximate=False)


def plain_shards(
    tokens,
    lengths,
    query_weight,
    key_weight,
    value_weight,
    output_weight,
    up_weight,
    up_bias,
    down_weight,
    first_gain,
    first_shift,
    second_gain,
    second_shift,
    output_bias,
    down_bias,
    cotangent,
):
    tok_rows = tokens.shape[0]
    series = lengths.shape[0]
    count = tok_rows // series
    heads_here = query_weight.shape[1] // DH
    groups = lax.axis_size("tensor")
    share = tok_rows // groups
    begin = lax.axis_index("tensor") * share
    scale_factor = 1.0 / math.sqrt(DH)
    allowed = allowed_mask(lengths, count)[:, None]

    def share_rows(array):
        return lax.dynamic_slice_in_dim(array, begin, share, 0)

    def to_heads(array):
        return array.reshape(series, count, heads_here, DH)

    def masked_scores(query_four, key_four):
        raw = (
            jnp.einsum("sqhd,skhd->shqk", query_four, key_four, preferred_element_type=jnp.float32)
            * scale_factor
        )
        return jnp.where(allowed, raw, -1e30)

    inputs = tokens.astype(jnp.float32)
    gain_one = first_gain.astype(jnp.float32)
    gain_two = second_gain.astype(jnp.float32)
    first_normed, first_scaled, first_inverse = norm_parts(
        inputs, gain_one, first_shift.astype(jnp.float32)
    )
    first_low = first_normed.astype(jnp.bfloat16)
    queries = jnp.dot(first_low, query_weight, preferred_element_type=jnp.float32).astype(
        jnp.bfloat16
    )
    key_rows = jnp.dot(first_low, key_weight, preferred_element_type=jnp.float32).astype(
        jnp.bfloat16
    )
    value_rows = jnp.dot(first_low, value_weight, preferred_element_type=jnp.float32).astype(
        jnp.bfloat16
    )
    query_four = to_heads(queries)
    key_four = to_heads(key_rows)
    value_four = to_heads(value_rows)
    scores = masked_scores(query_four, key_four)
    row_max = jnp.max(scores, axis=-1, keepdims=True)
    numerator = jnp.exp(scores - row_max)
    row_total = jnp.sum(numerator, axis=-1, keepdims=True)
    log_total = row_max + jnp.log(row_total)
    probs_low = (numerator / row_total).astype(jnp.bfloat16)
    heads_out = jnp.einsum(
        "shqk,skhd->sqhd", probs_low, value_four, preferred_element_type=jnp.float32
    )
    heads_low = heads_out.astype(jnp.bfloat16).reshape(tok_rows, heads_here * DH)
    attn_part = jnp.dot(heads_low, output_weight, preferred_element_type=jnp.float32)
    bias_attn = output_bias.astype(jnp.float32)
    bias_down = down_bias.astype(jnp.float32)
    grad_output = cotangent.astype(jnp.float32)
    attn_share = lax.psum_scatter(attn_part, "tensor", scatter_dimension=0, tiled=True)
    residual_share = share_rows(inputs) + attn_share + bias_attn
    second_share, second_scaled, second_inverse = norm_parts(
        residual_share, gain_two, second_shift.astype(jnp.float32)
    )
    second_low = lax.all_gather(second_share.astype(jnp.bfloat16), "tensor", axis=0, tiled=True)
    up_pre = jnp.dot(second_low, up_weight, preferred_element_type=jnp.float32) + up_bias.astype(
        jnp.float32
    )
    activated, gelu_pull = jax.vjp(gelu_exact, up_pre)
    activated = activated.astype(jnp.bfloat16)
    down_part = jnp.dot(activated, down_weight, preferred_element_type=jnp.float32)
    down_share = lax.psum_scatter(
        down_part.astype(jnp.bfloat16), "tensor", scatter_dimension=0, tiled=True
    ).astype(jnp.float32)
    out_share = (residual_share + down_share + bias_down).astype(jnp.bfloat16)
    block_out = lax.all_gather(out_share, "tensor", axis=0, tiled=True)
    down_bias_part = jnp.sum(share_rows(grad_output), axis=0)
    down_grad = jnp.einsum("tf,td->fd", activated, cotangent, preferred_element_type=jnp.float32)
    activated_grad = jnp.einsum(
        "td,fd->tf", cotangent, down_weight, preferred_element_type=jnp.float32
    )
    up_grad_pre = gelu_pull(activated_grad)[0].astype(jnp.bfloat16)
    up_bias_grad = jnp.sum(up_grad_pre.astype(jnp.float32), axis=0)
    up_grad = jnp.einsum("td,tf->df", second_low, up_grad_pre, preferred_element_type=jnp.float32)
    second_part = jnp.einsum(
        "tf,df->td", up_grad_pre, up_weight, preferred_element_type=jnp.float32
    )
    second_grad_share = lax.psum_scatter(second_part, "tensor", scatter_dimension=0, tiled=True)
    residual_share_grad = share_rows(grad_output) + norm_back(
        second_grad_share, second_scaled, second_inverse, gain_two
    )
    second_gain_part = jnp.sum(second_grad_share * second_scaled, axis=0)
    second_shift_part = jnp.sum(second_grad_share, axis=0)
    output_bias_part = jnp.sum(residual_share_grad, axis=0)
    residual_low = lax.all_gather(
        residual_share_grad.astype(jnp.bfloat16), "tensor", axis=0, tiled=True
    )
    output_grad = jnp.einsum(
        "tc,td->cd", heads_low, residual_low, preferred_element_type=jnp.float32
    )
    heads_grad = jnp.einsum(
        "td,cd->tc", residual_low, output_weight, preferred_element_type=jnp.float32
    )
    heads_grad_four = to_heads(heads_grad.astype(jnp.bfloat16))
    probs_again = jnp.exp(masked_scores(query_four, key_four) - log_total)
    value_rows_grad = jnp.einsum(
        "shqk,sqhd->skhd", probs_low, heads_grad_four, preferred_element_type=jnp.float32
    ).astype(jnp.bfloat16)
    probs_grad = jnp.einsum(
        "sqhd,skhd->shqk", heads_grad_four, value_four, preferred_element_type=jnp.float32
    )
    inner_sum = jnp.sum(probs_again * probs_grad, axis=-1, keepdims=True)
    scores_grad = (probs_again * (probs_grad - inner_sum)).astype(jnp.bfloat16)
    queries_grad = (
        (
            jnp.einsum("shqk,skhd->sqhd", scores_grad, key_four, preferred_element_type=jnp.float32)
            * scale_factor
        )
        .astype(jnp.bfloat16)
        .reshape(tok_rows, heads_here * DH)
    )
    key_rows_grad = (
        (
            jnp.einsum(
                "shqk,sqhd->skhd", scores_grad, query_four, preferred_element_type=jnp.float32
            )
            * scale_factor
        )
        .astype(jnp.bfloat16)
        .reshape(tok_rows, heads_here * DH)
    )
    value_rows_grad = value_rows_grad.reshape(tok_rows, heads_here * DH)
    query_grad = jnp.einsum(
        "td,tc->dc", first_low, queries_grad, preferred_element_type=jnp.float32
    )
    key_grad = jnp.einsum("td,tc->dc", first_low, key_rows_grad, preferred_element_type=jnp.float32)
    value_grad = jnp.einsum(
        "td,tc->dc", first_low, value_rows_grad, preferred_element_type=jnp.float32
    )
    first_part = (
        jnp.einsum("tc,dc->td", queries_grad, query_weight, preferred_element_type=jnp.float32)
        + jnp.einsum("tc,dc->td", key_rows_grad, key_weight, preferred_element_type=jnp.float32)
        + jnp.einsum("tc,dc->td", value_rows_grad, value_weight, preferred_element_type=jnp.float32)
    )
    first_grad_share = lax.psum_scatter(
        first_part.astype(jnp.bfloat16), "tensor", scatter_dimension=0, tiled=True
    ).astype(jnp.float32)
    scaled_share = share_rows(first_scaled)
    token_share = residual_share_grad + norm_back(
        first_grad_share, scaled_share, share_rows(first_inverse), gain_one
    )
    token_grad = lax.all_gather(token_share.astype(jnp.bfloat16), "tensor", axis=0, tiled=True)
    first_gain_part = jnp.sum(first_grad_share * scaled_share, axis=0)
    first_shift_part = jnp.sum(first_grad_share, axis=0)
    query_grad, key_grad, value_grad, output_grad, up_grad, up_bias_grad, down_grad = (
        lax.psum(query_grad.astype(jnp.bfloat16), "dp").astype(jnp.float32),
        lax.psum(key_grad.astype(jnp.bfloat16), "dp").astype(jnp.float32),
        lax.psum(value_grad.astype(jnp.bfloat16), "dp").astype(jnp.float32),
        lax.psum(output_grad.astype(jnp.bfloat16), "dp").astype(jnp.float32),
        lax.psum(up_grad.astype(jnp.bfloat16), "dp").astype(jnp.float32),
        lax.psum(up_bias_grad.astype(jnp.bfloat16), "dp").astype(jnp.float32),
        lax.psum(down_grad.astype(jnp.bfloat16), "dp").astype(jnp.float32),
    )
    (
        first_gain_grad,
        first_shift_grad,
        second_gain_grad,
        second_shift_grad,
        output_bias_grad,
        down_bias_grad,
    ) = lax.psum(
        (
            first_gain_part,
            first_shift_part,
            second_gain_part,
            second_shift_part,
            output_bias_part,
            down_bias_part,
        ),
        ("dp", "tensor"),
    )
    return (
        block_out,
        token_grad,
        query_grad,
        key_grad,
        value_grad,
        output_grad,
        up_grad,
        up_bias_grad,
        down_grad,
        first_gain_grad,
        first_shift_grad,
        second_gain_grad,
        second_shift_grad,
        output_bias_grad,
        down_bias_grad,
    )


F32 = jnp.float32
BF16 = jnp.bfloat16
MESH = pl.DeviceIdType.MESH
N_SEMS = 192

PARTS = (
    ("D", 0, 128, "a"), ("D", 128, 128, "d"), ("D", 256, 128, "d"), ("D", 384, 128, "a"),
    ("U", 0, 256, "a"), ("U", 256, 256, "d"), ("U", 512, 256, "a"), ("U", 768, 256, "a"),
    ("O", 0, 128, "a"), ("O", 128, 128, "a"), ("Q", 0, 128, "d"), ("Q", 128, 128, "d"),
    ("Q", 256, 128, "a"), ("Q", 384, 128, "d"), ("Q", 512, 128, "a"), ("Q", 640, 128, "a"),
    ("Q", 768, 128, "a"), ("Q", 896, 128, "d"),
)
ORDER = (
    "U1", "S0", "D0", "S1", "D1", "V0", "T0", "U3", "T1", "U0", "5.1", "W0", "U2", "0.1", "V1",
    "1.1", "3.1", "5.2", "2.1", "7.1", "1.2", "0.2", "4.1", "e5.3", "2.2", "B0", "3.2", "6.1",
    "e1.3", "A0", "7.2", "0.3", "A1", "e2.3", "e5.4", "F0", "e1.4", "4.2", "3.3", "G0", "e0.4",
    "e2.4", "6.2", "7.3", "B1", "e3.4", "5.5", "4.3", "A2", "A3", "e7.4", "6.3", "1.5", "Q1", "O0",
    "e4.4", "Q3", "2.5", "5.6", "F1", "Q0", "Q2", "e6.4", "13.1", "1.6", "G1", "W1", "X0", "17.1",
    "12.1", "2.6", "10.1", "8.1", "13.2", "11.1", "17.2", "9.1", "e13.3", "12.2", "10.2", "16.1",
    "e17.3", "8.2", "Y0", "11.2", "14.1", "e10.3", "12.3", "9.2", "15.1", "e11.3", "e12.4",
    "e13.4", "e8.4", "8.3", "16.2", "14.2", "9.3", "15.2", "16.3", "Y1", "Z0", "e17.4", "e9.4",
    "14.3", "Z1", "e10.4", "e16.4", "e11.4", "e14.4", "13.5", "15.3", "17.5", "13.6", "Z2",
    "e15.4", "10.5", "17.6", "X1", "11.5", "10.6", "11.6",
)


def dot(a, b):
    return jnp.dot(a, b, preferred_element_type=F32)


def dot_nt(a, b):
    return lax.dot_general(a, b, (((1,), (1,)), ((), ())), preferred_element_type=F32)


def dot_tn(a, b):
    return lax.dot_general(a, b, (((0,), (0,)), ((), ())), preferred_element_type=F32)


def span(start, size):
    return pl.ds(pl.multiple_of(start, 16), size)


def lanes(start, size):
    return pl.ds(pl.multiple_of(start, 128), size)


class Links:
    def __init__(self, sends, recvs, anyone):
        self.sends, self.recvs, self.anyone = sends, recvs, anyone
        self.used = 0

    def take(self, count=1):
        first = self.used
        self.used += count
        assert self.used <= N_SEMS
        return first

    def copy(self, src, dst, index, device):
        return pltpu.make_async_remote_copy(
            src_ref=src,
            dst_ref=dst,
            send_sem=self.sends.at[index],
            recv_sem=self.recvs.at[index],
            device_id=device,
            device_id_type=MESH,
        )

    def got(self, dst, index):
        self.copy(dst, dst, index, self.anyone).wait_recv()

    def sent(self, src, index):
        self.copy(src, src, index, self.anyone).wait_send()


def layer_kernel(
    count,
    tokens_hbm,
    lengths,
    query_hbm,
    key_hbm,
    value_hbm,
    output_hbm,
    up_hbm,
    up_bias,
    down_hbm,
    first_gain,
    first_shift,
    second_gain,
    second_shift,
    output_bias,
    down_bias,
    cotangent_hbm,
    block_out,
    token_grad,
    down_out,
    up_out,
    output_out,
    qkv_out,
    vec_out,
    tokens,
    cotangent,
    query_weight,
    key_weight,
    value_weight,
    wo_all,
    up_weight,
    down_weight,
    first_low,
    queries,
    key_rows,
    value_rows,
    probs,
    heads_own,
    heads_full,
    residual,
    second_low,
    act,
    ugp,
    mail,
    residual_grad,
    residual_low,
    dqkv,
    g_down,
    g_up,
    g_output,
    g_qkv,
    rx_down,
    rx_up,
    rx_output,
    rx_qkv,
    rz_down,
    rz_up,
    rz_output,
    rz_qkv,
    rm_down,
    rm_up,
    rm_output,
    rm_qkv,
    t_down,
    t_up,
    t_output,
    t_qkv,
    vec,
    vec_sib,
    vec_parts,
    vec_sum,
    vec_all,
    sends,
    recvs,
    local_sems,
):
    n_rows, width = tokens.shape
    half = n_rows // 2
    tile = 16 * count
    n_tiles = n_rows // tile
    half_tiles = n_tiles // 2
    heads_here = query_weight.shape[1] // DH
    cols = heads_here * DH
    hidden = up_weight.shape[1]
    scale_factor = 1.0 / math.sqrt(DH)

    dp = lax.axis_index("dp")
    t = lax.axis_index("tensor")
    x = dp % 2
    z = dp // 2
    c = t % 2
    t_sib = t + 1 - 2 * c
    t_opp = (t + 2) % 4
    t_diag = (t_sib + 2) % 4
    sib = (dp, t_sib)
    opp = (dp, t_opp)
    diag = (dp, t_diag)
    xp = (dp + 1 - 2 * x, t)
    adj = (dp + 2 - 4 * (z % 2), t)
    cross = (dp + 2 - 4 * (z % 2) + 1 - 2 * x, t)
    mid = ((3 - z) * 2 + x, t)
    is_mid = jnp.logical_or(z == 1, z == 2)
    is_end = jnp.logical_or(z == 0, z == 3)
    side = z // 2
    dp_peers = [((dp + k) % 8, t) for k in range(1, 8)]
    links = Links(sends, recvs, sib)

    barrier = pltpu.get_barrier_semaphore()
    for peer in [sib, opp, diag] + dp_peers:
        pl.semaphore_signal(barrier, inc=1, device_id=peer, device_id_type=MESH)

    own_rows = span(c * half, half)
    other_rows = span((1 - c) * half, half)
    own_start = c * half
    sib_start = (1 - c) * half
    own_wo = span(t * cols, cols)

    def turn_rows(i):
        return span((i % 2) * half + (i // 2) * tile, tile)

    def token_load(i):
        rows = turn_rows(i)
        return pltpu.make_async_copy(tokens_hbm.at[rows, :], tokens.at[rows, :], local_sems.at[i])

    loads = [
        pltpu.make_async_copy(src, dst, local_sems.at[n_tiles + n])
        for n, (src, dst) in enumerate(
            (
                (query_hbm, query_weight),
                (key_hbm, key_weight),
                (value_hbm, value_weight),
                (output_hbm, wo_all.at[own_wo, :]),
                (up_hbm, up_weight),
                (down_hbm, down_weight),
                (cotangent_hbm, cotangent),
            )
        )
    ]
    token_load(0).start()
    for load in loads[:3]:
        load.start()
    for i in range(1, n_tiles):
        token_load(i).start()
    for load in loads[3:]:
        load.start()
    free_sem = n_tiles + len(loads)

    def row(ref):
        return ref[...].astype(F32).reshape(1, ref.shape[0])

    def norm_parts(v):
        e = v - jnp.mean(v, axis=-1, keepdims=True)
        r = lax.rsqrt(jnp.mean(e * e, axis=-1, keepdims=True) + EPS)
        return e * r, r

    piece = cols // 4
    quarter = x + 2 * (z % 2)

    def wo_piece(owner, number):
        return wo_all.at[span(owner * cols + number * piece, piece), :]

    i_wo = links.take(9)
    by_y = links.copy(
        output_hbm.at[span(quarter * piece, piece), :], wo_piece(t, quarter), i_wo, opp
    )
    whole_to_sib = links.copy(output_hbm, wo_all.at[own_wo, :], i_wo + 1, sib)
    q_xp, q_adj = quarter + 1 - 2 * x, quarter + 2 - 4 * (z % 2)
    q_cross = q_adj + 1 - 2 * x
    mine = wo_piece(t_opp, quarter)
    to_x = links.copy(mine, mine, i_wo + 2, xp)
    to_z = links.copy(mine, mine, i_wo + 3, adj)
    from_x = wo_piece(t_opp, q_xp)
    on_z = links.copy(from_x, from_x, i_wo + 4, adj)
    others = ((quarter, None), (q_xp, i_wo + 2), (q_adj, i_wo + 3), (q_cross, i_wo + 4))
    relays = [
        links.copy(wo_piece(t_opp, q), wo_piece(t_opp, q), i_wo + 5 + n, sib)
        for n, (q, _i) in enumerate(others)
    ]

    def share_first():
        links.got(mine, i_wo)
        to_x.start()
        to_z.start()
        relays[0].start()

    def share_next():
        links.got(from_x, i_wo + 2)
        on_z.start()
        relays[1].start()

    def share_last():
        links.got(wo_piece(t_opp, q_adj), i_wo + 3)
        relays[2].start()
        links.got(wo_piece(t_opp, q_cross), i_wo + 4)
        relays[3].start()
        links.got(wo_all.at[span(t_sib * cols, cols), :], i_wo + 1)
        for n, q in enumerate((quarter, q_xp, q_adj, q_cross)):
            links.got(wo_piece(t_diag, q), i_wo + 5 + n)

    wo_sends = [by_y, whole_to_sib, to_x, to_z, on_z] + relays

    def allowed_of(number):
        def series_of(index):
            return jnp.floor((index + 0.5) * (1.0 / count))

        row_at = lax.broadcasted_iota(jnp.int32, (tile, 1), 0).astype(F32)
        col_at = lax.broadcasted_iota(jnp.int32, (1, tile), 1).astype(F32)
        row_series, col_series = series_of(row_at), series_of(col_at)
        n_series = lengths.shape[0]
        which = lax.broadcasted_iota(jnp.int32, (n_series, tile), 0).astype(F32)
        here = (which == col_series + (number * 16).astype(F32)).astype(BF16)
        all_lengths = jnp.broadcast_to(
            lengths[...].astype(F32).reshape(1, n_series), (8, n_series)
        ).astype(BF16)
        length = dot(all_lengths, here)[0:1, :]
        live = (col_at - count * col_series) >= (count - length)
        same = row_series == col_series
        seen = jnp.logical_and(live, col_at <= row_at)
        return jnp.logical_and(same, jnp.logical_or(seen, col_at == row_at))

    i_heads = links.take(3 * half_tiles)

    def head_slot(j):
        return span(j * tile, tile)

    def attend(i, _):
        h, j = i % 2, i // 2
        number = h * half_tiles + j
        rows = turn_rows(i)
        token_load(i).wait()
        xhat, _r = norm_parts(tokens[rows, :].astype(F32))
        first_low[rows, :] = (xhat * row(first_gain) + row(first_shift)).astype(BF16)

        @pl.when(i == 0)
        def _():
            for load in loads[:3]:
                load.wait()

        normed = first_low[rows, :]
        q = dot(normed, query_weight[...]).astype(BF16)
        k = dot(normed, key_weight[...]).astype(BF16)
        v = dot(normed, value_weight[...]).astype(BF16)
        queries[rows, :] = q
        key_rows[rows, :] = k
        value_rows[rows, :] = v

        @pl.when(i == 0)
        def _():
            pl.semaphore_wait(barrier, 10)
            by_y.start()
            whole_to_sib.start()

        allowed = allowed_of(number)
        for head in range(heads_here):
            at = slice(head * DH, (head + 1) * DH)
            scores = jnp.where(allowed, dot_nt(q[:, at], k[:, at]) * scale_factor, -1e30)
            numerator = jnp.exp(scores - jnp.max(scores, axis=-1, keepdims=True))
            share = numerator / jnp.sum(numerator, axis=-1, keepdims=True)
            probs[number * heads_here + head] = share
            heads_own[rows, at] = dot(share.astype(BF16), v[:, at]).astype(BF16)
        slot = heads_full.at[head_slot(j), lanes(t * cols, cols)]

        @pl.when(h == c)
        def _():
            heads_full[head_slot(j), lanes(t * cols, cols)] = heads_own[rows, :]
            links.copy(heads_own.at[rows, :], slot, i_heads + j, opp).start()

        @pl.when(h != c)
        def _():
            links.copy(heads_own.at[rows, :], slot, i_heads + half_tiles + j, sib).start()
            links.copy(heads_own.at[rows, :], slot, i_heads + 2 * half_tiles + j, diag).start()

        @pl.when(i == 3)
        def _():
            share_first()

        return 0

    lax.fori_loop(0, n_tiles, attend, 0)

    share_next()
    for load in loads[3:]:
        load.wait()
    share_last()

    i_second = links.take(half_tiles)
    vec[...] = jnp.zeros_like(vec)

    def in_turn(i):
        return jnp.where(i % 2 == 0, own_start, sib_start) + (i // 2) * tile

    def feed(i):
        rows = span(in_turn(i), tile)
        u = dot(second_low[rows, :], up_weight[...]) + row(up_bias)
        big = 0.5 * (1.0 + lax.erf(u * (1.0 / math.sqrt(2.0))))
        act[rows, :] = (u * big).astype(BF16)
        slope = big + u * (jnp.exp(-0.5 * u * u) * (1.0 / math.sqrt(2.0 * math.pi)))
        grad = (dot_nt(cotangent[rows, :], down_weight[...]) * slope).astype(BF16)
        ugp[rows, :] = grad
        vec[6:7, 0:hidden] += jnp.sum(grad.astype(F32), axis=0, keepdims=True)

    def project(j, _):
        here = head_slot(j)
        for n, who in enumerate((t_opp, t_sib, t_diag)):
            links.got(heads_full.at[here, lanes(who * cols, cols)], i_heads + n * half_tiles + j)
        rows = span(own_start + j * tile, tile)
        v = tokens[rows, :].astype(F32) + dot(heads_full[here, :], wo_all[...]) + row(output_bias)
        residual[here, :] = v
        xhat, _r = norm_parts(v)
        second_low[rows, :] = (xhat * row(second_gain) + row(second_shift)).astype(BF16)
        links.copy(second_low.at[rows, :], second_low.at[rows, :], i_second + j, sib).start()
        feed(2 * j)
        links.got(second_low.at[span(sib_start + j * tile, tile), :], i_second + j)
        feed(2 * j + 1)
        return 0

    lax.fori_loop(0, half_tiles, project, 0)

    class Tensor:
        def __init__(self, grads, rx, rz, rm, total, out):
            self.grads, self.rx, self.rz, self.rm, self.total, self.out = (
                grads, rx, rz, rm, total, out,
            )

    tensors = {
        "D": Tensor(g_down, rx_down, rz_down, rm_down, t_down, down_out),
        "U": Tensor(g_up, rx_up, rz_up, rm_up, t_up, up_out),
        "O": Tensor(g_output, rx_output, rz_output, rm_output, t_output, output_out),
        "Q": Tensor(g_qkv, rx_qkv, rz_qkv, rm_qkv, t_qkv, qkv_out),
    }

    class Part:
        def __init__(self, tensor, start, size, sem):
            self.size = size // 2
            self.start = start
            here = pl.ds(start // 2, self.size)
            self.grads, self.out = tensor.grads, tensor.out
            self.rx, self.rz, self.rm, self.total = (
                ref.at[here, :] for ref in (tensor.rx, tensor.rz, tensor.rm, tensor.total)
            )
            self.index = links.take(self.messages)
            self.sem = sem

        def half_at(self, which):
            return span(self.start + which * self.size, self.size)

        def send(self, src, dst, message, device):
            links.copy(src, dst, self.index + message, device).start()

        def got(self, dst, message):
            links.got(dst, self.index + message)

        def sent(self, src, message):
            links.sent(src, self.index + message)

        def add(self, rows, came):
            return (self.grads[rows, :].astype(F32) + came[...].astype(F32)).astype(BF16)

        def write(self, rows):
            return pltpu.make_async_copy(self.total, self.out.at[rows, :], local_sems.at[self.sem])

    class PartX(Part):
        messages = 5

        def begin(self):
            self.send(self.grads.at[self.half_at(1 - x), :], self.rx, 0, xp)

        def step(self, number):
            mine = self.half_at(x)
            grads, out = self.grads.at[mine, :], self.out.at[mine, :]
            if number == 1:
                self.got(self.rx, 0)
                self.grads[mine, :] = self.add(mine, self.rx)

                @pl.when(is_end)
                def _():
                    self.send(grads, self.rz, 1, adj)

            if number == 2:

                @pl.when(is_mid)
                def _():
                    self.got(self.rz, 1)
                    self.grads[mine, :] = self.add(mine, self.rz)
                    self.send(grads, self.rm, 2, mid)

            if number == 3:

                @pl.when(is_mid)
                def _():
                    self.got(self.rm, 2)
                    self.total[...] = self.add(mine, self.rm)
                    self.send(self.total, out, 3, adj)
                    self.send(self.total, out, 4, xp)
                    self.write(mine).start()

            if number == 4:

                @pl.when(is_end)
                def _():
                    self.got(out, 3)
                    self.send(out, out, 4, xp)

        def end(self):
            mine, other = self.half_at(x), self.half_at(1 - x)
            grads, out = self.grads.at[mine, :], self.out.at[mine, :]
            self.sent(self.grads.at[other, :], 0)
            self.got(self.out.at[other, :], 4)

            @pl.when(is_end)
            def _():
                self.sent(grads, 1)
                self.sent(out, 4)

            @pl.when(is_mid)
            def _():
                self.sent(grads, 2)
                self.sent(self.total, 3)
                self.sent(self.total, 4)
                self.write(mine).wait()

    class PartZ(Part):
        messages = 7

        def begin(self):
            far = self.grads.at[self.half_at(1 - side), :]

            @pl.when(is_end)
            def _():
                self.send(far, self.rz, 0, adj)

        def step(self, number):
            near, far = self.half_at(side), self.half_at(1 - side)

            @pl.when(is_end if number in (3, 4) else is_mid)
            def _():
                if number == 1:
                    self.got(self.rz, 0)
                    self.grads[far, :] = self.add(far, self.rz)
                    self.send(self.grads.at[far, :], self.rm, 1, mid)
                if number == 2:
                    self.got(self.rm, 1)
                    self.grads[near, :] = self.add(near, self.rm)
                    self.send(self.grads.at[near, :], self.rz, 2, adj)
                if number == 3:
                    self.got(self.rz, 2)
                    self.grads[near, :] = self.add(near, self.rz)
                    self.send(self.grads.at[near, :], self.rx, 3, xp)
                if number == 4:
                    self.got(self.rx, 3)
                    self.total[...] = self.add(near, self.rx)
                    self.send(self.total, self.out.at[near, :], 4, adj)
                    self.write(near).start()
                if number == 5:
                    self.got(self.out.at[near, :], 4)
                    self.send(self.out.at[near, :], self.out.at[near, :], 5, mid)
                if number == 6:
                    self.got(self.out.at[far, :], 5)
                    self.send(self.out.at[far, :], self.out.at[far, :], 6, adj)

        def end(self):
            near, far = self.half_at(side), self.half_at(1 - side)

            @pl.when(is_end)
            def _():
                self.got(self.out.at[far, :], 6)
                self.sent(self.grads.at[far, :], 0)
                self.sent(self.grads.at[near, :], 3)
                self.sent(self.total, 4)
                self.write(near).wait()

            @pl.when(is_mid)
            def _():
                self.sent(self.grads.at[far, :], 1)
                self.sent(self.grads.at[near, :], 2)
                self.sent(self.out.at[near, :], 5)
                self.sent(self.out.at[far, :], 6)

    parts = [
        {"a": PartX, "d": PartZ}[kind](tensors[name], start, size, free_sem + n)
        for n, (name, start, size, kind) in enumerate(PARTS)
    ]

    def begin_parts(name, first, size):
        for (which, start, rows, _kind), part in zip(PARTS, parts, strict=True):
            if which == name and first < start + rows <= first + size:
                part.begin()

    block = 256

    def down_grads(i):
        at = slice(i * block, (i + 1) * block)
        g_down[at, :] = dot_tn(act[:, at], cotangent[...]).astype(BF16)
        begin_parts("D", i * block, block)

    def up_grads(i):
        at = slice(i * block, (i + 1) * block)
        g_up[at, :] = dot_tn(second_low[:, at], ugp[...]).astype(BF16)
        begin_parts("U", i * block, block)

    def output_grads(_i):
        g_output[...] = dot_tn(heads_own[...], residual_low[...]).astype(BF16)
        begin_parts("O", 0, cols)

    def qkv_grads(i):
        at = slice(i * block, (i + 1) * block)
        g_qkv[at, :] = dot_tn(first_low[:, at], dqkv[...]).astype(BF16)
        begin_parts("Q", i * block, block)

    class RowSum:
        def __init__(self, number, part):
            self.snd, self.r1, self.cs, self.r2 = (mail.at[4 * number + n] for n in range(4))
            self.part = part
            self.index = links.take(2 * half_tiles)

        def far(self, j):
            here = head_slot(j)
            self.snd[here, :] = self.part(span(sib_start + j * tile, tile)).astype(BF16)
            links.copy(self.snd.at[here, :], self.r1.at[here, :], self.index + j, sib).start()

        def near(self, j):
            here = head_slot(j)
            mine = self.part(span(own_start + j * tile, tile))
            links.got(self.r1.at[here, :], self.index + j)
            self.cs[here, :] = (mine + self.r1[here, :].astype(F32)).astype(BF16)
            links.copy(
                self.cs.at[here, :], self.r2.at[here, :], self.index + half_tiles + j, opp
            ).start()

        def rows(self, j):
            here = head_slot(j)
            links.got(self.r2.at[here, :], self.index + half_tiles + j)
            return self.cs[here, :].astype(F32) + self.r2[here, :].astype(F32)

        def end(self, j):
            here = head_slot(j)
            links.sent(self.snd.at[here, :], self.index + j)
            links.sent(self.cs.at[here, :], self.index + half_tiles + j)

    second_sum = RowSum(0, lambda rows: dot_nt(ugp[rows, :], up_weight[...]))
    out_sum = RowSum(1, lambda rows: dot(act[rows, :], down_weight[...]))
    first_sum = RowSum(
        2,
        lambda rows: dot_nt(dqkv[rows, 0:cols], query_weight[...])
        + dot_nt(dqkv[rows, cols : 2 * cols], key_weight[...])
        + dot_nt(dqkv[rows, 2 * cols : 3 * cols], value_weight[...]),
    )
    row_sums = (second_sum, out_sum, first_sum)

    i_back = links.take(half_tiles)

    def add_to(at, value):
        vec[at : at + 1, :] += jnp.sum(value, axis=0, keepdims=True)

    def norm_back(incoming, xhat, r, gain):
        weighted = incoming * gain
        return r * (
            weighted
            - jnp.mean(weighted, axis=-1, keepdims=True)
            - xhat * jnp.mean(weighted * xhat, axis=-1, keepdims=True)
        )

    def second_back(j):
        local = head_slot(j)
        rows = span(own_start + j * tile, tile)
        incoming = second_sum.rows(j)
        xhat, r = norm_parts(residual[local, :])
        given = cotangent[rows, :].astype(F32)
        grad = given + norm_back(incoming, xhat, r, row(second_gain))
        residual_grad[local, :] = grad
        residual_low[rows, :] = grad.astype(BF16)
        links.copy(residual_low.at[rows, :], residual_low.at[rows, :], i_back + j, sib).start()
        add_to(2, incoming * xhat)
        add_to(3, incoming)
        add_to(4, grad)
        add_to(5, given)

    def attend_back(i):
        start = in_turn(i)
        rows = span(start, tile)
        number = start // tile
        if i % 2 == 1:
            links.got(residual_low.at[rows, :], i_back + i // 2)
        grads = dot_nt(residual_low[rows, :], wo_all[own_wo, :]).astype(BF16)
        for head in range(heads_here):
            at = slice(head * DH, (head + 1) * DH)
            share = probs[number * heads_here + head]
            q, k, v = queries[rows, at], key_rows[rows, at], value_rows[rows, at]
            share_grad = dot_nt(grads[:, at], v)
            inner = jnp.sum(share * share_grad, axis=-1, keepdims=True)
            scores_grad = (share * (share_grad - inner)).astype(BF16)
            dqkv[rows, head * DH : (head + 1) * DH] = (
                dot(scores_grad, k) * scale_factor
            ).astype(BF16)
            dqkv[rows, cols + head * DH : cols + (head + 1) * DH] = (
                dot_tn(scores_grad, q) * scale_factor
            ).astype(BF16)
            dqkv[rows, 2 * cols + head * DH : 2 * cols + (head + 1) * DH] = dot_tn(
                share.astype(BF16), grads[:, at]
            ).astype(BF16)

    i_out = links.take(2 * half_tiles)
    out_rows = mail.at[4]
    token_rows = mail.at[8]
    out_sem = free_sem + len(PARTS)

    def finished(j, number, rows_ref, out):
        rows = span(own_start + j * tile, tile)
        src = rows_ref.at[head_slot(j), :]
        n = number * half_tiles + j
        return (
            links.copy(src, out.at[rows, :], i_out + n, sib),
            pltpu.make_async_copy(src, out.at[rows, :], local_sems.at[out_sem + n]),
        )

    def finish_out(j):
        local = head_slot(j)
        links.sent(out_sum.snd.at[local, :], out_sum.index + j)
        out_rows[local, :] = (residual[local, :] + out_sum.rows(j) + row(down_bias)).astype(BF16)
        for each in finished(j, 0, out_rows, block_out):
            each.start()

    def first_back(j):
        local = head_slot(j)
        rows = span(own_start + j * tile, tile)
        incoming = first_sum.rows(j)
        xhat, r = norm_parts(tokens[rows, :].astype(F32))
        grad = residual_grad[local, :] + norm_back(incoming, xhat, r, row(first_gain))
        links.sent(first_sum.snd.at[local, :], first_sum.index + j)
        token_rows[local, :] = grad.astype(BF16)
        for each in finished(j, 1, token_rows, token_grad):
            each.start()
        add_to(0, incoming * xhat)
        add_to(1, incoming)

    i_vec = links.take(1 + 2 * 7)
    vec_send = links.copy(vec, vec_sib, i_vec, sib)
    part = width // 8
    mine_at = lanes(dp * part, part)
    part_sends = [
        links.copy(vec.at[:, lanes(peer[0] * part, part)], vec_parts.at[dp], i_vec + 1 + k, peer)
        for k, peer in enumerate(dp_peers)
    ]
    sum_sends = [
        links.copy(vec_sum, vec_all.at[:, mine_at], i_vec + 8 + k, peer)
        for k, peer in enumerate(dp_peers)
    ]

    def vectors(number):
        if number == 0:
            vec_send.start()
        if number == 1:
            links.got(vec_sib, i_vec)
            vec_send.wait_send()
            at_row = lax.broadcasted_iota(jnp.int32, vec.shape, 0)
            vec[...] = vec[...] + jnp.where(at_row < 6, vec_sib[...], 0.0)
            vec_parts[dp] = vec[:, mine_at]
            for send in part_sends:
                send.start()
        if number == 2:
            for k in range(7):
                links.got(vec_parts.at[(dp + 7 - k) % 8], i_vec + 1 + k)
            total = vec_parts[0]
            for k in range(1, 8):
                total = total + vec_parts[k]
            vec_sum[...] = total
            vec_all[:, mine_at] = total
            for send in sum_sends:
                send.start()

    tasks = {
        "D": down_grads,
        "U": up_grads,
        "O": output_grads,
        "Q": qkv_grads,
        "S": second_sum.far,
        "T": second_sum.near,
        "V": out_sum.far,
        "W": out_sum.near,
        "F": first_sum.far,
        "G": first_sum.near,
        "B": second_back,
        "A": attend_back,
        "X": finish_out,
        "Y": first_back,
        "Z": vectors,
    }
    for name in ORDER:
        if "." in name:
            number, step = name.removeprefix("e").split(".")
            parts[int(number)].step(int(step))
        else:
            tasks[name[0]](int(name[1:]))

    for k in range(7):
        links.got(vec_all.at[:, lanes(((dp + 7 - k) % 8) * part, part)], i_vec + 8 + k)
    vec_out[...] = vec_all[...]
    for each in parts:
        each.end()
    for send in wo_sends + part_sends + sum_sends:
        send.wait_send()
    for j in range(half_tiles):
        here = head_slot(j)
        rows = span(own_start + j * tile, tile)
        far_rows = span(sib_start + j * tile, tile)
        for number, (rows_ref, out) in enumerate(
            ((out_rows, block_out), (token_rows, token_grad))
        ):
            remote, local = finished(j, number, rows_ref, out)
            remote.wait_send()
            local.wait()
            links.got(out.at[far_rows, :], i_out + number * half_tiles + j)
        links.sent(heads_own.at[rows, :], i_heads + j)
        links.sent(heads_own.at[far_rows, :], i_heads + half_tiles + j)
        links.sent(heads_own.at[far_rows, :], i_heads + 2 * half_tiles + j)
        links.sent(second_low.at[rows, :], i_second + j)
        links.sent(residual_low.at[rows, :], i_back + j)
        links.sent(second_sum.snd.at[here, :], second_sum.index + j)
        for each in row_sums:
            links.sent(each.cs.at[here, :], each.index + half_tiles + j)


def results_kernel(cols, hidden, blocks, down, up, output, qkv, vec, *outs):
    (
        query_out,
        key_out,
        value_out,
        output_out,
        up_out,
        up_bias_out,
        down_out,
        *vectors,
    ) = outs
    for n, out in enumerate((query_out, key_out, value_out)):
        out[...] = qkv[:, n * cols : (n + 1) * cols].astype(F32)
    output_out[...] = output[...].astype(F32)
    up_out[...] = up[...].astype(F32)
    down_out[...] = down[...].astype(F32)

    @pl.when(pl.program_id(0) == blocks - 1)
    def _():
        up_bias_out[...] = vec[6, 0:hidden]
        for n, out in enumerate(vectors):
            out[...] = vec[n, :]


def kernel_shards(*args):
    tokens, lengths = args[0], args[1]
    n_rows, width = tokens.shape
    count = n_rows // lengths.shape[0]
    tile = 16 * count
    half = n_rows // 2
    cols = args[2].shape[1]
    hidden = args[6].shape[1]
    vmem = pltpu.VMEM
    grads = ((hidden, width), (width, hidden), (cols, width), (width, 3 * cols))
    halves = [(r // 2, n) for r, n in grads]
    any_space = pl.BlockSpec(memory_space=pl.ANY)
    in_vmem = pl.BlockSpec(memory_space=pltpu.VMEM)
    scratch = [
        vmem((n_rows, width), BF16),
        vmem((n_rows, width), BF16),
        vmem((width, cols), BF16),
        vmem((width, cols), BF16),
        vmem((width, cols), BF16),
        vmem((width, width), BF16),
        vmem((width, hidden), BF16),
        vmem((hidden, width), BF16),
        vmem((n_rows, width), BF16),
        vmem((n_rows, cols), BF16),
        vmem((n_rows, cols), BF16),
        vmem((n_rows, cols), BF16),
        vmem((n_rows // tile * (cols // DH), tile, tile), F32),
        vmem((n_rows, cols), BF16),
        vmem((half, width), BF16),
        vmem((half, width), F32),
        vmem((n_rows, width), BF16),
        vmem((n_rows, hidden), BF16),
        vmem((n_rows, hidden), BF16),
        vmem((12, half, width), BF16),
        vmem((half, width), F32),
        vmem((n_rows, width), BF16),
        vmem((n_rows, 3 * cols), BF16),
    ]
    scratch += [vmem(s, BF16) for s in grads]
    for _ in range(4):
        scratch += [vmem(s, BF16) for s in halves]
    scratch += [
        vmem((8, width), F32),
        vmem((8, width), F32),
        vmem((8, 8, width // 8), F32),
        vmem((8, width // 8), F32),
        vmem((8, width), F32),
        pltpu.SemaphoreType.DMA((N_SEMS,)),
        pltpu.SemaphoreType.DMA((N_SEMS,)),
        pltpu.SemaphoreType.DMA((48,)),
    ]
    block_out, token_grad, down, up, output, qkv, vec = pl.pallas_call(
        functools.partial(layer_kernel, count),
        out_shape=[
            jax.ShapeDtypeStruct((n_rows, width), BF16),
            jax.ShapeDtypeStruct((n_rows, width), BF16),
            *[jax.ShapeDtypeStruct(s, BF16) for s in grads],
            jax.ShapeDtypeStruct((8, width), F32),
        ],
        in_specs=[any_space if a.ndim == 2 else in_vmem for a in args],
        out_specs=[any_space] * 6 + [in_vmem],
        scratch_shapes=scratch,
        compiler_params=pltpu.CompilerParams(
            collective_id=0, has_side_effects=True, vmem_limit_bytes=63 * 2**20
        ),
        name="layer",
    )(*args)

    blocks = 4
    by_rows = [pl.BlockSpec((r // blocks, n), lambda i: (i, 0)) for r, n in grads]
    apart = pl.BlockSpec((width // blocks, cols), lambda i: (i, 0))
    f32_grads = [jax.ShapeDtypeStruct(s, F32) for s in grads]
    split = jax.ShapeDtypeStruct((width, cols), F32)
    vector = jax.ShapeDtypeStruct((width,), F32)
    query, key, value, output, up, up_bias, down, *vectors = pl.pallas_call(
        functools.partial(results_kernel, cols, hidden, blocks),
        grid=(blocks,),
        out_shape=[split] * 3
        + [f32_grads[2], f32_grads[1], jax.ShapeDtypeStruct((hidden,), F32), f32_grads[0]]
        + [vector] * 6,
        in_specs=by_rows + [in_vmem],
        out_specs=[apart] * 3 + [by_rows[2], by_rows[1], in_vmem, by_rows[0]] + [in_vmem] * 6,
        compiler_params=pltpu.CompilerParams(vmem_limit_bytes=48 * 2**20),
        name="results",
    )(down, up, output, qkv, vec)
    return (
        block_out,
        token_grad,
        query,
        key,
        value,
        output,
        up,
        up_bias,
        down,
        *vectors,
    )


def solution(mesh):
    fits = mesh.shape["dp"] == 8 and mesh.shape["tensor"] == 4
    return jax.shard_map(
        kernel_shards if fits else plain_shards,
        mesh=mesh,
        in_specs=(
            P("dp", None),
            P("dp"),
            P(None, "tensor"),
            P(None, "tensor"),
            P(None, "tensor"),
            P("tensor", None),
            P(None, "tensor"),
            P("tensor"),
            P("tensor", None),
            P(),
            P(),
            P(),
            P(),
            P(),
            P(),
            P("dp", None),
        ),
        out_specs=(
            P("dp", None),
            P("dp", None),
            P(None, "tensor"),
            P(None, "tensor"),
            P(None, "tensor"),
            P("tensor", None),
            P(None, "tensor"),
            P("tensor"),
            P("tensor", None),
            P(),
            P(),
            P(),
            P(),
            P(),
            P(),
        ),
        check_vma=False,
    )
```

```python
import functools
import math

import jax
import jax.numpy as jnp
from jax import lax
from jax.experimental import pallas as pl
from jax.experimental.pallas import tpu as pltpu
from jax.sharding import PartitionSpec as P

DH = 128


EPS = 1e-05


def norm_parts(rows, gain, shift):
    row_mean = jnp.mean(rows, axis=-1, keepdims=True)
    centred = rows - row_mean
    inverse = lax.rsqrt(jnp.mean(centred * centred, axis=-1, keepdims=True) + EPS)
    scaled = centred * inverse
    return (scaled * gain + shift, scaled, inverse)


def norm_back(incoming, scaled, inverse, gain):
    weighted = incoming * gain
    return inverse * (
        weighted
        - jnp.mean(weighted, axis=-1, keepdims=True)
        - scaled * jnp.mean(weighted * scaled, axis=-1, keepdims=True)
    )


def allowed_mask(lengths, count):
    position = jnp.arange(count, dtype=jnp.int32)
    start = (count - lengths)[:, None, None]
    query_pos = position[None, :, None]
    key_pos = position[None, None, :]
    return (key_pos >= start) & (key_pos <= query_pos) | (key_pos == query_pos)


def gelu_exact(values):
    return jax.nn.gelu(values, approximate=False)


def plain_shards(
    tokens,
    lengths,
    query_weight,
    key_weight,
    value_weight,
    output_weight,
    up_weight,
    up_bias,
    down_weight,
    first_gain,
    first_shift,
    second_gain,
    second_shift,
    output_bias,
    down_bias,
    cotangent,
):
    tok_rows = tokens.shape[0]
    series = lengths.shape[0]
    count = tok_rows // series
    heads_here = query_weight.shape[1] // DH
    groups = lax.axis_size("tensor")
    share = tok_rows // groups
    begin = lax.axis_index("tensor") * share
    scale_factor = 1.0 / math.sqrt(DH)
    allowed = allowed_mask(lengths, count)[:, None]

    def share_rows(array):
        return lax.dynamic_slice_in_dim(array, begin, share, 0)

    def to_heads(array):
        return array.reshape(series, count, heads_here, DH)

    def masked_scores(query_four, key_four):
        raw = (
            jnp.einsum("sqhd,skhd->shqk", query_four, key_four, preferred_element_type=jnp.float32)
            * scale_factor
        )
        return jnp.where(allowed, raw, -1e30)

    inputs = tokens.astype(jnp.float32)
    gain_one = first_gain.astype(jnp.float32)
    gain_two = second_gain.astype(jnp.float32)
    first_normed, first_scaled, first_inverse = norm_parts(
        inputs, gain_one, first_shift.astype(jnp.float32)
    )
    first_low = first_normed.astype(jnp.bfloat16)
    queries = jnp.dot(first_low, query_weight, preferred_element_type=jnp.float32).astype(
        jnp.bfloat16
    )
    key_rows = jnp.dot(first_low, key_weight, preferred_element_type=jnp.float32).astype(
        jnp.bfloat16
    )
    value_rows = jnp.dot(first_low, value_weight, preferred_element_type=jnp.float32).astype(
        jnp.bfloat16
    )
    query_four = to_heads(queries)
    key_four = to_heads(key_rows)
    value_four = to_heads(value_rows)
    scores = masked_scores(query_four, key_four)
    row_max = jnp.max(scores, axis=-1, keepdims=True)
    numerator = jnp.exp(scores - row_max)
    row_total = jnp.sum(numerator, axis=-1, keepdims=True)
    log_total = row_max + jnp.log(row_total)
    probs_low = (numerator / row_total).astype(jnp.bfloat16)
    heads_out = jnp.einsum(
        "shqk,skhd->sqhd", probs_low, value_four, preferred_element_type=jnp.float32
    )
    heads_low = heads_out.astype(jnp.bfloat16).reshape(tok_rows, heads_here * DH)
    attn_part = jnp.dot(heads_low, output_weight, preferred_element_type=jnp.float32)
    bias_attn = output_bias.astype(jnp.float32)
    bias_down = down_bias.astype(jnp.float32)
    grad_output = cotangent.astype(jnp.float32)
    attn_share = lax.psum_scatter(attn_part, "tensor", scatter_dimension=0, tiled=True)
    residual_share = share_rows(inputs) + attn_share + bias_attn
    second_share, second_scaled, second_inverse = norm_parts(
        residual_share, gain_two, second_shift.astype(jnp.float32)
    )
    second_low = lax.all_gather(second_share.astype(jnp.bfloat16), "tensor", axis=0, tiled=True)
    up_pre = jnp.dot(second_low, up_weight, preferred_element_type=jnp.float32) + up_bias.astype(
        jnp.float32
    )
    activated, gelu_pull = jax.vjp(gelu_exact, up_pre)
    activated = activated.astype(jnp.bfloat16)
    down_part = jnp.dot(activated, down_weight, preferred_element_type=jnp.float32)
    down_share = lax.psum_scatter(
        down_part.astype(jnp.bfloat16), "tensor", scatter_dimension=0, tiled=True
    ).astype(jnp.float32)
    out_share = (residual_share + down_share + bias_down).astype(jnp.bfloat16)
    block_out = lax.all_gather(out_share, "tensor", axis=0, tiled=True)
    down_bias_part = jnp.sum(share_rows(grad_output), axis=0)
    down_grad = jnp.einsum("tf,td->fd", activated, cotangent, preferred_element_type=jnp.float32)
    activated_grad = jnp.einsum(
        "td,fd->tf", cotangent, down_weight, preferred_element_type=jnp.float32
    )
    up_grad_pre = gelu_pull(activated_grad)[0].astype(jnp.bfloat16)
    up_bias_grad = jnp.sum(up_grad_pre.astype(jnp.float32), axis=0)
    up_grad = jnp.einsum("td,tf->df", second_low, up_grad_pre, preferred_element_type=jnp.float32)
    second_part = jnp.einsum(
        "tf,df->td", up_grad_pre, up_weight, preferred_element_type=jnp.float32
    )
    second_grad_share = lax.psum_scatter(second_part, "tensor", scatter_dimension=0, tiled=True)
    residual_share_grad = share_rows(grad_output) + norm_back(
        second_grad_share, second_scaled, second_inverse, gain_two
    )
    second_gain_part = jnp.sum(second_grad_share * second_scaled, axis=0)
    second_shift_part = jnp.sum(second_grad_share, axis=0)
    output_bias_part = jnp.sum(residual_share_grad, axis=0)
    residual_low = lax.all_gather(
        residual_share_grad.astype(jnp.bfloat16), "tensor", axis=0, tiled=True
    )
    output_grad = jnp.einsum(
        "tc,td->cd", heads_low, residual_low, preferred_element_type=jnp.float32
    )
    heads_grad = jnp.einsum(
        "td,cd->tc", residual_low, output_weight, preferred_element_type=jnp.float32
    )
    heads_grad_four = to_heads(heads_grad.astype(jnp.bfloat16))
    probs_again = jnp.exp(masked_scores(query_four, key_four) - log_total)
    value_rows_grad = jnp.einsum(
        "shqk,sqhd->skhd", probs_low, heads_grad_four, preferred_element_type=jnp.float32
    ).astype(jnp.bfloat16)
    probs_grad = jnp.einsum(
        "sqhd,skhd->shqk", heads_grad_four, value_four, preferred_element_type=jnp.float32
    )
    inner_sum = jnp.sum(probs_again * probs_grad, axis=-1, keepdims=True)
    scores_grad = (probs_again * (probs_grad - inner_sum)).astype(jnp.bfloat16)
    queries_grad = (
        (
            jnp.einsum("shqk,skhd->sqhd", scores_grad, key_four, preferred_element_type=jnp.float32)
            * scale_factor
        )
        .astype(jnp.bfloat16)
        .reshape(tok_rows, heads_here * DH)
    )
    key_rows_grad = (
        (
            jnp.einsum(
                "shqk,sqhd->skhd", scores_grad, query_four, preferred_element_type=jnp.float32
            )
            * scale_factor
        )
        .astype(jnp.bfloat16)
        .reshape(tok_rows, heads_here * DH)
    )
    value_rows_grad = value_rows_grad.reshape(tok_rows, heads_here * DH)
    query_grad = jnp.einsum(
        "td,tc->dc", first_low, queries_grad, preferred_element_type=jnp.float32
    )
    key_grad = jnp.einsum("td,tc->dc", first_low, key_rows_grad, preferred_element_type=jnp.float32)
    value_grad = jnp.einsum(
        "td,tc->dc", first_low, value_rows_grad, preferred_element_type=jnp.float32
    )
    first_part = (
        jnp.einsum("tc,dc->td", queries_grad, query_weight, preferred_element_type=jnp.float32)
        + jnp.einsum("tc,dc->td", key_rows_grad, key_weight, preferred_element_type=jnp.float32)
        + jnp.einsum("tc,dc->td", value_rows_grad, value_weight, preferred_element_type=jnp.float32)
    )
    first_grad_share = lax.psum_scatter(
        first_part.astype(jnp.bfloat16), "tensor", scatter_dimension=0, tiled=True
    ).astype(jnp.float32)
    scaled_share = share_rows(first_scaled)
    token_share = residual_share_grad + norm_back(
        first_grad_share, scaled_share, share_rows(first_inverse), gain_one
    )
    token_grad = lax.all_gather(token_share.astype(jnp.bfloat16), "tensor", axis=0, tiled=True)
    first_gain_part = jnp.sum(first_grad_share * scaled_share, axis=0)
    first_shift_part = jnp.sum(first_grad_share, axis=0)
    query_grad, key_grad, value_grad, output_grad, up_grad, up_bias_grad, down_grad = (
        lax.psum(query_grad.astype(jnp.bfloat16), "dp").astype(jnp.float32),
        lax.psum(key_grad.astype(jnp.bfloat16), "dp").astype(jnp.float32),
        lax.psum(value_grad.astype(jnp.bfloat16), "dp").astype(jnp.float32),
        lax.psum(output_grad.astype(jnp.bfloat16), "dp").astype(jnp.float32),
        lax.psum(up_grad.astype(jnp.bfloat16), "dp").astype(jnp.float32),
        lax.psum(up_bias_grad.astype(jnp.bfloat16), "dp").astype(jnp.float32),
        lax.psum(down_grad.astype(jnp.bfloat16), "dp").astype(jnp.float32),
    )
    (
        first_gain_grad,
        first_shift_grad,
        second_gain_grad,
        second_shift_grad,
        output_bias_grad,
        down_bias_grad,
    ) = lax.psum(
        (
            first_gain_part,
            first_shift_part,
            second_gain_part,
            second_shift_part,
            output_bias_part,
            down_bias_part,
        ),
        ("dp", "tensor"),
    )
    return (
        block_out,
        token_grad,
        query_grad,
        key_grad,
        value_grad,
        output_grad,
        up_grad,
        up_bias_grad,
        down_grad,
        first_gain_grad,
        first_shift_grad,
        second_gain_grad,
        second_shift_grad,
        output_bias_grad,
        down_bias_grad,
    )


F32 = jnp.float32
BF16 = jnp.bfloat16
MESH = pl.DeviceIdType.MESH
N_SENDS = 32
N_RECVS = 128
N_LOCAL = 19

PARTS = (
    ("D", 0, 128, "d"), ("D", 128, 128, "a"), ("D", 256, 128, "a"), ("D", 384, 128, "a"),
    ("U", 0, 256, "d"), ("U", 256, 256, "d"), ("U", 512, 256, "a"), ("U", 768, 256, "a"),
    ("O", 0, 128, "a"), ("O", 128, 128, "a"), ("Q", 0, 128, "a"), ("Q", 128, 128, "d"),
    ("Q", 256, 128, "a"), ("Q", 384, 128, "a"), ("Q", 512, 128, "d"), ("Q", 640, 128, "d"),
    ("Q", 768, 128, "d"), ("Q", 896, 128, "a"),
)
ORDER = (
    "P0", "E0", "P1", "E2", "E1", "V0", "S0", "E3", "U0", "D0", "S1", "U3", "T0", "D1", "U2", "T1",
    "V1", "U1", "W0", "4.1", "1.1", "0.1", "7.1", "4.2", "5.1", "2.1", "e4.3", "0.2", "1.2", "3.1",
    "B0", "5.2", "A0", "e0.3", "7.2", "6.1", "A1", "1.3", "F0", "e5.3", "e4.4", "2.2", "G0",
    "e1.4", "e0.4", "7.3", "3.2", "2.3", "6.2", "B1", "e5.4", "e7.4", "A2", "3.3", "4.5", "A3",
    "e2.4", "Q2", "6.3", "O0", "Q3", "Q0", "0.5", "F1", "e3.4", "Q1", "4.6", "5.5", "G1", "W1",
    "e6.4", "0.6", "14.1", "X0", "8.1", "15.1", "5.6", "16.1", "9.1", "14.2", "11.1", "17.1",
    "15.2", "10.1", "e14.3", "e15.3", "16.2", "8.2", "12.1", "e16.3", "Y0", "11.2", "9.2", "13.1",
    "e11.3", "e8.4", "e14.4", "e9.4", "8.3", "17.2", "10.2", "9.3", "12.2", "17.3", "13.2", "10.3",
    "Y1", "Z0", "e15.4", "e17.4", "12.3", "Z1", "e16.4", "e10.4", "e11.4", "14.5", "13.3", "15.5",
    "14.6", "Z2", "e12.4", "e13.4", "16.5", "15.6", "11.5", "X1", "16.6", "11.6",
)


def dot(a, b):
    return jnp.dot(a, b, preferred_element_type=F32)


def dot_nt(a, b):
    return lax.dot_general(a, b, (((1,), (1,)), ((), ())), preferred_element_type=F32)


def dot_tn(a, b):
    return lax.dot_general(a, b, (((0,), (0,)), ((), ())), preferred_element_type=F32)


def span(start, size):
    return pl.ds(pl.multiple_of(start, 16), size)


def lanes(start, size):
    return pl.ds(pl.multiple_of(start, 128), size)


class Links:
    def __init__(self, sends, recvs, anyone):
        self.sends, self.recvs, self.anyone = sends, recvs, anyone
        self.used = [0, 0]

    def group(self):
        self.used[0] += 1
        assert self.used[0] <= N_SENDS
        return self.used[0] - 1

    def take(self, count=1):
        first = self.used[1]
        self.used[1] += count
        assert self.used[1] <= N_RECVS
        return first

    def copy(self, src, dst, group, index, device):
        return pltpu.make_async_remote_copy(
            src_ref=src,
            dst_ref=dst,
            send_sem=self.sends.at[group],
            recv_sem=self.recvs.at[index],
            device_id=device,
            device_id_type=MESH,
        )

    def got(self, dst, index):
        self.copy(dst, dst, 0, index, self.anyone).wait_recv()

    def sent(self, like, group):
        self.copy(like, like, group, 0, self.anyone).wait_send()


def layer_kernel(
    count,
    tokens_hbm,
    lengths_hbm,
    query_hbm,
    key_hbm,
    value_hbm,
    output_hbm,
    up_hbm,
    up_bias_hbm,
    down_hbm,
    first_gain_hbm,
    first_shift_hbm,
    second_gain_hbm,
    second_shift_hbm,
    output_bias_hbm,
    down_bias_hbm,
    cotangent_hbm,
    block_out,
    token_grad,
    down_out,
    up_out,
    output_out,
    qkv_out,
    vec_out,
    lengths,
    up_bias,
    first_gain,
    first_shift,
    second_gain,
    second_shift,
    output_bias,
    down_bias,
    tokens,
    cotangent,
    query_weight,
    key_weight,
    value_weight,
    wo_all,
    up_weight,
    down_weight,
    first_low,
    queries,
    key_rows,
    value_rows,
    probs,
    heads_own,
    heads_full,
    residual,
    second_low,
    act,
    ugp,
    mail,
    residual_grad,
    residual_low,
    dqkv,
    g_down,
    g_up,
    g_output,
    g_qkv,
    rx_down,
    rx_up,
    rx_output,
    rx_qkv,
    rz_down,
    rz_up,
    rz_output,
    rz_qkv,
    rm_down,
    rm_up,
    rm_output,
    rm_qkv,
    vec,
    vec_sib,
    vec_parts,
    vec_sum,
    sends,
    recvs,
    local_sems,
):
    n_rows, width = tokens.shape
    half = n_rows // 2
    tile = 16 * count
    n_tiles = n_rows // tile
    half_tiles = n_tiles // 2
    heads_here = query_weight.shape[1] // DH
    cols = heads_here * DH
    hidden = up_weight.shape[1]
    scale_factor = 1.0 / math.sqrt(DH)

    dp = lax.axis_index("dp")
    t = lax.axis_index("tensor")
    x = dp % 2
    z = dp // 2
    c = t % 2
    t_sib = t + 1 - 2 * c
    t_opp = (t + 2) % 4
    t_diag = (t_sib + 2) % 4
    sib = (dp, t_sib)
    opp = (dp, t_opp)
    diag = (dp, t_diag)
    xp = (dp + 1 - 2 * x, t)
    adj = (dp + 2 - 4 * (z % 2), t)
    cross = (dp + 2 - 4 * (z % 2) + 1 - 2 * x, t)
    mid = ((3 - z) * 2 + x, t)
    is_mid = jnp.logical_or(z == 1, z == 2)
    is_end = jnp.logical_or(z == 0, z == 3)
    side = z // 2
    dp_peers = [((dp + k) % 8, t) for k in range(1, 8)]
    links = Links(sends, recvs, sib)

    barrier = pltpu.get_barrier_semaphore()
    for peer in [sib, opp, diag] + dp_peers:
        pl.semaphore_signal(barrier, inc=1, device_id=peer, device_id_type=MESH)

    other_rows = span((1 - c) * half, half)
    own_start = c * half
    sib_start = (1 - c) * half
    own_wo = span(t * cols, cols)

    def turn_rows(i):
        return span((i % 2) * half + (i // 2) * tile, tile)

    def token_load(i):
        rows = turn_rows(i)
        return pltpu.make_async_copy(tokens_hbm.at[rows, :], tokens.at[rows, :], local_sems.at[i])

    loads = [
        pltpu.make_async_copy(src, dst, local_sems.at[n_tiles + n])
        for n, (src, dst) in enumerate(
            (
                (query_hbm, query_weight),
                (key_hbm, key_weight),
                (value_hbm, value_weight),
                (lengths_hbm, lengths),
                (first_gain_hbm, first_gain),
                (first_shift_hbm, first_shift),
                (output_hbm, wo_all.at[own_wo, :]),
                (output_bias_hbm, output_bias),
                (second_gain_hbm, second_gain),
                (second_shift_hbm, second_shift),
                (up_bias_hbm, up_bias),
                (down_bias_hbm, down_bias),
                (up_hbm, up_weight),
                (down_hbm, down_weight),
                (cotangent_hbm, cotangent),
            )
        )
    ]
    token_load(0).start()
    early = 6
    for load in loads[:early]:
        load.start()
    for i in range(1, n_tiles):
        token_load(i).start()
    for load in loads[early:]:
        load.start()

    def row(ref):
        return ref[...].astype(F32).reshape(1, ref.shape[0])

    def norm_parts(v):
        e = v - jnp.mean(v, axis=-1, keepdims=True)
        r = lax.rsqrt(jnp.mean(e * e, axis=-1, keepdims=True) + EPS)
        return e * r, r

    piece = cols // 4
    quarter = x + 2 * (z % 2)

    def wo_piece(owner, number):
        return wo_all.at[span(owner * cols + number * piece, piece), :]

    i_wo = links.take(7)
    s_wo = links.group()
    by_y = links.copy(
        output_hbm.at[span(quarter * piece, piece), :], wo_piece(t, quarter), s_wo, i_wo, opp
    )
    whole_to_sib = links.copy(output_hbm, wo_all.at[own_wo, :], s_wo, i_wo + 1, sib)
    q_xp, q_adj = quarter + 1 - 2 * x, quarter + 2 - 4 * (z % 2)
    q_cross = q_adj + 1 - 2 * x
    mine = wo_piece(t_opp, quarter)
    to_x = links.copy(mine, mine, s_wo, i_wo + 2, xp)
    to_z = links.copy(mine, mine, s_wo, i_wo + 3, adj)

    def half_piece(number, which):
        return wo_all.at[span(t_opp * cols + number * piece + which * piece // 2, piece // 2), :]

    from_x, from_z = half_piece(q_xp, 0), half_piece(q_adj, 1)
    on_z = links.copy(from_x, from_x, s_wo, i_wo + 4, adj)
    on_x = links.copy(from_z, from_z, s_wo, i_wo + 5, xp)

    def relay(number):
        part = wo_piece(t_opp, number)
        links.copy(part, part, s_wo, i_wo + 6, sib).start()

    def share_first():
        links.got(mine, i_wo)
        to_x.start()
        to_z.start()
        relay(quarter)

    def share_next():
        links.got(wo_piece(t_opp, q_xp), i_wo + 2)
        on_z.start()
        links.got(wo_piece(t_opp, q_adj), i_wo + 3)
        on_x.start()
        relay(q_xp)
        relay(q_adj)

    def share_last():
        links.got(half_piece(q_cross, 0), i_wo + 4)
        links.got(half_piece(q_cross, 1), i_wo + 5)
        relay(q_cross)
        links.got(wo_all.at[span(t_sib * cols, cols), :], i_wo + 1)
        links.got(wo_all.at[span(t_diag * cols, cols), :], i_wo + 6)

    pl.semaphore_wait(barrier, 10)
    by_y.start()
    whole_to_sib.start()

    def allowed_of(number):
        def series_of(index):
            return jnp.floor((index + 0.5) * (1.0 / count))

        row_at = lax.broadcasted_iota(jnp.int32, (tile, 1), 0).astype(F32)
        col_at = lax.broadcasted_iota(jnp.int32, (1, tile), 1).astype(F32)
        row_series, col_series = series_of(row_at), series_of(col_at)
        n_series = lengths.shape[0]
        which = lax.broadcasted_iota(jnp.int32, (n_series, tile), 0).astype(F32)
        here = (which == col_series + (number * 16).astype(F32)).astype(BF16)
        all_lengths = jnp.broadcast_to(
            lengths[...].astype(F32).reshape(1, n_series), (8, n_series)
        ).astype(BF16)
        length = dot(all_lengths, here)[0:1, :]
        live = (col_at - count * col_series) >= (count - length)
        same = row_series == col_series
        seen = jnp.logical_and(live, col_at <= row_at)
        return jnp.logical_and(same, jnp.logical_or(seen, col_at == row_at))

    i_heads = links.take(half_tiles)
    s_heads = links.group()

    def head_slot(j):
        return span(j * tile, tile)

    def attend(i, _):
        h, j = i % 2, i // 2
        number = h * half_tiles + j
        rows = turn_rows(i)
        token_load(i).wait()

        @pl.when(i == 0)
        def _():
            for load in loads[:early]:
                load.wait()

        xhat, _r = norm_parts(tokens[rows, :].astype(F32))
        first_low[rows, :] = (xhat * row(first_gain) + row(first_shift)).astype(BF16)

        normed = first_low[rows, :]
        q = dot(normed, query_weight[...]).astype(BF16)
        k = dot(normed, key_weight[...]).astype(BF16)
        v = dot(normed, value_weight[...]).astype(BF16)
        queries[rows, :] = q
        key_rows[rows, :] = k
        value_rows[rows, :] = v

        allowed = allowed_of(number)
        for head in range(heads_here):
            at = slice(head * DH, (head + 1) * DH)
            scores = jnp.where(allowed, dot_nt(q[:, at], k[:, at]) * scale_factor, -1e30)
            numerator = jnp.exp(scores - jnp.max(scores, axis=-1, keepdims=True))
            share = numerator / jnp.sum(numerator, axis=-1, keepdims=True)
            probs[number * heads_here + head] = share
            heads_own[rows, at] = dot(share.astype(BF16), v[:, at]).astype(BF16)
        slot = heads_full.at[head_slot(j), lanes(t * cols, cols)]

        @pl.when(h == c)
        def _():
            heads_full[head_slot(j), lanes(t * cols, cols)] = heads_own[rows, :]
            links.copy(heads_own.at[rows, :], slot, s_heads, i_heads + j, opp).start()

        @pl.when(h != c)
        def _():
            links.copy(heads_own.at[rows, :], slot, s_heads, i_heads + j, sib).start()
            links.copy(heads_own.at[rows, :], slot, s_heads, i_heads + j, diag).start()

        @pl.when(i == 1)
        def _():
            share_first()

        return 0

    lax.fori_loop(0, n_tiles, attend, 0)

    share_next()

    i_second = links.take(half_tiles)
    s_second = links.group()
    vec[...] = jnp.zeros_like(vec)

    def in_turn(i):
        return jnp.where(i % 2 == 0, own_start, sib_start) + (i // 2) * tile

    def feed(i):
        rows = span(in_turn(i), tile)
        if i % 2 == 1:
            links.got(second_low.at[rows, :], i_second + i // 2)
        u = dot(second_low[rows, :], up_weight[...]) + row(up_bias)
        big = 0.5 * (1.0 + lax.erf(u * (1.0 / math.sqrt(2.0))))
        act[rows, :] = (u * big).astype(BF16)
        slope = big + u * (jnp.exp(-0.5 * u * u) * (1.0 / math.sqrt(2.0 * math.pi)))
        grad = (dot_nt(cotangent[rows, :], down_weight[...]) * slope).astype(BF16)
        ugp[rows, :] = grad
        vec[6:7, 0:hidden] += jnp.sum(grad.astype(F32), axis=0, keepdims=True)

    def project(j):
        if j == 0:
            for load in loads[early:]:
                load.wait()
            share_last()
        here = head_slot(j)
        links.got(heads_full.at[here, 0 : 3 * cols], i_heads + j)
        rows = span(own_start + j * tile, tile)
        v = tokens[rows, :].astype(F32) + dot(heads_full[here, :], wo_all[...]) + row(output_bias)
        residual[here, :] = v
        xhat, _r = norm_parts(v)
        second_low[rows, :] = (xhat * row(second_gain) + row(second_shift)).astype(BF16)
        links.copy(
            second_low.at[rows, :], second_low.at[rows, :], s_second, i_second + j, sib
        ).start()

    class Tensor:
        def __init__(self, grads, rx, rz, rm, out):
            self.grads, self.rx, self.rz, self.rm, self.out = grads, rx, rz, rm, out

    tensors = {
        "D": Tensor(g_down, rx_down, rz_down, rm_down, down_out),
        "U": Tensor(g_up, rx_up, rz_up, rm_up, up_out),
        "O": Tensor(g_output, rx_output, rz_output, rm_output, output_out),
        "Q": Tensor(g_qkv, rx_qkv, rz_qkv, rm_qkv, qkv_out),
    }

    class Part:
        def __init__(self, tensor, start, size):
            self.size = size // 2
            self.start = start
            here = pl.ds(start // 2, self.size)
            self.grads, self.out = tensor.grads, tensor.out
            self.rx, self.rz, self.rm = (
                ref.at[here, :] for ref in (tensor.rx, tensor.rz, tensor.rm)
            )
            self.index = links.take(4)
            self.group = links.group()

        def half_at(self, which):
            return span(self.start + which * self.size, self.size)

        def send(self, src, dst, message, device):
            links.copy(src, dst, self.group, self.index + message, device).start()

        def got(self, dst, message):
            links.got(dst, self.index + message)

        def add(self, rows, came):
            return (self.grads[rows, :].astype(F32) + came[...].astype(F32)).astype(BF16)

        def sent(self, copies):
            links.sent(self.grads.at[0 : copies * self.size, :], self.group)

    class PartX(Part):
        def begin(self):
            self.send(self.grads.at[self.half_at(1 - x), :], self.rx, 0, xp)

        def step(self, number):
            mine = self.half_at(x)
            grads, out = self.grads.at[mine, :], self.out.at[mine, :]
            if number == 1:
                self.got(self.rx, 0)
                self.grads[mine, :] = self.add(mine, self.rx)

                @pl.when(is_end)
                def _():
                    self.send(grads, self.rz, 1, adj)

            if number == 2:

                @pl.when(is_mid)
                def _():
                    self.got(self.rz, 1)
                    self.grads[mine, :] = self.add(mine, self.rz)
                    self.send(grads, self.rm, 2, mid)

            if number == 3:

                @pl.when(is_mid)
                def _():
                    self.got(self.rm, 2)
                    self.out[mine, :] = self.add(mine, self.rm)
                    self.send(out, out, 1, adj)
                    self.send(out, out, 3, xp)

            if number == 4:

                @pl.when(is_end)
                def _():
                    self.got(out, 1)
                    self.send(out, out, 3, xp)

        def end(self):
            self.got(self.out.at[self.half_at(1 - x), :], 3)

            @pl.when(is_end)
            def _():
                self.sent(3)

            @pl.when(is_mid)
            def _():
                self.sent(4)

    class PartZ(Part):
        def begin(self):
            far = self.grads.at[self.half_at(1 - side), :]

            @pl.when(is_end)
            def _():
                self.send(far, self.rz, 0, adj)

        def step(self, number):
            near, far = self.half_at(side), self.half_at(1 - side)

            @pl.when(is_end if number in (3, 4) else is_mid)
            def _():
                if number == 1:
                    self.got(self.rz, 0)
                    self.grads[far, :] = self.add(far, self.rz)
                    self.send(self.grads.at[far, :], self.rm, 1, mid)
                if number == 2:
                    self.got(self.rm, 1)
                    self.grads[near, :] = self.add(near, self.rm)
                    self.send(self.grads.at[near, :], self.rz, 0, adj)
                if number == 3:
                    self.got(self.rz, 0)
                    self.grads[near, :] = self.add(near, self.rz)
                    self.send(self.grads.at[near, :], self.rx, 1, xp)
                if number == 4:
                    self.got(self.rx, 1)
                    self.out[near, :] = self.add(near, self.rx)
                    self.send(self.out.at[near, :], self.out.at[near, :], 2, adj)
                if number == 5:
                    self.got(self.out.at[near, :], 2)
                    self.send(self.out.at[near, :], self.out.at[near, :], 3, mid)
                if number == 6:
                    self.got(self.out.at[far, :], 3)
                    self.send(self.out.at[far, :], self.out.at[far, :], 2, adj)

        def end(self):
            near, far = self.half_at(side), self.half_at(1 - side)

            @pl.when(is_end)
            def _():
                self.got(self.out.at[far, :], 2)
                self.sent(3)

            @pl.when(is_mid)
            def _():
                self.sent(4)

    parts = [
        {"a": PartX, "d": PartZ}[kind](tensors[name], start, size)
        for name, start, size, kind in PARTS
    ]

    def begin_parts(name, first, size):
        for (which, start, rows, _kind), part in zip(PARTS, parts, strict=True):
            if which == name and first < start + rows <= first + size:
                part.begin()

    block = 256

    def down_grads(i):
        at = slice(i * block, (i + 1) * block)
        g_down[at, :] = dot_tn(act[:, at], cotangent[...]).astype(BF16)
        begin_parts("D", i * block, block)

    def up_grads(i):
        at = slice(i * block, (i + 1) * block)
        g_up[at, :] = dot_tn(second_low[:, at], ugp[...]).astype(BF16)
        begin_parts("U", i * block, block)

    def output_grads(_i):
        g_output[...] = dot_tn(heads_own[...], residual_low[...]).astype(BF16)
        begin_parts("O", 0, cols)

    def qkv_grads(i):
        at = slice(i * block, (i + 1) * block)
        g_qkv[at, :] = dot_tn(first_low[:, at], dqkv[...]).astype(BF16)
        begin_parts("Q", i * block, block)

    class RowSum:
        def __init__(self, number, part):
            self.snd, self.r1, self.cs, self.r2 = (mail.at[4 * number + n] for n in range(4))
            self.part = part
            self.index = links.take(2 * half_tiles)
            self.group = links.group()

        def far(self, j):
            here = head_slot(j)
            self.snd[here, :] = self.part(span(sib_start + j * tile, tile)).astype(BF16)
            links.copy(
                self.snd.at[here, :], self.r1.at[here, :], self.group, self.index + j, sib
            ).start()

        def near(self, j):
            here = head_slot(j)
            mine = self.part(span(own_start + j * tile, tile))
            links.got(self.r1.at[here, :], self.index + j)
            self.cs[here, :] = (mine + self.r1[here, :].astype(F32)).astype(BF16)
            links.copy(
                self.cs.at[here, :],
                self.r2.at[here, :],
                self.group,
                self.index + half_tiles + j,
                opp,
            ).start()

        def rows(self, j):
            here = head_slot(j)
            links.got(self.r2.at[here, :], self.index + half_tiles + j)
            return self.cs[here, :].astype(F32) + self.r2[here, :].astype(F32)

        def end(self):
            links.sent(first_low, self.group)

    second_sum = RowSum(0, lambda rows: dot_nt(ugp[rows, :], up_weight[...]))
    out_sum = RowSum(1, lambda rows: dot(act[rows, :], down_weight[...]))
    first_sum = RowSum(
        2,
        lambda rows: dot_nt(dqkv[rows, 0:cols], query_weight[...])
        + dot_nt(dqkv[rows, cols : 2 * cols], key_weight[...])
        + dot_nt(dqkv[rows, 2 * cols : 3 * cols], value_weight[...]),
    )
    row_sums = (second_sum, out_sum, first_sum)

    i_back = links.take(half_tiles)
    s_back = links.group()

    def add_to(at, value):
        vec[at : at + 1, :] += jnp.sum(value, axis=0, keepdims=True)

    def norm_back(incoming, xhat, r, gain):
        weighted = incoming * gain
        return r * (
            weighted
            - jnp.mean(weighted, axis=-1, keepdims=True)
            - xhat * jnp.mean(weighted * xhat, axis=-1, keepdims=True)
        )

    def second_back(j):
        local = head_slot(j)
        rows = span(own_start + j * tile, tile)
        incoming = second_sum.rows(j)
        xhat, r = norm_parts(residual[local, :])
        given = cotangent[rows, :].astype(F32)
        grad = given + norm_back(incoming, xhat, r, row(second_gain))
        residual_grad[local, :] = grad
        residual_low[rows, :] = grad.astype(BF16)
        links.copy(
            residual_low.at[rows, :], residual_low.at[rows, :], s_back, i_back + j, sib
        ).start()
        add_to(2, incoming * xhat)
        add_to(3, incoming)
        add_to(4, grad)
        add_to(5, given)

    def attend_back(i):
        start = in_turn(i)
        rows = span(start, tile)
        number = start // tile
        if i % 2 == 1:
            links.got(residual_low.at[rows, :], i_back + i // 2)
        grads = dot_nt(residual_low[rows, :], wo_all[own_wo, :]).astype(BF16)
        for head in range(heads_here):
            at = slice(head * DH, (head + 1) * DH)
            share = probs[number * heads_here + head]
            q, k, v = queries[rows, at], key_rows[rows, at], value_rows[rows, at]
            share_grad = dot_nt(grads[:, at], v)
            inner = jnp.sum(share * share_grad, axis=-1, keepdims=True)
            scores_grad = (share * (share_grad - inner)).astype(BF16)
            dqkv[rows, head * DH : (head + 1) * DH] = (
                dot(scores_grad, k) * scale_factor
            ).astype(BF16)
            dqkv[rows, cols + head * DH : cols + (head + 1) * DH] = (
                dot_tn(scores_grad, q) * scale_factor
            ).astype(BF16)
            dqkv[rows, 2 * cols + head * DH : 2 * cols + (head + 1) * DH] = dot_tn(
                share.astype(BF16), grads[:, at]
            ).astype(BF16)

    i_out = links.take(2)
    s_out = links.group()

    def finished(j, number, out, values):
        rows = span(own_start + j * tile, tile)
        out[rows, :] = values.astype(BF16)
        links.copy(out.at[rows, :], out.at[rows, :], s_out, i_out + number, sib).start()

    def finish_out(j):
        local = head_slot(j)
        finished(j, 0, block_out, residual[local, :] + out_sum.rows(j) + row(down_bias))

    def first_back(j):
        local = head_slot(j)
        rows = span(own_start + j * tile, tile)
        incoming = first_sum.rows(j)
        xhat, r = norm_parts(tokens[rows, :].astype(F32))
        grad = residual_grad[local, :] + norm_back(incoming, xhat, r, row(first_gain))
        finished(j, 1, token_grad, grad)
        add_to(0, incoming * xhat)
        add_to(1, incoming)

    i_vec = links.take(3)
    s_vec = [links.group() for _ in range(3)]
    part = width // 8
    mine_at = lanes(dp * part, part)
    seven = vec_parts.at[0:7]

    def vectors(number):
        if number == 0:
            links.copy(vec, vec_sib, s_vec[0], i_vec, sib).start()
        if number == 1:
            links.got(vec_sib, i_vec)
            links.sent(vec, s_vec[0])
            at_row = lax.broadcasted_iota(jnp.int32, vec.shape, 0)
            vec[...] = vec[...] + jnp.where(at_row < 6, vec_sib[...], 0.0)
            vec_parts[dp] = vec[:, mine_at]
            for peer in dp_peers:
                links.copy(
                    vec.at[:, lanes(peer[0] * part, part)],
                    vec_parts.at[dp],
                    s_vec[1],
                    i_vec + 1,
                    peer,
                ).start()
        if number == 2:
            links.got(seven, i_vec + 1)
            total = vec_parts[0]
            for k in range(1, 8):
                total = total + vec_parts[k]
            vec_sum[...] = total
            vec_out[:, mine_at] = total
            for peer in dp_peers:
                links.copy(vec_sum, vec_out.at[:, mine_at], s_vec[2], i_vec + 2, peer).start()
        if number == 3:
            links.got(seven, i_vec + 2)

    tasks = {
        "D": down_grads,
        "U": up_grads,
        "O": output_grads,
        "Q": qkv_grads,
        "S": second_sum.far,
        "T": second_sum.near,
        "V": out_sum.far,
        "W": out_sum.near,
        "F": first_sum.far,
        "G": first_sum.near,
        "B": second_back,
        "A": attend_back,
        "X": finish_out,
        "Y": first_back,
        "Z": vectors,
        "P": project,
        "E": feed,
    }
    for name in ORDER:
        if "." in name:
            number, step = name.removeprefix("e").split(".")
            parts[int(number)].step(int(step))
        else:
            tasks[name[0]](int(name[1:]))

    vectors(3)

    for each in parts:
        each.end()
    links.sent(wo_all.at[0 : 3 * cols, :], s_wo)
    links.sent(heads_full.at[:, 0 : 3 * cols], s_heads)
    links.sent(second_low.at[0:half, :], s_second)
    links.sent(residual_low.at[0:half, :], s_back)
    for each in row_sums:
        each.end()
    for number, out in enumerate((block_out, token_grad)):
        links.got(out.at[other_rows, :], i_out + number)
    links.sent(first_low, s_out)
    links.sent(seven, s_vec[1])
    links.sent(seven, s_vec[2])


def results_kernel(cols, hidden, *refs):
    qkv, down, up, output, block, token, vec = refs[:7]
    outs, small, wide, sems = refs[7:15], refs[15:22], refs[22:28], refs[28]
    writes = [
        pltpu.make_async_copy(src, dst, sems.at[n])
        for n, (src, dst) in enumerate(zip((block, token, *wide), outs, strict=True))
    ]
    writes[0].start()
    writes[1].start()
    for n in range(3):
        wide[n][...] = qkv[:, n * cols : (n + 1) * cols].astype(F32)
        writes[2 + n].start()
    for n, grads in enumerate((down, up, output)):
        wide[3 + n][...] = grads[...].astype(F32)
        writes[5 + n].start()
    small[0][...] = vec[6, 0:hidden]
    for n, out in enumerate(small[1:]):
        out[...] = vec[n, :]
    for write in writes:
        write.wait()


def kernel_shards(*args):
    tokens, lengths = args[0], args[1]
    n_rows, width = tokens.shape
    count = n_rows // lengths.shape[0]
    tile = 16 * count
    half = n_rows // 2
    cols = args[2].shape[1]
    hidden = args[6].shape[1]
    vmem = pltpu.VMEM
    grads = ((hidden, width), (width, hidden), (cols, width), (width, 3 * cols))
    halves = [(r // 2, n) for r, n in grads]
    any_space = pl.BlockSpec(memory_space=pl.ANY)
    in_vmem = pl.BlockSpec(memory_space=pltpu.VMEM)
    scratch = [vmem(args[n].shape, args[n].dtype) for n in (1, 7, 9, 10, 11, 12, 13, 14)]
    scratch += [
        vmem((n_rows, width), BF16),
        vmem((n_rows, width), BF16),
        vmem((width, cols), BF16),
        vmem((width, cols), BF16),
        vmem((width, cols), BF16),
        vmem((width, width), BF16),
        vmem((width, hidden), BF16),
        vmem((hidden, width), BF16),
        vmem((n_rows, width), BF16),
        vmem((n_rows, cols), BF16),
        vmem((n_rows, cols), BF16),
        vmem((n_rows, cols), BF16),
        vmem((n_rows // tile * (cols // DH), tile, tile), F32),
        vmem((n_rows, cols), BF16),
        vmem((half, width), BF16),
        vmem((half, width), F32),
        vmem((n_rows, width), BF16),
        vmem((n_rows, hidden), BF16),
        vmem((n_rows, hidden), BF16),
        vmem((12, half, width), BF16),
        vmem((half, width), F32),
        vmem((n_rows, width), BF16),
        vmem((n_rows, 3 * cols), BF16),
    ]
    scratch += [vmem(s, BF16) for s in grads]
    for _ in range(3):
        scratch += [vmem(s, BF16) for s in halves]
    scratch += [
        vmem((8, width), F32),
        vmem((8, width), F32),
        vmem((8, 8, width // 8), F32),
        vmem((8, width // 8), F32),
        pltpu.SemaphoreType.DMA((N_SENDS,)),
        pltpu.SemaphoreType.DMA((N_RECVS,)),
        pltpu.SemaphoreType.DMA((N_LOCAL,)),
    ]
    block_out, token_grad, down, up, output, qkv, vec = pl.pallas_call(
        functools.partial(layer_kernel, count),
        out_shape=[
            vmem((n_rows, width), BF16),
            vmem((n_rows, width), BF16),
            *[vmem(s, BF16) for s in grads],
            vmem((8, width), F32),
        ],
        in_specs=[any_space] * len(args),
        out_specs=[in_vmem] * 7,
        scratch_shapes=scratch,
        compiler_params=pltpu.CompilerParams(
            collective_id=0, has_side_effects=True, vmem_limit_bytes=54 * 2**20
        ),
        name="layer",
    )(*args)

    split = (width, cols)
    f32_grads = [split] * 3 + list(grads[:3])
    vector = jax.ShapeDtypeStruct((width,), F32)
    rows = (n_rows, width)
    block_out, token_grad, query, key, value, down, up, output, up_bias, *vectors = pl.pallas_call(
        functools.partial(results_kernel, cols, hidden),
        out_shape=[jax.ShapeDtypeStruct(rows, BF16)] * 2
        + [jax.ShapeDtypeStruct(s, F32) for s in f32_grads]
        + [jax.ShapeDtypeStruct((hidden,), F32)]
        + [vector] * 6,
        in_specs=[in_vmem] * 7,
        out_specs=[any_space] * 8 + [in_vmem] * 7,
        scratch_shapes=[vmem(s, F32) for s in f32_grads] + [pltpu.SemaphoreType.DMA((8,))],
        compiler_params=pltpu.CompilerParams(vmem_limit_bytes=16 * 2**20),
        name="results",
    )(qkv, down, up, output, block_out, token_grad, vec)
    return (
        block_out,
        token_grad,
        query,
        key,
        value,
        output,
        up,
        up_bias,
        down,
        *vectors,
    )


def solution(mesh):
    fits = mesh.shape["dp"] == 8 and mesh.shape["tensor"] == 4
    return jax.shard_map(
        kernel_shards if fits else plain_shards,
        mesh=mesh,
        in_specs=(
            P("dp", None),
            P("dp"),
            P(None, "tensor"),
            P(None, "tensor"),
            P(None, "tensor"),
            P("tensor", None),
            P(None, "tensor"),
            P("tensor"),
            P("tensor", None),
            P(),
            P(),
            P(),
            P(),
            P(),
            P(),
            P("dp", None),
        ),
        out_specs=(
            P("dp", None),
            P("dp", None),
            P(None, "tensor"),
            P(None, "tensor"),
            P(None, "tensor"),
            P("tensor", None),
            P(None, "tensor"),
            P("tensor"),
            P("tensor", None),
            P(),
            P(),
            P(),
            P(),
            P(),
            P(),
        ),
        check_vma=False,
    )
```

```python
import functools
import math

import jax
import jax.numpy as jnp
from jax import lax
from jax.experimental import pallas as pl
from jax.experimental.pallas import tpu as pltpu
from jax.sharding import PartitionSpec as P

DH = 128


EPS = 1e-05


def norm_parts(rows, gain, shift):
    row_mean = jnp.mean(rows, axis=-1, keepdims=True)
    centred = rows - row_mean
    inverse = lax.rsqrt(jnp.mean(centred * centred, axis=-1, keepdims=True) + EPS)
    scaled = centred * inverse
    return (scaled * gain + shift, scaled, inverse)


def norm_back(incoming, scaled, inverse, gain):
    weighted = incoming * gain
    return inverse * (
        weighted
        - jnp.mean(weighted, axis=-1, keepdims=True)
        - scaled * jnp.mean(weighted * scaled, axis=-1, keepdims=True)
    )


def allowed_mask(lengths, count):
    position = jnp.arange(count, dtype=jnp.int32)
    start = (count - lengths)[:, None, None]
    query_pos = position[None, :, None]
    key_pos = position[None, None, :]
    return (key_pos >= start) & (key_pos <= query_pos) | (key_pos == query_pos)


def gelu_exact(values):
    return jax.nn.gelu(values, approximate=False)


def plain_shards(
    tokens,
    lengths,
    query_weight,
    key_weight,
    value_weight,
    output_weight,
    up_weight,
    up_bias,
    down_weight,
    first_gain,
    first_shift,
    second_gain,
    second_shift,
    output_bias,
    down_bias,
    cotangent,
):
    tok_rows = tokens.shape[0]
    series = lengths.shape[0]
    count = tok_rows // series
    heads_here = query_weight.shape[1] // DH
    groups = lax.axis_size("tensor")
    share = tok_rows // groups
    begin = lax.axis_index("tensor") * share
    scale_factor = 1.0 / math.sqrt(DH)
    allowed = allowed_mask(lengths, count)[:, None]

    def share_rows(array):
        return lax.dynamic_slice_in_dim(array, begin, share, 0)

    def to_heads(array):
        return array.reshape(series, count, heads_here, DH)

    def masked_scores(query_four, key_four):
        raw = (
            jnp.einsum("sqhd,skhd->shqk", query_four, key_four, preferred_element_type=jnp.float32)
            * scale_factor
        )
        return jnp.where(allowed, raw, -1e30)

    inputs = tokens.astype(jnp.float32)
    gain_one = first_gain.astype(jnp.float32)
    gain_two = second_gain.astype(jnp.float32)
    first_normed, first_scaled, first_inverse = norm_parts(
        inputs, gain_one, first_shift.astype(jnp.float32)
    )
    first_low = first_normed.astype(jnp.bfloat16)
    queries = jnp.dot(first_low, query_weight, preferred_element_type=jnp.float32).astype(
        jnp.bfloat16
    )
    key_rows = jnp.dot(first_low, key_weight, preferred_element_type=jnp.float32).astype(
        jnp.bfloat16
    )
    value_rows = jnp.dot(first_low, value_weight, preferred_element_type=jnp.float32).astype(
        jnp.bfloat16
    )
    query_four = to_heads(queries)
    key_four = to_heads(key_rows)
    value_four = to_heads(value_rows)
    scores = masked_scores(query_four, key_four)
    row_max = jnp.max(scores, axis=-1, keepdims=True)
    numerator = jnp.exp(scores - row_max)
    row_total = jnp.sum(numerator, axis=-1, keepdims=True)
    log_total = row_max + jnp.log(row_total)
    probs_low = (numerator / row_total).astype(jnp.bfloat16)
    heads_out = jnp.einsum(
        "shqk,skhd->sqhd", probs_low, value_four, preferred_element_type=jnp.float32
    )
    heads_low = heads_out.astype(jnp.bfloat16).reshape(tok_rows, heads_here * DH)
    attn_part = jnp.dot(heads_low, output_weight, preferred_element_type=jnp.float32)
    bias_attn = output_bias.astype(jnp.float32)
    bias_down = down_bias.astype(jnp.float32)
    grad_output = cotangent.astype(jnp.float32)
    attn_share = lax.psum_scatter(attn_part, "tensor", scatter_dimension=0, tiled=True)
    residual_share = share_rows(inputs) + attn_share + bias_attn
    second_share, second_scaled, second_inverse = norm_parts(
        residual_share, gain_two, second_shift.astype(jnp.float32)
    )
    second_low = lax.all_gather(second_share.astype(jnp.bfloat16), "tensor", axis=0, tiled=True)
    up_pre = jnp.dot(second_low, up_weight, preferred_element_type=jnp.float32) + up_bias.astype(
        jnp.float32
    )
    activated, gelu_pull = jax.vjp(gelu_exact, up_pre)
    activated = activated.astype(jnp.bfloat16)
    down_part = jnp.dot(activated, down_weight, preferred_element_type=jnp.float32)
    down_share = lax.psum_scatter(
        down_part.astype(jnp.bfloat16), "tensor", scatter_dimension=0, tiled=True
    ).astype(jnp.float32)
    out_share = (residual_share + down_share + bias_down).astype(jnp.bfloat16)
    block_out = lax.all_gather(out_share, "tensor", axis=0, tiled=True)
    down_bias_part = jnp.sum(share_rows(grad_output), axis=0)
    down_grad = jnp.einsum("tf,td->fd", activated, cotangent, preferred_element_type=jnp.float32)
    activated_grad = jnp.einsum(
        "td,fd->tf", cotangent, down_weight, preferred_element_type=jnp.float32
    )
    up_grad_pre = gelu_pull(activated_grad)[0].astype(jnp.bfloat16)
    up_bias_grad = jnp.sum(up_grad_pre.astype(jnp.float32), axis=0)
    up_grad = jnp.einsum("td,tf->df", second_low, up_grad_pre, preferred_element_type=jnp.float32)
    second_part = jnp.einsum(
        "tf,df->td", up_grad_pre, up_weight, preferred_element_type=jnp.float32
    )
    second_grad_share = lax.psum_scatter(second_part, "tensor", scatter_dimension=0, tiled=True)
    residual_share_grad = share_rows(grad_output) + norm_back(
        second_grad_share, second_scaled, second_inverse, gain_two
    )
    second_gain_part = jnp.sum(second_grad_share * second_scaled, axis=0)
    second_shift_part = jnp.sum(second_grad_share, axis=0)
    output_bias_part = jnp.sum(residual_share_grad, axis=0)
    residual_low = lax.all_gather(
        residual_share_grad.astype(jnp.bfloat16), "tensor", axis=0, tiled=True
    )
    output_grad = jnp.einsum(
        "tc,td->cd", heads_low, residual_low, preferred_element_type=jnp.float32
    )
    heads_grad = jnp.einsum(
        "td,cd->tc", residual_low, output_weight, preferred_element_type=jnp.float32
    )
    heads_grad_four = to_heads(heads_grad.astype(jnp.bfloat16))
    probs_again = jnp.exp(masked_scores(query_four, key_four) - log_total)
    value_rows_grad = jnp.einsum(
        "shqk,sqhd->skhd", probs_low, heads_grad_four, preferred_element_type=jnp.float32
    ).astype(jnp.bfloat16)
    probs_grad = jnp.einsum(
        "sqhd,skhd->shqk", heads_grad_four, value_four, preferred_element_type=jnp.float32
    )
    inner_sum = jnp.sum(probs_again * probs_grad, axis=-1, keepdims=True)
    scores_grad = (probs_again * (probs_grad - inner_sum)).astype(jnp.bfloat16)
    queries_grad = (
        (
            jnp.einsum("shqk,skhd->sqhd", scores_grad, key_four, preferred_element_type=jnp.float32)
            * scale_factor
        )
        .astype(jnp.bfloat16)
        .reshape(tok_rows, heads_here * DH)
    )
    key_rows_grad = (
        (
            jnp.einsum(
                "shqk,sqhd->skhd", scores_grad, query_four, preferred_element_type=jnp.float32
            )
            * scale_factor
        )
        .astype(jnp.bfloat16)
        .reshape(tok_rows, heads_here * DH)
    )
    value_rows_grad = value_rows_grad.reshape(tok_rows, heads_here * DH)
    query_grad = jnp.einsum(
        "td,tc->dc", first_low, queries_grad, preferred_element_type=jnp.float32
    )
    key_grad = jnp.einsum("td,tc->dc", first_low, key_rows_grad, preferred_element_type=jnp.float32)
    value_grad = jnp.einsum(
        "td,tc->dc", first_low, value_rows_grad, preferred_element_type=jnp.float32
    )
    first_part = (
        jnp.einsum("tc,dc->td", queries_grad, query_weight, preferred_element_type=jnp.float32)
        + jnp.einsum("tc,dc->td", key_rows_grad, key_weight, preferred_element_type=jnp.float32)
        + jnp.einsum("tc,dc->td", value_rows_grad, value_weight, preferred_element_type=jnp.float32)
    )
    first_grad_share = lax.psum_scatter(
        first_part.astype(jnp.bfloat16), "tensor", scatter_dimension=0, tiled=True
    ).astype(jnp.float32)
    scaled_share = share_rows(first_scaled)
    token_share = residual_share_grad + norm_back(
        first_grad_share, scaled_share, share_rows(first_inverse), gain_one
    )
    token_grad = lax.all_gather(token_share.astype(jnp.bfloat16), "tensor", axis=0, tiled=True)
    first_gain_part = jnp.sum(first_grad_share * scaled_share, axis=0)
    first_shift_part = jnp.sum(first_grad_share, axis=0)
    query_grad, key_grad, value_grad, output_grad, up_grad, up_bias_grad, down_grad = (
        lax.psum(query_grad.astype(jnp.bfloat16), "dp").astype(jnp.float32),
        lax.psum(key_grad.astype(jnp.bfloat16), "dp").astype(jnp.float32),
        lax.psum(value_grad.astype(jnp.bfloat16), "dp").astype(jnp.float32),
        lax.psum(output_grad.astype(jnp.bfloat16), "dp").astype(jnp.float32),
        lax.psum(up_grad.astype(jnp.bfloat16), "dp").astype(jnp.float32),
        lax.psum(up_bias_grad.astype(jnp.bfloat16), "dp").astype(jnp.float32),
        lax.psum(down_grad.astype(jnp.bfloat16), "dp").astype(jnp.float32),
    )
    (
        first_gain_grad,
        first_shift_grad,
        second_gain_grad,
        second_shift_grad,
        output_bias_grad,
        down_bias_grad,
    ) = lax.psum(
        (
            first_gain_part,
            first_shift_part,
            second_gain_part,
            second_shift_part,
            output_bias_part,
            down_bias_part,
        ),
        ("dp", "tensor"),
    )
    return (
        block_out,
        token_grad,
        query_grad,
        key_grad,
        value_grad,
        output_grad,
        up_grad,
        up_bias_grad,
        down_grad,
        first_gain_grad,
        first_shift_grad,
        second_gain_grad,
        second_shift_grad,
        output_bias_grad,
        down_bias_grad,
    )


F32 = jnp.float32
BF16 = jnp.bfloat16
MESH = pl.DeviceIdType.MESH
N_LOCAL = 19

TASKS = "DUOQSTVWFGBAXYZHKPE"
PARTS = (
    ("D", 0, 64, "a"), ("D", 64, 64, "d"), ("D", 128, 64, "a"), ("D", 192, 64, "a"),
    ("D", 256, 64, "d"), ("D", 320, 64, "a"), ("D", 384, 64, "a"), ("D", 448, 64, "a"),
    ("U", 0, 128, "a"), ("U", 128, 128, "d"), ("U", 256, 128, "d"), ("U", 384, 128, "a"),
    ("U", 512, 128, "a"), ("U", 640, 128, "a"), ("U", 768, 128, "b"), ("U", 896, 128, "a"),
    ("O", 0, 64, "a"), ("O", 64, 64, "b"), ("O", 128, 64, "a"), ("O", 192, 64, "d"),
    ("Q", 0, 64, "d"), ("Q", 64, 64, "a"), ("Q", 128, 64, "a"), ("Q", 192, 64, "a"),
    ("Q", 256, 64, "a"), ("Q", 320, 64, "a"), ("Q", 384, 64, "a"), ("Q", 448, 64, "d"),
    ("Q", 512, 64, "a"), ("Q", 576, 64, "a"), ("Q", 640, 64, "d"), ("Q", 704, 64, "d"),
    ("Q", 768, 64, "a"), ("Q", 832, 64, "a"), ("Q", 896, 64, "a"), ("Q", 960, 64, "d"),
)
ORDER = (
    1150, 1151, 1160, 1161, 1162, 1163, 1170, 1180, 1171, 1182, 1181, 1040, 1060, 1183, 1011, 1001,
    1041, 1061, 1050, 1000, 1010, 1013, 101, 111, 1051, 1070, 1012, 41, 51, 61, 11, 102, 71, 91,
    42, 1, 103, 12, 21, 43, 141, 92, 31, 13, 112, 81, 93, 52, 142, 1100, 151, 62, 113, 1110, 121,
    53, 72, 1111, 2, 63, 131, 1080, 114, 104, 54, 44, 22, 143, 73, 32, 1090, 64, 14, 94, 74, 3, 82,
    23, 152, 144, 122, 1101, 4, 1112, 24, 132, 33, 83, 1113, 153, 105, 1031, 45, 1032, 123, 1081,
    34, 15, 1033, 1030, 133, 1020, 84, 95, 1091, 271, 106, 1071, 154, 241, 301, 46, 251, 124, 311,
    16, 1120, 134, 261, 351, 96, 281, 201, 272, 291, 302, 171, 312, 321, 352, 191, 331, 202, 242,
    341, 273, 252, 172, 211, 303, 262, 221, 313, 192, 282, 231, 353, 243, 1130, 203, 292, 253, 322,
    263, 161, 332, 283, 342, 181, 193, 244, 254, 264, 284, 294, 324, 274, 304, 314, 293, 212, 323,
    173, 222, 333, 232, 343, 162, 213, 182, 174, 1131, 334, 223, 275, 1140, 354, 344, 204, 214,
    233, 305, 1141, 194, 224, 234, 315, 163, 355, 183, 205, 276, 306, 1142, 164, 184, 195, 316,
    356, 206, 1121, 196,
)

N_ROWS = {name: sum(p[2] for p in PARTS if p[0] == name) for name in "DUOQ"}
N_SENDS = len({(p[0], p[3], p[1] * 3 // N_ROWS[p[0]]) for p in PARTS}) + 11
N_RECVS = 3 * len(PARTS) + 38


def dot(a, b):
    return jnp.dot(a, b, preferred_element_type=F32)


def dot_nt(a, b):
    return lax.dot_general(a, b, (((1,), (1,)), ((), ())), preferred_element_type=F32)


def dot_tn(a, b):
    return lax.dot_general(a, b, (((0,), (0,)), ((), ())), preferred_element_type=F32)


def span(start, size):
    return pl.ds(pl.multiple_of(start, 16), size)


def lanes(start, size):
    return pl.ds(pl.multiple_of(start, 128), size)


class Links:
    def __init__(self, sends, recvs, anyone):
        self.sends, self.recvs, self.anyone = sends, recvs, anyone
        self.used = [0, 0]

    def group(self):
        self.used[0] += 1
        assert self.used[0] <= N_SENDS
        return self.used[0] - 1

    def take(self, count=1):
        first = self.used[1]
        self.used[1] += count
        assert self.used[1] <= N_RECVS
        return first

    def copy(self, src, dst, group, index, device):
        return pltpu.make_async_remote_copy(
            src_ref=src,
            dst_ref=dst,
            send_sem=self.sends.at[group],
            recv_sem=self.recvs.at[index],
            device_id=device,
            device_id_type=MESH,
        )

    def got(self, dst, index):
        self.copy(dst, dst, 0, index, self.anyone).wait_recv()

    def sent(self, like, group):
        self.copy(like, like, group, 0, self.anyone).wait_send()


def layer_kernel(
    count,
    tokens_hbm,
    lengths_hbm,
    query_hbm,
    key_hbm,
    value_hbm,
    output_hbm,
    up_hbm,
    up_bias_hbm,
    down_hbm,
    first_gain_hbm,
    first_shift_hbm,
    second_gain_hbm,
    second_shift_hbm,
    output_bias_hbm,
    down_bias_hbm,
    cotangent_hbm,
    block_out,
    token_grad,
    down_out,
    up_out,
    output_out,
    qkv_out,
    vec_out,
    lengths,
    up_bias,
    first_gain,
    first_shift,
    second_gain,
    second_shift,
    output_bias,
    down_bias,
    tokens,
    cotangent,
    query_weight,
    key_weight,
    value_weight,
    wo_all,
    up_weight,
    down_weight,
    first_low,
    queries,
    key_rows,
    value_rows,
    probs,
    heads_own,
    heads_full,
    residual,
    second_low,
    act,
    ugp,
    mail,
    residual_grad,
    residual_low,
    dqkv,
    g_down,
    g_up,
    g_output,
    g_qkv,
    rx_down,
    rx_up,
    rx_output,
    rx_qkv,
    rz_down,
    rz_up,
    rz_output,
    rz_qkv,
    rm_down,
    rm_up,
    rm_output,
    rm_qkv,
    vec,
    vec_sib,
    vec_parts,
    vec_sum,
    sends,
    recvs,
    local_sems,
):
    n_rows, width = tokens.shape
    half = n_rows // 2
    tile = 16 * count
    n_tiles = n_rows // tile
    half_tiles = n_tiles // 2
    heads_here = query_weight.shape[1] // DH
    cols = heads_here * DH
    hidden = up_weight.shape[1]
    scale_factor = 1.0 / math.sqrt(DH)

    dp = lax.axis_index("dp")
    t = lax.axis_index("tensor")
    x = dp % 2
    z = dp // 2
    c = t % 2
    t_sib = t + 1 - 2 * c
    t_opp = (t + 2) % 4
    t_diag = (t_sib + 2) % 4
    sib = (dp, t_sib)
    opp = (dp, t_opp)
    diag = (dp, t_diag)
    xp = (dp + 1 - 2 * x, t)
    adj = (dp + 2 - 4 * (z % 2), t)
    cross = (dp + 2 - 4 * (z % 2) + 1 - 2 * x, t)
    mid = ((3 - z) * 2 + x, t)
    is_mid = jnp.logical_or(z == 1, z == 2)
    is_end = jnp.logical_or(z == 0, z == 3)
    side = z // 2
    dp_peers = [((dp + k) % 8, t) for k in range(1, 8)]
    links = Links(sends, recvs, sib)

    barrier = pltpu.get_barrier_semaphore()
    peers = [sib, opp, diag, (adj[0], t_sib), (xp[0], t_sib)] + dp_peers
    for peer in peers:
        pl.semaphore_signal(barrier, inc=1, device_id=peer, device_id_type=MESH)

    other_rows = span((1 - c) * half, half)
    own_start = c * half
    sib_start = (1 - c) * half
    own_wo = span(t * cols, cols)

    def turn_rows(i):
        return span((i % 2) * half + (i // 2) * tile, tile)

    def token_load(i):
        rows = turn_rows(i)
        return pltpu.make_async_copy(tokens_hbm.at[rows, :], tokens.at[rows, :], local_sems.at[i])

    loads = [
        pltpu.make_async_copy(src, dst, local_sems.at[n_tiles + n])
        for n, (src, dst) in enumerate(
            (
                (query_hbm, query_weight),
                (key_hbm, key_weight),
                (value_hbm, value_weight),
                (lengths_hbm, lengths),
                (first_gain_hbm, first_gain),
                (first_shift_hbm, first_shift),
                (output_hbm, wo_all.at[own_wo, :]),
                (output_bias_hbm, output_bias),
                (second_gain_hbm, second_gain),
                (second_shift_hbm, second_shift),
                (up_bias_hbm, up_bias),
                (down_bias_hbm, down_bias),
                (up_hbm, up_weight),
                (down_hbm, down_weight),
                (cotangent_hbm, cotangent),
            )
        )
    ]
    token_load(0).start()
    early = 6
    for load in loads[:early]:
        load.start()
    for i in range(1, n_tiles):
        token_load(i).start()
    for load in loads[early:]:
        load.start()

    def row(ref):
        return ref[...].astype(F32).reshape(1, ref.shape[0])

    def norm_parts(v):
        e = v - jnp.mean(v, axis=-1, keepdims=True)
        r = lax.rsqrt(jnp.mean(e * e, axis=-1, keepdims=True) + EPS)
        return e * r, r

    piece = cols // 4
    quarter = x + 2 * (z % 2)

    def wo_piece(owner, number):
        return wo_all.at[span(owner * cols + number * piece, piece), :]

    i_wo = links.take(7)
    s_wo = links.group()
    by_y = links.copy(
        output_hbm.at[span(quarter * piece, piece), :], wo_piece(t, quarter), s_wo, i_wo, opp
    )
    whole_to_sib = links.copy(output_hbm, wo_all.at[own_wo, :], s_wo, i_wo + 1, sib)
    q_xp, q_adj = quarter + 1 - 2 * x, quarter + 2 - 4 * (z % 2)
    q_cross = q_adj + 1 - 2 * x
    mine = wo_piece(t_opp, quarter)
    to_x = links.copy(mine, mine, s_wo, i_wo + 2, xp)
    to_z = links.copy(mine, mine, s_wo, i_wo + 3, adj)

    def half_piece(number, which):
        return wo_all.at[span(t_opp * cols + number * piece + which * piece // 2, piece // 2), :]

    from_x, from_z = half_piece(q_xp, 0), half_piece(q_adj, 1)
    on_z = [links.copy(from_x, from_x, s_wo, i_wo + 4, (adj[0], v)) for v in (t, t_sib)]
    on_x = [links.copy(from_z, from_z, s_wo, i_wo + 5, (xp[0], v)) for v in (t, t_sib)]

    def relay(number):
        part = wo_piece(t_opp, number)
        links.copy(part, part, s_wo, i_wo + 6, sib).start()

    def share_first():
        links.got(mine, i_wo)
        to_x.start()
        to_z.start()
        relay(quarter)

    def share_next():
        links.got(wo_piece(t_opp, q_xp), i_wo + 2)
        for each in on_z:
            each.start()
        links.got(wo_piece(t_opp, q_adj), i_wo + 3)
        for each in on_x:
            each.start()
        relay(q_xp)
        relay(q_adj)

    def share_last():
        links.got(wo_piece(t_opp, q_cross), i_wo + 4)
        links.got(wo_piece(t_diag, q_cross), i_wo + 5)
        links.got(wo_all.at[span(t_diag * cols, 3 * piece), :], i_wo + 6)

    pl.semaphore_wait(barrier, len(peers))
    by_y.start()
    whole_to_sib.start()

    def allowed_of(number):
        def series_of(index):
            return jnp.floor((index + 0.5) * (1.0 / count))

        row_at = lax.broadcasted_iota(jnp.int32, (tile, 1), 0).astype(F32)
        col_at = lax.broadcasted_iota(jnp.int32, (1, tile), 1).astype(F32)
        row_series, col_series = series_of(row_at), series_of(col_at)
        n_series = lengths.shape[0]
        which = lax.broadcasted_iota(jnp.int32, (n_series, tile), 0).astype(F32)
        here = (which == col_series + (number * 16).astype(F32)).astype(BF16)
        all_lengths = jnp.broadcast_to(
            lengths[...].astype(F32).reshape(1, n_series), (8, n_series)
        ).astype(BF16)
        length = dot(all_lengths, here)[0:1, :]
        live = (col_at - count * col_series) >= (count - length)
        same = row_series == col_series
        seen = jnp.logical_and(live, col_at <= row_at)
        return jnp.logical_and(same, jnp.logical_or(seen, col_at == row_at))

    i_heads = links.take(2 * half_tiles + 1)
    i_near = i_heads + half_tiles + 1
    s_heads = links.group()

    def head_slot(j):
        return span(j * tile, tile)

    cut = tile // 32 * 16 + 16
    pieces = [[(0, tile)]] * (half_tiles - 1) + [[(0, cut), (cut, tile - cut)]]

    def attend(i, _):
        h, j = i % 2, i // 2
        number = h * half_tiles + j
        rows = turn_rows(i)
        token_load(i).wait()

        @pl.when(i == 0)
        def _():
            for load in loads[:early]:
                load.wait()

        xhat, _r = norm_parts(tokens[rows, :].astype(F32))
        first_low[rows, :] = (xhat * row(first_gain) + row(first_shift)).astype(BF16)

        normed = first_low[rows, :]
        q = dot(normed, query_weight[...]).astype(BF16)
        k = dot(normed, key_weight[...]).astype(BF16)
        v = dot(normed, value_weight[...]).astype(BF16)
        queries[rows, :] = q
        key_rows[rows, :] = k
        value_rows[rows, :] = v

        allowed = allowed_of(number)
        for head in range(heads_here):
            at = slice(head * DH, (head + 1) * DH)
            scores = jnp.where(allowed, dot_nt(q[:, at], k[:, at]) * scale_factor, -1e30)
            numerator = jnp.exp(scores - jnp.max(scores, axis=-1, keepdims=True))
            share = numerator / jnp.sum(numerator, axis=-1, keepdims=True)
            probs[number * heads_here + head] = share
            heads_own[rows, at] = dot(share.astype(BF16), v[:, at]).astype(BF16)
        mine = lanes(t * cols, cols)
        slot = heads_full.at[head_slot(j), mine]

        def over_y(device):
            @pl.when(j < half_tiles - 1)
            def _():
                links.copy(heads_own.at[rows, :], slot, s_heads, i_heads + j, device).start()

            @pl.when(j == half_tiles - 1)
            def _():
                for n, (start, size) in enumerate(pieces[-1]):
                    links.copy(
                        heads_own.at[span(h * half + j * tile + start, size), :],
                        heads_full.at[span(j * tile + start, size), mine],
                        s_heads,
                        i_heads + j + n,
                        device,
                    ).start()

        @pl.when(h == c)
        def _():
            heads_full[head_slot(j), mine] = heads_own[rows, :]
            over_y(opp)

        @pl.when(h != c)
        def _():
            links.copy(heads_own.at[rows, :], slot, s_heads, i_near + j, sib).start()
            over_y(diag)

        @pl.when(i == 1)
        def _():
            share_first()

        return 0

    lax.fori_loop(0, n_tiles, attend, 0)

    share_next()

    i_second = links.take(half_tiles + 1)
    s_second = links.group()
    vec[...] = jnp.zeros_like(vec)

    def in_turn(i):
        return jnp.where(i % 2 == 0, own_start, sib_start) + (i // 2) * tile

    chip = 2 * cols
    own_k, other_k = lanes((t // 2) * chip, chip), lanes((1 - t // 2) * chip, chip)

    def prepare(j):
        here = head_slot(j)
        if j == 0:
            for load in loads[early:]:
                load.wait()
            links.got(wo_all.at[span(t_sib * cols, cols), :], i_wo + 1)
        links.got(heads_full.at[here, lanes(t_sib * cols, cols)], i_near + j)
        residual[here, :] = dot(heads_full[here, own_k], wo_all[span((t // 2) * chip, chip), :])

    def down_slot(i):
        return residual_grad.at[head_slot(i // 2), (i % 2) * hidden : (i % 2 + 1) * hidden]

    def prepare_feed(i):
        down_slot(i)[...] = dot_nt(cotangent[span(in_turn(i), tile), :], down_weight[...])

    def feed(i):
        here = pieces[i // 2] if i % 2 == 1 else [(0, tile)]
        for n, (start, size) in enumerate(here):
            rows = span(in_turn(i) + start, size)
            if i % 2 == 1:
                links.got(second_low.at[rows, :], i_second + i // 2 + n)
            u = dot(second_low[rows, :], up_weight[...]) + row(up_bias)
            big = 0.5 * (1.0 + lax.erf(u * (1.0 / math.sqrt(2.0))))
            act[rows, :] = (u * big).astype(BF16)
            slope = big + u * (jnp.exp(-0.5 * u * u) * (1.0 / math.sqrt(2.0 * math.pi)))
            grad = (down_slot(i)[start : start + size, :] * slope).astype(BF16)
            ugp[rows, :] = grad
            vec[6:7, 0:hidden] += jnp.sum(grad.astype(F32), axis=0, keepdims=True)

    def project(j):
        if j == 0:
            share_last()
        for n, (start, size) in enumerate(pieces[j]):
            here = span(j * tile + start, size)
            links.got(heads_full.at[here, other_k], i_heads + j + n)
            rows = span(own_start + j * tile + start, size)
            other = dot(heads_full[here, other_k], wo_all[span((1 - t // 2) * chip, chip), :])
            v = tokens[rows, :].astype(F32) + (residual[here, :] + other) + row(output_bias)
            residual[here, :] = v
            xhat, _r = norm_parts(v)
            second_low[rows, :] = (xhat * row(second_gain) + row(second_shift)).astype(BF16)
            links.copy(
                second_low.at[rows, :], second_low.at[rows, :], s_second, i_second + j + n, sib
            ).start()

    class Tensor:
        def __init__(self, grads, rx, rz, rm, out, long):
            self.grads, self.rx, self.rz, self.rm, self.out = grads, rx, rz, rm, out
            self.long = long
            self.final = links.take()
            self.groups = {}

        def group_of(self, kind, start):
            key = kind, start * 3 // self.grads.shape[0]
            if key not in self.groups:
                self.groups[key] = links.group()
            return self.groups[key]

        def end(self, name):
            mine = [p for p in PARTS if p[0] == name]
            halves = {kind: sum(p[2] // 2 for p in mine if p[3] == kind) for kind in "abcdh"}
            for here, copies, came in (
                (is_mid, {"a": 4, "b": 5, "c": 4, "d": 4, "h": 4}, {"a": 1, "b": 0, "c": 1, "d": 0, "h": 1}),
                (is_end, {"a": 3, "b": 2, "c": 3, "d": 3, "h": 3}, {"a": 1, "b": 2, "c": 1, "d": 1, "h": 1}),
            ):

                @pl.when(here)
                def _(copies=copies, came=came):
                    rows = sum(came[kind] * halves[kind] for kind in "abcdh")
                    assert rows <= self.long.shape[0]
                    if rows > 0:
                        links.got(self.long.at[0:rows, :], self.final)
                    for (kind, which), group in self.groups.items():
                        rows = sum(
                            copies[kind] * p[2] // 2
                            for p in mine
                            if p[3] == kind and p[1] * 3 // self.grads.shape[0] == which
                        )
                        assert rows <= self.long.shape[0]
                        links.sent(self.long.at[0:rows, :], group)

    tensors = {
        "D": Tensor(g_down, rx_down, rz_down, rm_down, down_out, wo_all),
        "U": Tensor(g_up, rx_up, rz_up, rm_up, up_out, up_weight),
        "O": Tensor(g_output, rx_output, rz_output, rm_output, output_out, wo_all),
        "Q": Tensor(g_qkv, rx_qkv, rz_qkv, rm_qkv, qkv_out, dqkv),
    }

    class Part:
        def __init__(self, tensor, start, size, kind):
            self.size = size // 2
            self.start = start
            here = pl.ds(start // 2, self.size)
            self.grads, self.out = tensor.grads, tensor.out
            self.rx, self.rm = tensor.rx.at[here, :], tensor.rm.at[here, :]
            self.rz = tensor.rz.at[pl.ds(start, self.size), :]
            self.rz_whole = tensor.rz.at[pl.ds(start, size), :]
            self.index = links.take(3)
            self.final = tensor.final
            self.group = tensor.group_of(kind, start)

        def half_at(self, which):
            return span(self.start + which * self.size, self.size)

        def send(self, src, dst, message, device):
            links.copy(src, dst, self.group, self.index + message, device).start()

        def send_last(self, ref, device):
            links.copy(ref, ref, self.group, self.final, device).start()

        def got(self, dst, message):
            links.got(dst, self.index + message)

        def add(self, rows, came):
            return (self.grads[rows, :].astype(F32) + came[...].astype(F32)).astype(BF16)

    class PartX(Part):
        def begin(self):
            self.send(self.grads.at[self.half_at(1 - x), :], self.rx, 0, xp)

        def step(self, number):
            mine = self.half_at(x)
            grads, out = self.grads.at[mine, :], self.out.at[mine, :]
            if number == 1:
                self.got(self.rx, 0)
                self.grads[mine, :] = self.add(mine, self.rx)

                @pl.when(is_end)
                def _():
                    self.send(grads, self.rz, 1, adj)

            if number == 2:

                @pl.when(is_mid)
                def _():
                    self.got(self.rz, 1)
                    self.grads[mine, :] = self.add(mine, self.rz)
                    self.send(grads, self.rm, 2, mid)

            if number == 3:

                @pl.when(is_mid)
                def _():
                    self.got(self.rm, 2)
                    self.out[mine, :] = self.add(mine, self.rm)
                    self.send(out, out, 1, adj)
                    self.send_last(out, xp)

            if number == 4:

                @pl.when(is_end)
                def _():
                    self.got(out, 1)
                    self.send_last(out, xp)

    class PartE(Part):
        def begin(self):
            self.send(self.grads.at[self.half_at(1 - x), :], self.rx, 0, xp)

        def step(self, number):
            size = self.size // 2
            mine = self.half_at(x)
            near = span(self.start + x * self.size + side * size, size)
            far = span(self.start + x * self.size + (1 - side) * size, size)
            near_out, far_out = self.out.at[near, :], self.out.at[far, :]
            rz, rm = self.rz.at[0:size, :], self.rm.at[0:size, :]
            if number == 1:
                self.got(self.rx, 0)
                self.grads[mine, :] = self.add(mine, self.rx)

            @pl.when(is_end if number in (1, 4, 7) else is_mid)
            def _():
                if number == 1:
                    self.send(self.grads.at[far, :], rz, 1, adj)
                if number == 2:
                    self.got(rz, 1)
                    self.grads[far, :] = self.add(far, rz)
                    self.send(self.grads.at[far, :], rm, 2, mid)
                if number == 3:
                    self.got(rm, 2)
                    self.grads[near, :] = self.add(near, rm)
                    self.send(self.grads.at[near, :], rz, 1, adj)
                if number == 4:
                    self.got(rz, 1)
                    self.out[near, :] = self.add(near, rz)
                    self.send(near_out, near_out, 0, adj)
                    self.send_last(near_out, xp)
                if number == 5:
                    self.got(near_out, 0)
                    self.send(near_out, near_out, 1, mid)
                    self.send_last(near_out, xp)
                if number == 6:
                    self.got(far_out, 1)
                    self.send(far_out, far_out, 0, adj)
                    self.send_last(far_out, xp)
                if number == 7:
                    self.got(far_out, 0)
                    self.send_last(far_out, xp)

    class PartH(Part):
        def begin(self):
            @pl.when(is_end)
            def _():
                whole = self.grads.at[pl.ds(self.start, 2 * self.size), :]
                self.send(whole, self.rz_whole, 0, adj)

        def step(self, number):
            size = self.size // 2
            near, far = self.half_at(side), self.half_at(1 - side)
            near_at = self.start + side * self.size
            far_at = self.start + (1 - side) * self.size
            near_mine = span(near_at + x * size, size)
            near_other = span(near_at + (1 - x) * size, size)
            far_mine = span(far_at + x * size, size)
            near_out, far_out = self.out.at[near_mine, :], self.out.at[far_mine, :]
            rx = self.rx.at[0:size, :]

            @pl.when(is_end if number > 4 else is_mid)
            def _():
                if number == 1:
                    whole = pl.ds(self.start, 2 * self.size)
                    self.got(self.rz_whole, 0)
                    self.grads[whole, :] = self.add(whole, self.rz_whole)
                    self.send(self.grads.at[far, :], self.rm, 1, mid)
                if number == 2:
                    self.got(self.rm, 1)
                    self.grads[near, :] = self.add(near, self.rm)
                    self.send(self.grads.at[near_other, :], rx, 2, xp)
                if number == 3:
                    self.got(rx, 2)
                    self.out[near_mine, :] = self.add(near_mine, rx)
                    self.send(near_out, near_out, 0, adj)
                    self.send(near_out, near_out, 0, mid)
                    self.send_last(near_out, xp)
                if number == 4:
                    self.got(far_out, 0)
                    self.send(far_out, far_out, 1, adj)
                    self.send_last(far_out, xp)
                if number == 5:
                    self.got(near_out, 0)
                    self.send_last(near_out, xp)
                if number == 6:
                    self.got(far_out, 1)
                    self.send_last(far_out, xp)

    class PartZ(Part):
        def begin(self):
            far = self.grads.at[self.half_at(1 - side), :]

            @pl.when(is_end)
            def _():
                self.send(far, self.rz, 0, adj)

        def step(self, number):
            near, far = self.half_at(side), self.half_at(1 - side)
            near_out, far_out = self.out.at[near, :], self.out.at[far, :]

            @pl.when(is_end if number in (3, 4) else is_mid)
            def _():
                if number == 1:
                    self.got(self.rz, 0)
                    self.grads[far, :] = self.add(far, self.rz)
                    self.send(self.grads.at[far, :], self.rm, 1, mid)
                if number == 2:
                    self.got(self.rm, 1)
                    self.grads[near, :] = self.add(near, self.rm)
                    self.send(self.grads.at[near, :], self.rz, 0, adj)
                if number == 3:
                    self.got(self.rz, 0)
                    self.grads[near, :] = self.add(near, self.rz)
                    self.send(self.grads.at[near, :], self.rx, 1, xp)
                if number == 4:
                    self.got(self.rx, 1)
                    self.out[near, :] = self.add(near, self.rx)
                    self.send(near_out, near_out, 0, adj)
                if number == 5:
                    self.got(near_out, 0)
                    self.send(near_out, near_out, 2, mid)
                if number == 6:
                    self.got(far_out, 2)
                    self.send_last(far_out, adj)

    class PartM(Part):
        def begin(self):
            @pl.when(is_end)
            def _():
                whole = self.grads.at[pl.ds(self.start, 2 * self.size), :]
                self.send(whole, self.rz_whole, 0, adj)

        def step(self, number):
            near, far = self.half_at(side), self.half_at(1 - side)
            near_out, far_out = self.out.at[near, :], self.out.at[far, :]

            @pl.when(is_mid)
            def _():
                if number == 1:
                    whole = pl.ds(self.start, 2 * self.size)
                    self.got(self.rz_whole, 0)
                    self.grads[whole, :] = self.add(whole, self.rz_whole)
                    self.send(self.grads.at[far, :], self.rm, 1, mid)
                if number == 2:
                    self.got(self.rm, 1)
                    self.grads[near, :] = self.add(near, self.rm)
                    self.send(self.grads.at[near, :], self.rx, 2, xp)
                if number == 3:
                    self.got(self.rx, 2)
                    self.out[near, :] = self.add(near, self.rx)
                    self.send_last(near_out, adj)
                    self.send(near_out, near_out, 0, mid)
                if number == 4:
                    self.got(far_out, 0)
                    self.send_last(far_out, adj)

    parts = [
        {"a": PartX, "b": PartM, "c": PartE, "d": PartZ, "h": PartH}[kind](tensors[name], start, size, kind)
        for name, start, size, kind in PARTS
    ]

    def begin_parts(name, first, size):
        for (which, start, rows, _kind), part in zip(PARTS, parts, strict=True):
            if which == name and first < start + rows <= first + size:
                part.begin()

    block = 256

    def down_grads(i):
        at = slice(i * block, (i + 1) * block)
        g_down[at, :] = dot_tn(act[:, at], cotangent[...]).astype(BF16)
        begin_parts("D", i * block, block)

    def up_grads(i):
        at = slice(i * block, (i + 1) * block)
        g_up[at, :] = dot_tn(second_low[:, at], ugp[...]).astype(BF16)
        begin_parts("U", i * block, block)

    def output_grads(_i):
        g_output[...] = dot_tn(heads_own[...], residual_low[...]).astype(BF16)
        begin_parts("O", 0, cols)

    def qkv_grads(i):
        at = slice(i * block, (i + 1) * block)
        g_qkv[at, :] = dot_tn(first_low[:, at], dqkv[...]).astype(BF16)
        begin_parts("Q", i * block, block)

    class RowSum:
        def __init__(self, number, part, snd):
            self.snd = snd
            self.r1, self.cs, self.r2 = (mail.at[3 * number + n] for n in range(3))
            self.part = part
            self.index = links.take(2 * half_tiles)
            self.group = links.group()

        def far(self, j):
            here = head_slot(j)
            self.snd[here, :] = self.part(span(sib_start + j * tile, tile)).astype(BF16)
            links.copy(
                self.snd.at[here, :], self.r1.at[here, :], self.group, self.index + j, sib
            ).start()

        def near(self, j):
            here = head_slot(j)
            mine = self.part(span(own_start + j * tile, tile))
            links.got(self.r1.at[here, :], self.index + j)
            self.cs[here, :] = (mine + self.r1[here, :].astype(F32)).astype(BF16)
            links.copy(
                self.cs.at[here, :],
                self.r2.at[here, :],
                self.group,
                self.index + half_tiles + j,
                opp,
            ).start()

        def rows(self, j):
            here = head_slot(j)
            links.got(self.r2.at[here, :], self.index + half_tiles + j)
            return self.cs[here, :].astype(F32) + self.r2[here, :].astype(F32)

        def end(self):
            links.sent(first_low, self.group)

    second_sum = RowSum(0, lambda rows: dot_nt(ugp[rows, :], up_weight[...]), mail.at[9])
    out_sum = RowSum(1, lambda rows: dot(act[rows, :], down_weight[...]), mail.at[10])
    first_sum = RowSum(
        2,
        lambda rows: dot_nt(dqkv[rows, 0:cols], query_weight[...])
        + dot_nt(dqkv[rows, cols : 2 * cols], key_weight[...])
        + dot_nt(dqkv[rows, 2 * cols : 3 * cols], value_weight[...]),
        heads_full,
    )
    row_sums = (second_sum, out_sum, first_sum)

    i_back = links.take(half_tiles)
    s_back = links.group()

    def add_to(at, value):
        vec[at : at + 1, :] += jnp.sum(value, axis=0, keepdims=True)

    def norm_back(incoming, xhat, r, gain):
        weighted = incoming * gain
        return r * (
            weighted
            - jnp.mean(weighted, axis=-1, keepdims=True)
            - xhat * jnp.mean(weighted * xhat, axis=-1, keepdims=True)
        )

    def second_back(j):
        local = head_slot(j)
        rows = span(own_start + j * tile, tile)
        incoming = second_sum.rows(j)
        xhat, r = norm_parts(residual[local, :])
        given = cotangent[rows, :].astype(F32)
        grad = given + norm_back(incoming, xhat, r, row(second_gain))
        residual_grad[local, :] = grad
        residual_low[rows, :] = grad.astype(BF16)
        links.copy(
            residual_low.at[rows, :], residual_low.at[rows, :], s_back, i_back + j, sib
        ).start()
        add_to(2, incoming * xhat)
        add_to(3, incoming)
        add_to(4, grad)
        add_to(5, given)

    def attend_back(i):
        start = in_turn(i)
        rows = span(start, tile)
        number = start // tile
        if i % 2 == 1:
            links.got(residual_low.at[rows, :], i_back + i // 2)
        grads = dot_nt(residual_low[rows, :], wo_all[own_wo, :]).astype(BF16)
        for head in range(heads_here):
            at = slice(head * DH, (head + 1) * DH)
            share = probs[number * heads_here + head]
            q, k, v = queries[rows, at], key_rows[rows, at], value_rows[rows, at]
            share_grad = dot_nt(grads[:, at], v)
            inner = jnp.sum(share * share_grad, axis=-1, keepdims=True)
            scores_grad = (share * (share_grad - inner)).astype(BF16)
            dqkv[rows, head * DH : (head + 1) * DH] = (
                dot(scores_grad, k) * scale_factor
            ).astype(BF16)
            dqkv[rows, cols + head * DH : cols + (head + 1) * DH] = (
                dot_tn(scores_grad, q) * scale_factor
            ).astype(BF16)
            dqkv[rows, 2 * cols + head * DH : 2 * cols + (head + 1) * DH] = dot_tn(
                share.astype(BF16), grads[:, at]
            ).astype(BF16)

    i_out = links.take(2)
    s_out = links.group()

    def finished(j, number, out, values):
        rows = span(own_start + j * tile, tile)
        out[rows, :] = values.astype(BF16)
        links.copy(out.at[rows, :], out.at[rows, :], s_out, i_out + number, sib).start()

    def finish_out(j):
        local = head_slot(j)
        finished(j, 0, block_out, residual[local, :] + out_sum.rows(j) + row(down_bias))

    def first_back(j):
        local = head_slot(j)
        rows = span(own_start + j * tile, tile)
        incoming = first_sum.rows(j)
        xhat, r = norm_parts(tokens[rows, :].astype(F32))
        grad = residual_grad[local, :] + norm_back(incoming, xhat, r, row(first_gain))
        finished(j, 1, token_grad, grad)
        add_to(0, incoming * xhat)
        add_to(1, incoming)

    i_vec = links.take(3)
    s_vec = [links.group() for _ in range(3)]
    part = width // 8
    mine_at = lanes(dp * part, part)
    seven = vec_parts.at[0:7]

    def vectors(number):
        if number == 0:
            links.copy(vec, vec_sib, s_vec[0], i_vec, sib).start()
        if number == 1:
            links.got(vec_sib, i_vec)
            links.sent(vec, s_vec[0])
            at_row = lax.broadcasted_iota(jnp.int32, vec.shape, 0)
            vec[...] = vec[...] + jnp.where(at_row < 6, vec_sib[...], 0.0)
            vec_parts[dp] = vec[:, mine_at]
            for peer in dp_peers:
                links.copy(
                    vec.at[:, lanes(peer[0] * part, part)],
                    vec_parts.at[dp],
                    s_vec[1],
                    i_vec + 1,
                    peer,
                ).start()
        if number == 2:
            links.got(seven, i_vec + 1)
            total = vec_parts[0]
            for k in range(1, 8):
                total = total + vec_parts[k]
            vec_sum[...] = total
            vec_out[:, mine_at] = total
            for peer in dp_peers:
                links.copy(vec_sum, vec_out.at[:, mine_at], s_vec[2], i_vec + 2, peer).start()
        if number == 3:
            links.got(seven, i_vec + 2)

    tasks = {
        "D": down_grads,
        "U": up_grads,
        "O": output_grads,
        "Q": qkv_grads,
        "S": second_sum.far,
        "T": second_sum.near,
        "V": out_sum.far,
        "W": out_sum.near,
        "F": first_sum.far,
        "G": first_sum.near,
        "B": second_back,
        "A": attend_back,
        "X": finish_out,
        "Y": first_back,
        "Z": vectors,
        "H": prepare,
        "K": prepare_feed,
        "P": project,
        "E": feed,
    }
    for code in ORDER:
        if code < 1000:
            parts[code // 10].step(code % 10)
        else:
            tasks[TASKS[code // 10 - 100]](code % 10)

    vectors(3)

    for name, tensor in tensors.items():
        tensor.end(name)
    links.sent(wo_all.at[0 : 3 * cols, :], s_wo)
    links.sent(heads_full.at[:, 0 : 3 * cols], s_heads)
    links.sent(second_low.at[0:half, :], s_second)
    links.sent(residual_low.at[0:half, :], s_back)
    for each in row_sums:
        each.end()
    for number, out in enumerate((block_out, token_grad)):
        links.got(out.at[other_rows, :], i_out + number)
    links.sent(first_low, s_out)
    links.sent(seven, s_vec[1])
    links.sent(seven, s_vec[2])


def results_kernel(cols, hidden, *refs):
    qkv, down, up, output, block, token, vec = refs[:7]
    outs, wide, small, sems = refs[7:22], refs[22:28], refs[28:35], refs[35]
    writes = [
        pltpu.make_async_copy(src, dst, sems.at[n])
        for n, (src, dst) in enumerate(zip((block, token, *wide, *small), outs, strict=True))
    ]
    writes[0].start()
    writes[1].start()
    small[0][...] = vec[6, 0:hidden]
    for n, ref in enumerate(small[1:]):
        ref[...] = vec[n, :]
    for write in writes[8:]:
        write.start()
    for n in range(3):
        wide[n][...] = qkv[:, n * cols : (n + 1) * cols].astype(F32)
        writes[2 + n].start()
    for n, grads in enumerate((down, up, output)):
        wide[3 + n][...] = grads[...].astype(F32)
        writes[5 + n].start()
    for write in writes:
        write.wait()


def kernel_shards(*args):
    tokens, lengths = args[0], args[1]
    n_rows, width = tokens.shape
    count = n_rows // lengths.shape[0]
    tile = 16 * count
    half = n_rows // 2
    cols = args[2].shape[1]
    hidden = args[6].shape[1]
    vmem = pltpu.VMEM
    grads = ((hidden, width), (width, hidden), (cols, width), (width, 3 * cols))
    halves = [(r // 2, n) for r, n in grads]
    any_space = pl.BlockSpec(memory_space=pl.ANY)
    in_vmem = pl.BlockSpec(memory_space=pltpu.VMEM)
    scratch = [vmem(args[n].shape, args[n].dtype) for n in (1, 7, 9, 10, 11, 12, 13, 14)]
    scratch += [
        vmem((n_rows, width), BF16),
        vmem((n_rows, width), BF16),
        vmem((width, cols), BF16),
        vmem((width, cols), BF16),
        vmem((width, cols), BF16),
        vmem((width, width), BF16),
        vmem((width, hidden), BF16),
        vmem((hidden, width), BF16),
        vmem((n_rows, width), BF16),
        vmem((n_rows, cols), BF16),
        vmem((n_rows, cols), BF16),
        vmem((n_rows, cols), BF16),
        vmem((n_rows // tile * (cols // DH), tile, tile), F32),
        vmem((n_rows, cols), BF16),
        vmem((half, width), BF16),
        vmem((half, width), F32),
        vmem((n_rows, width), BF16),
        vmem((n_rows, hidden), BF16),
        vmem((n_rows, hidden), BF16),
        vmem((11, half, width), BF16),
        vmem((half, width), F32),
        vmem((n_rows, width), BF16),
        vmem((n_rows, 3 * cols), BF16),
    ]
    scratch += [vmem(s, BF16) for s in grads]
    for shapes in (halves, grads, halves):
        scratch += [vmem(s, BF16) for s in shapes]
    scratch += [
        vmem((8, width), F32),
        vmem((8, width), F32),
        vmem((8, 8, width // 8), F32),
        vmem((8, width // 8), F32),
        pltpu.SemaphoreType.DMA((N_SENDS,)),
        pltpu.SemaphoreType.DMA((N_RECVS,)),
        pltpu.SemaphoreType.DMA((N_LOCAL,)),
    ]
    block_out, token_grad, down, up, output, qkv, vec = pl.pallas_call(
        functools.partial(layer_kernel, count),
        out_shape=[
            vmem((n_rows, width), BF16),
            vmem((n_rows, width), BF16),
            *[vmem(s, BF16) for s in grads],
            vmem((8, width), F32),
        ],
        in_specs=[any_space] * len(args),
        out_specs=[in_vmem] * 7,
        scratch_shapes=scratch,
        compiler_params=pltpu.CompilerParams(
            collective_id=0, has_side_effects=True, vmem_limit_bytes=56 * 2**20
        ),
        name="layer",
    )(*args)

    split = (width, cols)
    f32_grads = [split] * 3 + list(grads[:3])
    vector = jax.ShapeDtypeStruct((width,), F32)
    rows = (n_rows, width)
    block_out, token_grad, query, key, value, down, up, output, up_bias, *vectors = pl.pallas_call(
        functools.partial(results_kernel, cols, hidden),
        out_shape=[jax.ShapeDtypeStruct(rows, BF16)] * 2
        + [jax.ShapeDtypeStruct(s, F32) for s in f32_grads]
        + [jax.ShapeDtypeStruct((hidden,), F32)]
        + [vector] * 6,
        in_specs=[in_vmem] * 7,
        out_specs=[any_space] * 15,
        scratch_shapes=[vmem(s, F32) for s in (*f32_grads, (hidden,), *[(width,)] * 6)]
        + [pltpu.SemaphoreType.DMA((15,))],
        compiler_params=pltpu.CompilerParams(vmem_limit_bytes=16 * 2**20),
        name="results",
    )(qkv, down, up, output, block_out, token_grad, vec)
    return (
        block_out,
        token_grad,
        query,
        key,
        value,
        output,
        up,
        up_bias,
        down,
        *vectors,
    )


def solution(mesh):
    fits = mesh.shape["dp"] == 8 and mesh.shape["tensor"] == 4
    return jax.shard_map(
        kernel_shards if fits else plain_shards,
        mesh=mesh,
        in_specs=(
            P("dp", None),
            P("dp"),
            P(None, "tensor"),
            P(None, "tensor"),
            P(None, "tensor"),
            P("tensor", None),
            P(None, "tensor"),
            P("tensor"),
            P("tensor", None),
            P(),
            P(),
            P(),
            P(),
            P(),
            P(),
            P("dp", None),
        ),
        out_specs=(
            P("dp", None),
            P("dp", None),
            P(None, "tensor"),
            P(None, "tensor"),
            P(None, "tensor"),
            P("tensor", None),
            P(None, "tensor"),
            P("tensor"),
            P("tensor", None),
            P(),
            P(),
            P(),
            P(),
            P(),
            P(),
        ),
        check_vma=False,
    )
```

```python
import functools
import math

import jax
import jax.numpy as jnp
from jax import lax
from jax.experimental import pallas as pl
from jax.experimental.pallas import tpu as pltpu
from jax.sharding import PartitionSpec as P

DH = 128


EPS = 1e-05


def norm_parts(rows, gain, shift):
    row_mean = jnp.mean(rows, axis=-1, keepdims=True)
    centred = rows - row_mean
    inverse = lax.rsqrt(jnp.mean(centred * centred, axis=-1, keepdims=True) + EPS)
    scaled = centred * inverse
    return (scaled * gain + shift, scaled, inverse)


def norm_back(incoming, scaled, inverse, gain):
    weighted = incoming * gain
    return inverse * (
        weighted
        - jnp.mean(weighted, axis=-1, keepdims=True)
        - scaled * jnp.mean(weighted * scaled, axis=-1, keepdims=True)
    )


def allowed_mask(lengths, count):
    position = jnp.arange(count, dtype=jnp.int32)
    start = (count - lengths)[:, None, None]
    query_pos = position[None, :, None]
    key_pos = position[None, None, :]
    return (key_pos >= start) & (key_pos <= query_pos) | (key_pos == query_pos)


def gelu_exact(values):
    return jax.nn.gelu(values, approximate=False)


def plain_shards(
    tokens,
    lengths,
    query_weight,
    key_weight,
    value_weight,
    output_weight,
    up_weight,
    up_bias,
    down_weight,
    first_gain,
    first_shift,
    second_gain,
    second_shift,
    output_bias,
    down_bias,
    cotangent,
):
    tok_rows = tokens.shape[0]
    series = lengths.shape[0]
    count = tok_rows // series
    heads_here = query_weight.shape[1] // DH
    groups = lax.axis_size("tensor")
    share = tok_rows // groups
    begin = lax.axis_index("tensor") * share
    scale_factor = 1.0 / math.sqrt(DH)
    allowed = allowed_mask(lengths, count)[:, None]

    def share_rows(array):
        return lax.dynamic_slice_in_dim(array, begin, share, 0)

    def to_heads(array):
        return array.reshape(series, count, heads_here, DH)

    def masked_scores(query_four, key_four):
        raw = (
            jnp.einsum("sqhd,skhd->shqk", query_four, key_four, preferred_element_type=jnp.float32)
            * scale_factor
        )
        return jnp.where(allowed, raw, -1e30)

    inputs = tokens.astype(jnp.float32)
    gain_one = first_gain.astype(jnp.float32)
    gain_two = second_gain.astype(jnp.float32)
    first_normed, first_scaled, first_inverse = norm_parts(
        inputs, gain_one, first_shift.astype(jnp.float32)
    )
    first_low = first_normed.astype(jnp.bfloat16)
    queries = jnp.dot(first_low, query_weight, preferred_element_type=jnp.float32).astype(
        jnp.bfloat16
    )
    key_rows = jnp.dot(first_low, key_weight, preferred_element_type=jnp.float32).astype(
        jnp.bfloat16
    )
    value_rows = jnp.dot(first_low, value_weight, preferred_element_type=jnp.float32).astype(
        jnp.bfloat16
    )
    query_four = to_heads(queries)
    key_four = to_heads(key_rows)
    value_four = to_heads(value_rows)
    scores = masked_scores(query_four, key_four)
    row_max = jnp.max(scores, axis=-1, keepdims=True)
    numerator = jnp.exp(scores - row_max)
    row_total = jnp.sum(numerator, axis=-1, keepdims=True)
    log_total = row_max + jnp.log(row_total)
    probs_low = (numerator / row_total).astype(jnp.bfloat16)
    heads_out = jnp.einsum(
        "shqk,skhd->sqhd", probs_low, value_four, preferred_element_type=jnp.float32
    )
    heads_low = heads_out.astype(jnp.bfloat16).reshape(tok_rows, heads_here * DH)
    attn_part = jnp.dot(heads_low, output_weight, preferred_element_type=jnp.float32)
    bias_attn = output_bias.astype(jnp.float32)
    bias_down = down_bias.astype(jnp.float32)
    grad_output = cotangent.astype(jnp.float32)
    attn_share = lax.psum_scatter(attn_part, "tensor", scatter_dimension=0, tiled=True)
    residual_share = share_rows(inputs) + attn_share + bias_attn
    second_share, second_scaled, second_inverse = norm_parts(
        residual_share, gain_two, second_shift.astype(jnp.float32)
    )
    second_low = lax.all_gather(second_share.astype(jnp.bfloat16), "tensor", axis=0, tiled=True)
    up_pre = jnp.dot(second_low, up_weight, preferred_element_type=jnp.float32) + up_bias.astype(
        jnp.float32
    )
    activated, gelu_pull = jax.vjp(gelu_exact, up_pre)
    activated = activated.astype(jnp.bfloat16)
    down_part = jnp.dot(activated, down_weight, preferred_element_type=jnp.float32)
    down_share = lax.psum_scatter(
        down_part.astype(jnp.bfloat16), "tensor", scatter_dimension=0, tiled=True
    ).astype(jnp.float32)
    out_share = (residual_share + down_share + bias_down).astype(jnp.bfloat16)
    block_out = lax.all_gather(out_share, "tensor", axis=0, tiled=True)
    down_bias_part = jnp.sum(share_rows(grad_output), axis=0)
    down_grad = jnp.einsum("tf,td->fd", activated, cotangent, preferred_element_type=jnp.float32)
    activated_grad = jnp.einsum(
        "td,fd->tf", cotangent, down_weight, preferred_element_type=jnp.float32
    )
    up_grad_pre = gelu_pull(activated_grad)[0].astype(jnp.bfloat16)
    up_bias_grad = jnp.sum(up_grad_pre.astype(jnp.float32), axis=0)
    up_grad = jnp.einsum("td,tf->df", second_low, up_grad_pre, preferred_element_type=jnp.float32)
    second_part = jnp.einsum(
        "tf,df->td", up_grad_pre, up_weight, preferred_element_type=jnp.float32
    )
    second_grad_share = lax.psum_scatter(second_part, "tensor", scatter_dimension=0, tiled=True)
    residual_share_grad = share_rows(grad_output) + norm_back(
        second_grad_share, second_scaled, second_inverse, gain_two
    )
    second_gain_part = jnp.sum(second_grad_share * second_scaled, axis=0)
    second_shift_part = jnp.sum(second_grad_share, axis=0)
    output_bias_part = jnp.sum(residual_share_grad, axis=0)
    residual_low = lax.all_gather(
        residual_share_grad.astype(jnp.bfloat16), "tensor", axis=0, tiled=True
    )
    output_grad = jnp.einsum(
        "tc,td->cd", heads_low, residual_low, preferred_element_type=jnp.float32
    )
    heads_grad = jnp.einsum(
        "td,cd->tc", residual_low, output_weight, preferred_element_type=jnp.float32
    )
    heads_grad_four = to_heads(heads_grad.astype(jnp.bfloat16))
    probs_again = jnp.exp(masked_scores(query_four, key_four) - log_total)
    value_rows_grad = jnp.einsum(
        "shqk,sqhd->skhd", probs_low, heads_grad_four, preferred_element_type=jnp.float32
    ).astype(jnp.bfloat16)
    probs_grad = jnp.einsum(
        "sqhd,skhd->shqk", heads_grad_four, value_four, preferred_element_type=jnp.float32
    )
    inner_sum = jnp.sum(probs_again * probs_grad, axis=-1, keepdims=True)
    scores_grad = (probs_again * (probs_grad - inner_sum)).astype(jnp.bfloat16)
    queries_grad = (
        (
            jnp.einsum("shqk,skhd->sqhd", scores_grad, key_four, preferred_element_type=jnp.float32)
            * scale_factor
        )
        .astype(jnp.bfloat16)
        .reshape(tok_rows, heads_here * DH)
    )
    key_rows_grad = (
        (
            jnp.einsum(
                "shqk,sqhd->skhd", scores_grad, query_four, preferred_element_type=jnp.float32
            )
            * scale_factor
        )
        .astype(jnp.bfloat16)
        .reshape(tok_rows, heads_here * DH)
    )
    value_rows_grad = value_rows_grad.reshape(tok_rows, heads_here * DH)
    query_grad = jnp.einsum(
        "td,tc->dc", first_low, queries_grad, preferred_element_type=jnp.float32
    )
    key_grad = jnp.einsum("td,tc->dc", first_low, key_rows_grad, preferred_element_type=jnp.float32)
    value_grad = jnp.einsum(
        "td,tc->dc", first_low, value_rows_grad, preferred_element_type=jnp.float32
    )
    first_part = (
        jnp.einsum("tc,dc->td", queries_grad, query_weight, preferred_element_type=jnp.float32)
        + jnp.einsum("tc,dc->td", key_rows_grad, key_weight, preferred_element_type=jnp.float32)
        + jnp.einsum("tc,dc->td", value_rows_grad, value_weight, preferred_element_type=jnp.float32)
    )
    first_grad_share = lax.psum_scatter(
        first_part.astype(jnp.bfloat16), "tensor", scatter_dimension=0, tiled=True
    ).astype(jnp.float32)
    scaled_share = share_rows(first_scaled)
    token_share = residual_share_grad + norm_back(
        first_grad_share, scaled_share, share_rows(first_inverse), gain_one
    )
    token_grad = lax.all_gather(token_share.astype(jnp.bfloat16), "tensor", axis=0, tiled=True)
    first_gain_part = jnp.sum(first_grad_share * scaled_share, axis=0)
    first_shift_part = jnp.sum(first_grad_share, axis=0)
    query_grad, key_grad, value_grad, output_grad, up_grad, up_bias_grad, down_grad = (
        lax.psum(query_grad.astype(jnp.bfloat16), "dp").astype(jnp.float32),
        lax.psum(key_grad.astype(jnp.bfloat16), "dp").astype(jnp.float32),
        lax.psum(value_grad.astype(jnp.bfloat16), "dp").astype(jnp.float32),
        lax.psum(output_grad.astype(jnp.bfloat16), "dp").astype(jnp.float32),
        lax.psum(up_grad.astype(jnp.bfloat16), "dp").astype(jnp.float32),
        lax.psum(up_bias_grad.astype(jnp.bfloat16), "dp").astype(jnp.float32),
        lax.psum(down_grad.astype(jnp.bfloat16), "dp").astype(jnp.float32),
    )
    (
        first_gain_grad,
        first_shift_grad,
        second_gain_grad,
        second_shift_grad,
        output_bias_grad,
        down_bias_grad,
    ) = lax.psum(
        (
            first_gain_part,
            first_shift_part,
            second_gain_part,
            second_shift_part,
            output_bias_part,
            down_bias_part,
        ),
        ("dp", "tensor"),
    )
    return (
        block_out,
        token_grad,
        query_grad,
        key_grad,
        value_grad,
        output_grad,
        up_grad,
        up_bias_grad,
        down_grad,
        first_gain_grad,
        first_shift_grad,
        second_gain_grad,
        second_shift_grad,
        output_bias_grad,
        down_bias_grad,
    )


F32 = jnp.float32
BF16 = jnp.bfloat16
MESH = pl.DeviceIdType.MESH
N_LOCAL = 19

TASKS = "DUOQSTVWFGBAXYZHKPE"
PARTS = (
    ("D", 0, 64, "a"), ("D", 64, 64, "d"), ("D", 128, 64, "a"), ("D", 192, 64, "a"),
    ("D", 256, 64, "d"), ("D", 320, 64, "a"), ("D", 384, 64, "a"), ("D", 448, 64, "a"),
    ("U", 0, 128, "a"), ("U", 128, 128, "d"), ("U", 256, 128, "d"), ("U", 384, 128, "a"),
    ("U", 512, 128, "a"), ("U", 640, 128, "a"), ("U", 768, 128, "b"), ("U", 896, 128, "a"),
    ("O", 0, 64, "a"), ("O", 64, 64, "b"), ("O", 128, 64, "a"), ("O", 192, 64, "d"),
    ("Q", 0, 64, "d"), ("Q", 64, 64, "a"), ("Q", 128, 64, "a"), ("Q", 192, 64, "a"),
    ("Q", 256, 64, "a"), ("Q", 320, 64, "a"), ("Q", 384, 64, "a"), ("Q", 448, 64, "d"),
    ("Q", 512, 64, "a"), ("Q", 576, 64, "a"), ("Q", 640, 64, "d"), ("Q", 704, 64, "d"),
    ("Q", 768, 64, "a"), ("Q", 832, 64, "a"), ("Q", 896, 64, "a"), ("Q", 960, 64, "d"),
)
ORDER = (
    1150, 1151, 1160, 1161, 1162, 1163, 1170, 1180, 1171, 1181, 1040, 1182, 1183, 1011, 1001, 1050,
    1041, 1061, 101, 1000, 1060, 41, 1010, 1051, 11, 102, 1013, 91, 42, 12, 141, 111, 92, 51, 61,
    112, 1012, 1, 103, 52, 142, 71, 62, 113, 21, 81, 93, 31, 2, 53, 72, 63, 22, 143, 1100, 43, 131,
    82, 73, 13, 151, 3, 1110, 54, 1070, 44, 32, 132, 23, 104, 144, 114, 94, 1111, 152, 74, 83,
    1101, 121, 33, 45, 64, 1112, 4, 133, 105, 1080, 24, 14, 95, 153, 1113, 1031, 122, 1033, 106,
    15, 46, 1090, 271, 351, 96, 1032, 301, 1030, 16, 1081, 201, 272, 1020, 123, 311, 352, 171, 202,
    241, 321, 191, 251, 302, 312, 1091, 242, 281, 322, 341, 172, 353, 192, 252, 282, 243, 342, 323,
    261, 211, 221, 291, 262, 273, 253, 84, 1130, 212, 283, 343, 222, 303, 203, 231, 263, 292, 1120,
    213, 331, 232, 274, 313, 193, 324, 223, 173, 1071, 293, 204, 332, 244, 233, 161, 154, 205, 162,
    194, 284, 314, 174, 1131, 1140, 333, 275, 195, 224, 181, 34, 163, 182, 315, 1141, 294, 196,
    214, 234, 124, 355, 183, 344, 354, 316, 304, 334, 264, 206, 305, 164, 1142, 1121, 356, 184,
    306, 134, 276, 254,
)

N_ROWS = {name: sum(p[2] for p in PARTS if p[0] == name) for name in "DUOQ"}
N_SENDS = len({(p[0], p[3], p[1] * 3 // N_ROWS[p[0]]) for p in PARTS}) + 11
N_RECVS = 3 * len(PARTS) + 38


def dot(a, b):
    return jnp.dot(a, b, preferred_element_type=F32)


def dot_nt(a, b):
    return lax.dot_general(a, b, (((1,), (1,)), ((), ())), preferred_element_type=F32)


def dot_tn(a, b):
    return lax.dot_general(a, b, (((0,), (0,)), ((), ())), preferred_element_type=F32)


def span(start, size):
    return pl.ds(pl.multiple_of(start, 16), size)


def lanes(start, size):
    return pl.ds(pl.multiple_of(start, 128), size)


class Links:
    def __init__(self, sends, recvs, anyone):
        self.sends, self.recvs, self.anyone = sends, recvs, anyone
        self.used = [0, 0]

    def group(self):
        self.used[0] += 1
        assert self.used[0] <= N_SENDS
        return self.used[0] - 1

    def take(self, count=1):
        first = self.used[1]
        self.used[1] += count
        assert self.used[1] <= N_RECVS
        return first

    def copy(self, src, dst, group, index, device):
        return pltpu.make_async_remote_copy(
            src_ref=src,
            dst_ref=dst,
            send_sem=self.sends.at[group],
            recv_sem=self.recvs.at[index],
            device_id=device,
            device_id_type=MESH,
        )

    def got(self, dst, index):
        self.copy(dst, dst, 0, index, self.anyone).wait_recv()

    def sent(self, like, group):
        self.copy(like, like, group, 0, self.anyone).wait_send()


def layer_kernel(
    count,
    tokens_hbm,
    lengths_hbm,
    query_hbm,
    key_hbm,
    value_hbm,
    output_hbm,
    up_hbm,
    up_bias_hbm,
    down_hbm,
    first_gain_hbm,
    first_shift_hbm,
    second_gain_hbm,
    second_shift_hbm,
    output_bias_hbm,
    down_bias_hbm,
    cotangent_hbm,
    block_out,
    token_grad,
    down_out,
    up_out,
    output_out,
    qkv_out,
    vec_out,
    lengths,
    up_bias,
    first_gain,
    first_shift,
    second_gain,
    second_shift,
    output_bias,
    down_bias,
    tokens,
    cotangent,
    query_weight,
    key_weight,
    value_weight,
    wo_all,
    up_weight,
    down_weight,
    first_low,
    queries,
    key_rows,
    value_rows,
    probs,
    heads_own,
    heads_full,
    residual,
    second_low,
    act,
    ugp,
    mail,
    residual_grad,
    residual_low,
    dqkv,
    g_down,
    g_up,
    g_output,
    g_qkv,
    rx_down,
    rx_up,
    rx_output,
    rx_qkv,
    rz_down,
    rz_up,
    rz_output,
    rz_qkv,
    rm_down,
    rm_up,
    rm_output,
    rm_qkv,
    vec,
    vec_sib,
    vec_parts,
    vec_sum,
    sends,
    recvs,
    local_sems,
):
    n_rows, width = tokens.shape
    half = n_rows // 2
    tile = 16 * count
    n_tiles = n_rows // tile
    half_tiles = n_tiles // 2
    heads_here = query_weight.shape[1] // DH
    cols = heads_here * DH
    hidden = up_weight.shape[1]
    scale_factor = 1.0 / math.sqrt(DH)

    dp = lax.axis_index("dp")
    t = lax.axis_index("tensor")
    x = dp % 2
    z = dp // 2
    c = t % 2
    t_sib = t + 1 - 2 * c
    t_opp = (t + 2) % 4
    t_diag = (t_sib + 2) % 4
    sib = (dp, t_sib)
    opp = (dp, t_opp)
    diag = (dp, t_diag)
    xp = (dp + 1 - 2 * x, t)
    adj = (dp + 2 - 4 * (z % 2), t)
    cross = (dp + 2 - 4 * (z % 2) + 1 - 2 * x, t)
    mid = ((3 - z) * 2 + x, t)
    is_mid = jnp.logical_or(z == 1, z == 2)
    is_end = jnp.logical_or(z == 0, z == 3)
    side = z // 2
    dp_peers = [((dp + k) % 8, t) for k in range(1, 8)]
    links = Links(sends, recvs, sib)

    barrier = pltpu.get_barrier_semaphore()
    peers = [sib, opp, diag, (adj[0], t_sib), (xp[0], t_sib)] + dp_peers
    for peer in peers:
        pl.semaphore_signal(barrier, inc=1, device_id=peer, device_id_type=MESH)

    other_rows = span((1 - c) * half, half)
    own_start = c * half
    sib_start = (1 - c) * half
    own_wo = span(t * cols, cols)

    def turn_rows(i):
        return span((i % 2) * half + (i // 2) * tile, tile)

    def token_load(i):
        rows = turn_rows(i)
        return pltpu.make_async_copy(tokens_hbm.at[rows, :], tokens.at[rows, :], local_sems.at[i])

    loads = [
        pltpu.make_async_copy(src, dst, local_sems.at[n_tiles + n])
        for n, (src, dst) in enumerate(
            (
                (query_hbm, query_weight),
                (key_hbm, key_weight),
                (value_hbm, value_weight),
                (lengths_hbm, lengths),
                (first_gain_hbm, first_gain),
                (first_shift_hbm, first_shift),
                (output_hbm, wo_all.at[own_wo, :]),
                (output_bias_hbm, output_bias),
                (second_gain_hbm, second_gain),
                (second_shift_hbm, second_shift),
                (up_bias_hbm, up_bias),
                (down_bias_hbm, down_bias),
                (up_hbm, up_weight),
                (down_hbm, down_weight),
                (cotangent_hbm, cotangent),
            )
        )
    ]
    token_load(0).start()
    early = 6
    for load in loads[:early]:
        load.start()
    for i in range(1, n_tiles):
        token_load(i).start()
    for load in loads[early:]:
        load.start()

    def row(ref):
        return ref[...].astype(F32).reshape(1, ref.shape[0])

    def norm_parts(v):
        e = v - jnp.mean(v, axis=-1, keepdims=True)
        r = lax.rsqrt(jnp.mean(e * e, axis=-1, keepdims=True) + EPS)
        return e * r, r

    piece = cols // 4
    quarter = x + 2 * (z % 2)

    def wo_piece(owner, number):
        return wo_all.at[span(owner * cols + number * piece, piece), :]

    i_wo = links.take(7)
    s_wo = links.group()
    by_y = links.copy(
        output_hbm.at[span(quarter * piece, piece), :], wo_piece(t, quarter), s_wo, i_wo, opp
    )
    whole_to_sib = links.copy(output_hbm, wo_all.at[own_wo, :], s_wo, i_wo + 1, sib)
    q_xp, q_adj = quarter + 1 - 2 * x, quarter + 2 - 4 * (z % 2)
    q_cross = q_adj + 1 - 2 * x
    mine = wo_piece(t_opp, quarter)
    to_x = links.copy(mine, mine, s_wo, i_wo + 2, xp)
    to_z = links.copy(mine, mine, s_wo, i_wo + 3, adj)

    def half_piece(number, which):
        return wo_all.at[span(t_opp * cols + number * piece + which * piece // 2, piece // 2), :]

    from_x, from_z = half_piece(q_xp, 0), half_piece(q_adj, 1)
    on_z = [links.copy(from_x, from_x, s_wo, i_wo + 4, (adj[0], v)) for v in (t, t_sib)]
    on_x = [links.copy(from_z, from_z, s_wo, i_wo + 5, (xp[0], v)) for v in (t, t_sib)]

    def relay(number):
        part = wo_piece(t_opp, number)
        links.copy(part, part, s_wo, i_wo + 6, sib).start()

    def share_first():
        links.got(mine, i_wo)
        to_x.start()
        to_z.start()
        relay(quarter)

    def share_next():
        links.got(wo_piece(t_opp, q_xp), i_wo + 2)
        for each in on_z:
            each.start()
        links.got(wo_piece(t_opp, q_adj), i_wo + 3)
        for each in on_x:
            each.start()
        relay(q_xp)
        relay(q_adj)

    def share_last():
        links.got(wo_piece(t_opp, q_cross), i_wo + 4)
        links.got(wo_piece(t_diag, q_cross), i_wo + 5)
        links.got(wo_all.at[span(t_diag * cols, 3 * piece), :], i_wo + 6)

    pl.semaphore_wait(barrier, len(peers))
    by_y.start()
    whole_to_sib.start()

    def allowed_of(number):
        def series_of(index):
            return jnp.floor((index + 0.5) * (1.0 / count))

        row_at = lax.broadcasted_iota(jnp.int32, (tile, 1), 0).astype(F32)
        col_at = lax.broadcasted_iota(jnp.int32, (1, tile), 1).astype(F32)
        row_series, col_series = series_of(row_at), series_of(col_at)
        n_series = lengths.shape[0]
        which = lax.broadcasted_iota(jnp.int32, (n_series, tile), 0).astype(F32)
        here = (which == col_series + (number * 16).astype(F32)).astype(BF16)
        all_lengths = jnp.broadcast_to(
            lengths[...].astype(F32).reshape(1, n_series), (8, n_series)
        ).astype(BF16)
        length = dot(all_lengths, here)[0:1, :]
        live = (col_at - count * col_series) >= (count - length)
        same = row_series == col_series
        seen = jnp.logical_and(live, col_at <= row_at)
        return jnp.logical_and(same, jnp.logical_or(seen, col_at == row_at))

    i_heads = links.take(2 * half_tiles + 1)
    i_near = i_heads + half_tiles + 1
    s_heads = links.group()

    def head_slot(j):
        return span(j * tile, tile)

    cut = tile // 32 * 16 + 16
    pieces = [[(0, tile)]] * (half_tiles - 1) + [[(0, cut), (cut, tile - cut)]]

    def attend(i, _):
        h, j = i % 2, i // 2
        number = h * half_tiles + j
        rows = turn_rows(i)
        token_load(i).wait()

        @pl.when(i == 0)
        def _():
            for load in loads[:early]:
                load.wait()

        xhat, _r = norm_parts(tokens[rows, :].astype(F32))
        first_low[rows, :] = (xhat * row(first_gain) + row(first_shift)).astype(BF16)

        normed = first_low[rows, :]
        q = dot(normed, query_weight[...]).astype(BF16)
        k = dot(normed, key_weight[...]).astype(BF16)
        v = dot(normed, value_weight[...]).astype(BF16)
        queries[rows, :] = q
        key_rows[rows, :] = k
        value_rows[rows, :] = v

        allowed = allowed_of(number)
        for head in range(heads_here):
            at = slice(head * DH, (head + 1) * DH)
            scores = jnp.where(allowed, dot_nt(q[:, at], k[:, at]) * scale_factor, -1e30)
            numerator = jnp.exp(scores - jnp.max(scores, axis=-1, keepdims=True))
            share = numerator / jnp.sum(numerator, axis=-1, keepdims=True)
            probs[number * heads_here + head] = share
            heads_own[rows, at] = dot(share.astype(BF16), v[:, at]).astype(BF16)
        mine = lanes(t * cols, cols)
        slot = heads_full.at[head_slot(j), mine]

        def over_y(device):
            @pl.when(j < half_tiles - 1)
            def _():
                links.copy(heads_own.at[rows, :], slot, s_heads, i_heads + j, device).start()

            @pl.when(j == half_tiles - 1)
            def _():
                for n, (start, size) in enumerate(pieces[-1]):
                    links.copy(
                        heads_own.at[span(h * half + j * tile + start, size), :],
                        heads_full.at[span(j * tile + start, size), mine],
                        s_heads,
                        i_heads + j + n,
                        device,
                    ).start()

        @pl.when(h == c)
        def _():
            heads_full[head_slot(j), mine] = heads_own[rows, :]
            over_y(opp)

        @pl.when(h != c)
        def _():
            links.copy(heads_own.at[rows, :], slot, s_heads, i_near + j, sib).start()
            over_y(diag)

        @pl.when(i == 1)
        def _():
            share_first()

        return 0

    lax.fori_loop(0, n_tiles, attend, 0)

    share_next()

    i_second = links.take(half_tiles + 1)
    s_second = links.group()
    vec[...] = jnp.zeros_like(vec)

    def in_turn(i):
        return jnp.where(i % 2 == 0, own_start, sib_start) + (i // 2) * tile

    chip = 2 * cols
    own_k, other_k = lanes((t // 2) * chip, chip), lanes((1 - t // 2) * chip, chip)

    def prepare(j):
        here = head_slot(j)
        if j == 0:
            for load in loads[early:]:
                load.wait()
            links.got(wo_all.at[span(t_sib * cols, cols), :], i_wo + 1)
        links.got(heads_full.at[here, lanes(t_sib * cols, cols)], i_near + j)
        residual[here, :] = dot(heads_full[here, own_k], wo_all[span((t // 2) * chip, chip), :])

    def down_slot(i):
        return residual_grad.at[head_slot(i // 2), (i % 2) * hidden : (i % 2 + 1) * hidden]

    def prepare_feed(i):
        down_slot(i)[...] = dot_nt(cotangent[span(in_turn(i), tile), :], down_weight[...])

    def feed(i):
        here = pieces[i // 2] if i % 2 == 1 else [(0, tile)]
        for n, (start, size) in enumerate(here):
            rows = span(in_turn(i) + start, size)
            if i % 2 == 1:
                links.got(second_low.at[rows, :], i_second + i // 2 + n)
            u = dot(second_low[rows, :], up_weight[...]) + row(up_bias)
            big = 0.5 * (1.0 + lax.erf(u * (1.0 / math.sqrt(2.0))))
            act[rows, :] = (u * big).astype(BF16)
            slope = big + u * (jnp.exp(-0.5 * u * u) * (1.0 / math.sqrt(2.0 * math.pi)))
            grad = (down_slot(i)[start : start + size, :] * slope).astype(BF16)
            ugp[rows, :] = grad
            vec[6:7, 0:hidden] += jnp.sum(grad.astype(F32), axis=0, keepdims=True)

    def project(j):
        if j == 0:
            share_last()
        for n, (start, size) in enumerate(pieces[j]):
            here = span(j * tile + start, size)
            links.got(heads_full.at[here, other_k], i_heads + j + n)
            rows = span(own_start + j * tile + start, size)
            other = dot(heads_full[here, other_k], wo_all[span((1 - t // 2) * chip, chip), :])
            v = tokens[rows, :].astype(F32) + (residual[here, :] + other) + row(output_bias)
            residual[here, :] = v
            xhat, _r = norm_parts(v)
            second_low[rows, :] = (xhat * row(second_gain) + row(second_shift)).astype(BF16)
            links.copy(
                second_low.at[rows, :], second_low.at[rows, :], s_second, i_second + j + n, sib
            ).start()

    class Tensor:
        def __init__(self, grads, rx, rz, rm, out, long):
            self.grads, self.rx, self.rz, self.rm, self.out = grads, rx, rz, rm, out
            self.long = long
            self.final = links.take()
            self.groups = {}

        def group_of(self, kind, start):
            key = kind, start * 3 // self.grads.shape[0]
            if key not in self.groups:
                self.groups[key] = links.group()
            return self.groups[key]

        def end(self, name):
            mine = [p for p in PARTS if p[0] == name]
            halves = {kind: sum(p[2] // 2 for p in mine if p[3] == kind) for kind in "abcdh"}
            for here, copies, came in (
                (is_mid, {"a": 4, "b": 5, "c": 4, "d": 4, "h": 4}, {"a": 1, "b": 0, "c": 1, "d": 0, "h": 1}),
                (is_end, {"a": 3, "b": 2, "c": 3, "d": 3, "h": 3}, {"a": 1, "b": 2, "c": 1, "d": 1, "h": 1}),
            ):

                @pl.when(here)
                def _(copies=copies, came=came):
                    rows = sum(came[kind] * halves[kind] for kind in "abcdh")
                    assert rows <= self.long.shape[0]
                    if rows > 0:
                        links.got(self.long.at[0:rows, :], self.final)
                    for (kind, which), group in self.groups.items():
                        rows = sum(
                            copies[kind] * p[2] // 2
                            for p in mine
                            if p[3] == kind and p[1] * 3 // self.grads.shape[0] == which
                        )
                        assert rows <= self.long.shape[0]
                        links.sent(self.long.at[0:rows, :], group)

    tensors = {
        "D": Tensor(g_down, rx_down, rz_down, rm_down, down_out, wo_all),
        "U": Tensor(g_up, rx_up, rz_up, rm_up, up_out, up_weight),
        "O": Tensor(g_output, rx_output, rz_output, rm_output, output_out, wo_all),
        "Q": Tensor(g_qkv, rx_qkv, rz_qkv, rm_qkv, qkv_out, dqkv),
    }

    class Part:
        def __init__(self, tensor, start, size, kind):
            self.size = size // 2
            self.start = start
            here = pl.ds(start // 2, self.size)
            self.grads, self.out = tensor.grads, tensor.out
            self.rx, self.rm = tensor.rx.at[here, :], tensor.rm.at[here, :]
            self.rz = tensor.rz.at[pl.ds(start, self.size), :]
            self.rz_whole = tensor.rz.at[pl.ds(start, size), :]
            self.index = links.take(3)
            self.final = tensor.final
            self.group = tensor.group_of(kind, start)

        def half_at(self, which):
            return span(self.start + which * self.size, self.size)

        def send(self, src, dst, message, device):
            links.copy(src, dst, self.group, self.index + message, device).start()

        def send_last(self, ref, device):
            links.copy(ref, ref, self.group, self.final, device).start()

        def got(self, dst, message):
            links.got(dst, self.index + message)

        def add(self, rows, came):
            return (self.grads[rows, :].astype(F32) + came[...].astype(F32)).astype(BF16)

    class PartX(Part):
        def begin(self):
            self.send(self.grads.at[self.half_at(1 - x), :], self.rx, 0, xp)

        def step(self, number):
            mine = self.half_at(x)
            grads, out = self.grads.at[mine, :], self.out.at[mine, :]
            if number == 1:
                self.got(self.rx, 0)
                self.grads[mine, :] = self.add(mine, self.rx)

                @pl.when(is_end)
                def _():
                    self.send(grads, self.rz, 1, adj)

            if number == 2:

                @pl.when(is_mid)
                def _():
                    self.got(self.rz, 1)
                    self.grads[mine, :] = self.add(mine, self.rz)
                    self.send(grads, self.rm, 2, mid)

            if number == 3:

                @pl.when(is_mid)
                def _():
                    self.got(self.rm, 2)
                    self.out[mine, :] = self.add(mine, self.rm)
                    self.send(out, out, 1, adj)
                    self.send_last(out, xp)

            if number == 4:

                @pl.when(is_end)
                def _():
                    self.got(out, 1)
                    self.send_last(out, xp)

    class PartE(Part):
        def begin(self):
            self.send(self.grads.at[self.half_at(1 - x), :], self.rx, 0, xp)

        def step(self, number):
            size = self.size // 2
            mine = self.half_at(x)
            near = span(self.start + x * self.size + side * size, size)
            far = span(self.start + x * self.size + (1 - side) * size, size)
            near_out, far_out = self.out.at[near, :], self.out.at[far, :]
            rz, rm = self.rz.at[0:size, :], self.rm.at[0:size, :]
            if number == 1:
                self.got(self.rx, 0)
                self.grads[mine, :] = self.add(mine, self.rx)

            @pl.when(is_end if number in (1, 4, 7) else is_mid)
            def _():
                if number == 1:
                    self.send(self.grads.at[far, :], rz, 1, adj)
                if number == 2:
                    self.got(rz, 1)
                    self.grads[far, :] = self.add(far, rz)
                    self.send(self.grads.at[far, :], rm, 2, mid)
                if number == 3:
                    self.got(rm, 2)
                    self.grads[near, :] = self.add(near, rm)
                    self.send(self.grads.at[near, :], rz, 1, adj)
                if number == 4:
                    self.got(rz, 1)
                    self.out[near, :] = self.add(near, rz)
                    self.send(near_out, near_out, 0, adj)
                    self.send_last(near_out, xp)
                if number == 5:
                    self.got(near_out, 0)
                    self.send(near_out, near_out, 1, mid)
                    self.send_last(near_out, xp)
                if number == 6:
                    self.got(far_out, 1)
                    self.send(far_out, far_out, 0, adj)
                    self.send_last(far_out, xp)
                if number == 7:
                    self.got(far_out, 0)
                    self.send_last(far_out, xp)

    class PartH(Part):
        def begin(self):
            @pl.when(is_end)
            def _():
                whole = self.grads.at[pl.ds(self.start, 2 * self.size), :]
                self.send(whole, self.rz_whole, 0, adj)

        def step(self, number):
            size = self.size // 2
            near, far = self.half_at(side), self.half_at(1 - side)
            near_at = self.start + side * self.size
            far_at = self.start + (1 - side) * self.size
            near_mine = span(near_at + x * size, size)
            near_other = span(near_at + (1 - x) * size, size)
            far_mine = span(far_at + x * size, size)
            near_out, far_out = self.out.at[near_mine, :], self.out.at[far_mine, :]
            rx = self.rx.at[0:size, :]

            @pl.when(is_end if number > 4 else is_mid)
            def _():
                if number == 1:
                    whole = pl.ds(self.start, 2 * self.size)
                    self.got(self.rz_whole, 0)
                    self.grads[whole, :] = self.add(whole, self.rz_whole)
                    self.send(self.grads.at[far, :], self.rm, 1, mid)
                if number == 2:
                    self.got(self.rm, 1)
                    self.grads[near, :] = self.add(near, self.rm)
                    self.send(self.grads.at[near_other, :], rx, 2, xp)
                if number == 3:
                    self.got(rx, 2)
                    self.out[near_mine, :] = self.add(near_mine, rx)
                    self.send(near_out, near_out, 0, adj)
                    self.send(near_out, near_out, 0, mid)
                    self.send_last(near_out, xp)
                if number == 4:
                    self.got(far_out, 0)
                    self.send(far_out, far_out, 1, adj)
                    self.send_last(far_out, xp)
                if number == 5:
                    self.got(near_out, 0)
                    self.send_last(near_out, xp)
                if number == 6:
                    self.got(far_out, 1)
                    self.send_last(far_out, xp)

    class PartZ(Part):
        def begin(self):
            far = self.grads.at[self.half_at(1 - side), :]

            @pl.when(is_end)
            def _():
                self.send(far, self.rz, 0, adj)

        def step(self, number):
            near, far = self.half_at(side), self.half_at(1 - side)
            near_out, far_out = self.out.at[near, :], self.out.at[far, :]

            @pl.when(is_end if number in (3, 4) else is_mid)
            def _():
                if number == 1:
                    self.got(self.rz, 0)
                    self.grads[far, :] = self.add(far, self.rz)
                    self.send(self.grads.at[far, :], self.rm, 1, mid)
                if number == 2:
                    self.got(self.rm, 1)
                    self.grads[near, :] = self.add(near, self.rm)
                    self.send(self.grads.at[near, :], self.rz, 0, adj)
                if number == 3:
                    self.got(self.rz, 0)
                    self.grads[near, :] = self.add(near, self.rz)
                    self.send(self.grads.at[near, :], self.rx, 1, xp)
                if number == 4:
                    self.got(self.rx, 1)
                    self.out[near, :] = self.add(near, self.rx)
                    self.send(near_out, near_out, 0, adj)
                if number == 5:
                    self.got(near_out, 0)
                    self.send(near_out, near_out, 2, mid)
                if number == 6:
                    self.got(far_out, 2)
                    self.send_last(far_out, adj)

    class PartM(Part):
        def begin(self):
            @pl.when(is_end)
            def _():
                whole = self.grads.at[pl.ds(self.start, 2 * self.size), :]
                self.send(whole, self.rz_whole, 0, adj)

        def step(self, number):
            near, far = self.half_at(side), self.half_at(1 - side)
            near_out, far_out = self.out.at[near, :], self.out.at[far, :]

            @pl.when(is_mid)
            def _():
                if number == 1:
                    whole = pl.ds(self.start, 2 * self.size)
                    self.got(self.rz_whole, 0)
                    self.grads[whole, :] = self.add(whole, self.rz_whole)
                    self.send(self.grads.at[far, :], self.rm, 1, mid)
                if number == 2:
                    self.got(self.rm, 1)
                    self.grads[near, :] = self.add(near, self.rm)
                    self.send(self.grads.at[near, :], self.rx, 2, xp)
                if number == 3:
                    self.got(self.rx, 2)
                    self.out[near, :] = self.add(near, self.rx)
                    self.send_last(near_out, adj)
                    self.send(near_out, near_out, 0, mid)
                if number == 4:
                    self.got(far_out, 0)
                    self.send_last(far_out, adj)

    parts = [
        {"a": PartX, "b": PartM, "c": PartE, "d": PartZ, "h": PartH}[kind](tensors[name], start, size, kind)
        for name, start, size, kind in PARTS
    ]

    def begin_parts(name, first, size):
        for (which, start, rows, _kind), part in zip(PARTS, parts, strict=True):
            if which == name and first < start + rows <= first + size:
                part.begin()

    block = 256

    def down_grads(i):
        at = slice(i * block, (i + 1) * block)
        g_down[at, :] = dot_tn(act[:, at], cotangent[...]).astype(BF16)
        begin_parts("D", i * block, block)

    def up_grads(i):
        at = slice(i * block, (i + 1) * block)
        g_up[at, :] = dot_tn(second_low[:, at], ugp[...]).astype(BF16)
        begin_parts("U", i * block, block)

    def output_grads(_i):
        g_output[...] = dot_tn(heads_own[...], residual_low[...]).astype(BF16)
        begin_parts("O", 0, cols)

    def qkv_grads(i):
        at = slice(i * block, (i + 1) * block)
        g_qkv[at, :] = dot_tn(first_low[:, at], dqkv[...]).astype(BF16)
        begin_parts("Q", i * block, block)

    class RowSum:
        def __init__(self, number, part, snd):
            self.snd = snd
            self.r1, self.cs, self.r2 = (mail.at[3 * number + n] for n in range(3))
            self.part = part
            self.index = links.take(2 * half_tiles)
            self.group = links.group()

        def far(self, j):
            here = head_slot(j)
            self.snd[here, :] = self.part(span(sib_start + j * tile, tile)).astype(BF16)
            links.copy(
                self.snd.at[here, :], self.r1.at[here, :], self.group, self.index + j, sib
            ).start()

        def near(self, j):
            here = head_slot(j)
            mine = self.part(span(own_start + j * tile, tile))
            links.got(self.r1.at[here, :], self.index + j)
            self.cs[here, :] = (mine + self.r1[here, :].astype(F32)).astype(BF16)
            links.copy(
                self.cs.at[here, :],
                self.r2.at[here, :],
                self.group,
                self.index + half_tiles + j,
                opp,
            ).start()

        def rows(self, j):
            here = head_slot(j)
            links.got(self.r2.at[here, :], self.index + half_tiles + j)
            return self.cs[here, :].astype(F32) + self.r2[here, :].astype(F32)

        def end(self):
            links.sent(first_low, self.group)

    second_sum = RowSum(0, lambda rows: dot_nt(ugp[rows, :], up_weight[...]), mail.at[9])
    out_sum = RowSum(1, lambda rows: dot(act[rows, :], down_weight[...]), mail.at[10])
    first_sum = RowSum(
        2,
        lambda rows: dot_nt(dqkv[rows, 0:cols], query_weight[...])
        + dot_nt(dqkv[rows, cols : 2 * cols], key_weight[...])
        + dot_nt(dqkv[rows, 2 * cols : 3 * cols], value_weight[...]),
        heads_full,
    )
    row_sums = (second_sum, out_sum, first_sum)

    i_back = links.take(half_tiles)
    s_back = links.group()

    def add_to(at, value):
        vec[at : at + 1, :] += jnp.sum(value, axis=0, keepdims=True)

    def norm_back(incoming, xhat, r, gain):
        weighted = incoming * gain
        return r * (
            weighted
            - jnp.mean(weighted, axis=-1, keepdims=True)
            - xhat * jnp.mean(weighted * xhat, axis=-1, keepdims=True)
        )

    def second_back(j):
        local = head_slot(j)
        rows = span(own_start + j * tile, tile)
        incoming = second_sum.rows(j)
        xhat, r = norm_parts(residual[local, :])
        given = cotangent[rows, :].astype(F32)
        grad = given + norm_back(incoming, xhat, r, row(second_gain))
        residual_grad[local, :] = grad
        residual_low[rows, :] = grad.astype(BF16)
        links.copy(
            residual_low.at[rows, :], residual_low.at[rows, :], s_back, i_back + j, sib
        ).start()
        add_to(2, incoming * xhat)
        add_to(3, incoming)
        add_to(4, grad)
        add_to(5, given)

    def attend_back(i):
        start = in_turn(i)
        rows = span(start, tile)
        number = start // tile
        if i % 2 == 1:
            links.got(residual_low.at[rows, :], i_back + i // 2)
        grads = dot_nt(residual_low[rows, :], wo_all[own_wo, :]).astype(BF16)
        for head in range(heads_here):
            at = slice(head * DH, (head + 1) * DH)
            share = probs[number * heads_here + head]
            q, k, v = queries[rows, at], key_rows[rows, at], value_rows[rows, at]
            share_grad = dot_nt(grads[:, at], v)
            inner = jnp.sum(share * share_grad, axis=-1, keepdims=True)
            scores_grad = (share * (share_grad - inner)).astype(BF16)
            dqkv[rows, head * DH : (head + 1) * DH] = (
                dot(scores_grad, k) * scale_factor
            ).astype(BF16)
            dqkv[rows, cols + head * DH : cols + (head + 1) * DH] = (
                dot_tn(scores_grad, q) * scale_factor
            ).astype(BF16)
            dqkv[rows, 2 * cols + head * DH : 2 * cols + (head + 1) * DH] = dot_tn(
                share.astype(BF16), grads[:, at]
            ).astype(BF16)

    i_out = links.take(2)
    s_out = links.group()

    def finished(j, number, out, values):
        rows = span(own_start + j * tile, tile)
        out[rows, :] = values.astype(BF16)
        links.copy(out.at[rows, :], out.at[rows, :], s_out, i_out + number, sib).start()

    def finish_out(j):
        local = head_slot(j)
        finished(j, 0, block_out, residual[local, :] + out_sum.rows(j) + row(down_bias))

    def first_back(j):
        local = head_slot(j)
        rows = span(own_start + j * tile, tile)
        incoming = first_sum.rows(j)
        xhat, r = norm_parts(tokens[rows, :].astype(F32))
        grad = residual_grad[local, :] + norm_back(incoming, xhat, r, row(first_gain))
        finished(j, 1, token_grad, grad)
        add_to(0, incoming * xhat)
        add_to(1, incoming)

    i_vec = links.take(3)
    s_vec = [links.group() for _ in range(3)]
    part = width // 8
    mine_at = lanes(dp * part, part)
    seven = vec_parts.at[0:7]

    def vectors(number):
        if number == 0:
            links.copy(vec, vec_sib, s_vec[0], i_vec, sib).start()
        if number == 1:
            links.got(vec_sib, i_vec)
            links.sent(vec, s_vec[0])
            at_row = lax.broadcasted_iota(jnp.int32, vec.shape, 0)
            vec[...] = vec[...] + jnp.where(at_row < 6, vec_sib[...], 0.0)
            vec_parts[dp] = vec[:, mine_at]
            for peer in dp_peers:
                links.copy(
                    vec.at[:, lanes(peer[0] * part, part)],
                    vec_parts.at[dp],
                    s_vec[1],
                    i_vec + 1,
                    peer,
                ).start()
        if number == 2:
            links.got(seven, i_vec + 1)
            total = vec_parts[0]
            for k in range(1, 8):
                total = total + vec_parts[k]
            vec_sum[...] = total
            vec_out[:, mine_at] = total
            for peer in dp_peers:
                links.copy(vec_sum, vec_out.at[:, mine_at], s_vec[2], i_vec + 2, peer).start()
        if number == 3:
            links.got(seven, i_vec + 2)

    tasks = {
        "D": down_grads,
        "U": up_grads,
        "O": output_grads,
        "Q": qkv_grads,
        "S": second_sum.far,
        "T": second_sum.near,
        "V": out_sum.far,
        "W": out_sum.near,
        "F": first_sum.far,
        "G": first_sum.near,
        "B": second_back,
        "A": attend_back,
        "X": finish_out,
        "Y": first_back,
        "Z": vectors,
        "H": prepare,
        "K": prepare_feed,
        "P": project,
        "E": feed,
    }
    for code in ORDER:
        if code < 1000:
            parts[code // 10].step(code % 10)
        else:
            tasks[TASKS[code // 10 - 100]](code % 10)

    vectors(3)

    for name, tensor in tensors.items():
        tensor.end(name)
    links.sent(wo_all.at[0 : 3 * cols, :], s_wo)
    links.sent(heads_full.at[:, 0 : 3 * cols], s_heads)
    links.sent(second_low.at[0:half, :], s_second)
    links.sent(residual_low.at[0:half, :], s_back)
    for each in row_sums:
        each.end()
    for number, out in enumerate((block_out, token_grad)):
        links.got(out.at[other_rows, :], i_out + number)
    links.sent(first_low, s_out)
    links.sent(seven, s_vec[1])
    links.sent(seven, s_vec[2])


def results_kernel(cols, hidden, *refs):
    qkv, down, up, output, block, token, vec = refs[:7]
    outs, wide, small, sems = refs[7:22], refs[22:28], refs[28:35], refs[35]
    writes = [
        pltpu.make_async_copy(src, dst, sems.at[n])
        for n, (src, dst) in enumerate(zip((block, token, *wide, *small), outs, strict=True))
    ]
    writes[0].start()
    writes[1].start()
    small[0][...] = vec[6, 0:hidden]
    for n, ref in enumerate(small[1:]):
        ref[...] = vec[n, :]
    for write in writes[8:]:
        write.start()
    for n in range(3):
        wide[n][...] = qkv[:, n * cols : (n + 1) * cols].astype(F32)
        writes[2 + n].start()
    for n, grads in enumerate((down, up, output)):
        wide[3 + n][...] = grads[...].astype(F32)
        writes[5 + n].start()
    for write in writes:
        write.wait()


def kernel_shards(*args):
    tokens, lengths = args[0], args[1]
    n_rows, width = tokens.shape
    count = n_rows // lengths.shape[0]
    tile = 16 * count
    half = n_rows // 2
    cols = args[2].shape[1]
    hidden = args[6].shape[1]
    vmem = pltpu.VMEM
    grads = ((hidden, width), (width, hidden), (cols, width), (width, 3 * cols))
    halves = [(r // 2, n) for r, n in grads]
    any_space = pl.BlockSpec(memory_space=pl.ANY)
    in_vmem = pl.BlockSpec(memory_space=pltpu.VMEM)
    scratch = [vmem(args[n].shape, args[n].dtype) for n in (1, 7, 9, 10, 11, 12, 13, 14)]
    scratch += [
        vmem((n_rows, width), BF16),
        vmem((n_rows, width), BF16),
        vmem((width, cols), BF16),
        vmem((width, cols), BF16),
        vmem((width, cols), BF16),
        vmem((width, width), BF16),
        vmem((width, hidden), BF16),
        vmem((hidden, width), BF16),
        vmem((n_rows, width), BF16),
        vmem((n_rows, cols), BF16),
        vmem((n_rows, cols), BF16),
        vmem((n_rows, cols), BF16),
        vmem((n_rows // tile * (cols // DH), tile, tile), F32),
        vmem((n_rows, cols), BF16),
        vmem((half, width), BF16),
        vmem((half, width), F32),
        vmem((n_rows, width), BF16),
        vmem((n_rows, hidden), BF16),
        vmem((n_rows, hidden), BF16),
        vmem((11, half, width), BF16),
        vmem((half, width), F32),
        vmem((n_rows, width), BF16),
        vmem((n_rows, 3 * cols), BF16),
    ]
    scratch += [vmem(s, BF16) for s in grads]
    for shapes in (halves, grads, halves):
        scratch += [vmem(s, BF16) for s in shapes]
    scratch += [
        vmem((8, width), F32),
        vmem((8, width), F32),
        vmem((8, 8, width // 8), F32),
        vmem((8, width // 8), F32),
        pltpu.SemaphoreType.DMA((N_SENDS,)),
        pltpu.SemaphoreType.DMA((N_RECVS,)),
        pltpu.SemaphoreType.DMA((N_LOCAL,)),
    ]
    block_out, token_grad, down, up, output, qkv, vec = pl.pallas_call(
        functools.partial(layer_kernel, count),
        out_shape=[
            vmem((n_rows, width), BF16),
            vmem((n_rows, width), BF16),
            *[vmem(s, BF16) for s in grads],
            vmem((8, width), F32),
        ],
        in_specs=[any_space] * len(args),
        out_specs=[in_vmem] * 7,
        scratch_shapes=scratch,
        compiler_params=pltpu.CompilerParams(
            collective_id=0, has_side_effects=True, vmem_limit_bytes=56 * 2**20
        ),
        name="layer",
    )(*args)

    split = (width, cols)
    f32_grads = [split] * 3 + list(grads[:3])
    vector = jax.ShapeDtypeStruct((width,), F32)
    rows = (n_rows, width)
    block_out, token_grad, query, key, value, down, up, output, up_bias, *vectors = pl.pallas_call(
        functools.partial(results_kernel, cols, hidden),
        out_shape=[jax.ShapeDtypeStruct(rows, BF16)] * 2
        + [jax.ShapeDtypeStruct(s, F32) for s in f32_grads]
        + [jax.ShapeDtypeStruct((hidden,), F32)]
        + [vector] * 6,
        in_specs=[in_vmem] * 7,
        out_specs=[any_space] * 15,
        scratch_shapes=[vmem(s, F32) for s in (*f32_grads, (hidden,), *[(width,)] * 6)]
        + [pltpu.SemaphoreType.DMA((15,))],
        compiler_params=pltpu.CompilerParams(vmem_limit_bytes=16 * 2**20),
        name="results",
    )(qkv, down, up, output, block_out, token_grad, vec)
    return (
        block_out,
        token_grad,
        query,
        key,
        value,
        output,
        up,
        up_bias,
        down,
        *vectors,
    )


def solution(mesh):
    fits = mesh.shape["dp"] == 8 and mesh.shape["tensor"] == 4
    return jax.shard_map(
        kernel_shards if fits else plain_shards,
        mesh=mesh,
        in_specs=(
            P("dp", None),
            P("dp"),
            P(None, "tensor"),
            P(None, "tensor"),
            P(None, "tensor"),
            P("tensor", None),
            P(None, "tensor"),
            P("tensor"),
            P("tensor", None),
            P(),
            P(),
            P(),
            P(),
            P(),
            P(),
            P("dp", None),
        ),
        out_specs=(
            P("dp", None),
            P("dp", None),
            P(None, "tensor"),
            P(None, "tensor"),
            P(None, "tensor"),
            P("tensor", None),
            P(None, "tensor"),
            P("tensor"),
            P("tensor", None),
            P(),
            P(),
            P(),
            P(),
            P(),
            P(),
        ),
        check_vma=False,
    )
```

```python
import functools
import math

import jax
import jax.numpy as jnp
from jax import lax
from jax.experimental import pallas as pl
from jax.experimental.pallas import tpu as pltpu
from jax.sharding import PartitionSpec as P

DH = 128


EPS = 1e-05


def norm_parts(rows, gain, shift):
    row_mean = jnp.mean(rows, axis=-1, keepdims=True)
    centred = rows - row_mean
    inverse = lax.rsqrt(jnp.mean(centred * centred, axis=-1, keepdims=True) + EPS)
    scaled = centred * inverse
    return (scaled * gain + shift, scaled, inverse)


def norm_back(incoming, scaled, inverse, gain):
    weighted = incoming * gain
    return inverse * (
        weighted
        - jnp.mean(weighted, axis=-1, keepdims=True)
        - scaled * jnp.mean(weighted * scaled, axis=-1, keepdims=True)
    )


def allowed_mask(lengths, count):
    position = jnp.arange(count, dtype=jnp.int32)
    start = (count - lengths)[:, None, None]
    query_pos = position[None, :, None]
    key_pos = position[None, None, :]
    return (key_pos >= start) & (key_pos <= query_pos) | (key_pos == query_pos)


def gelu_exact(values):
    return jax.nn.gelu(values, approximate=False)


def plain_shards(
    tokens,
    lengths,
    query_weight,
    key_weight,
    value_weight,
    output_weight,
    up_weight,
    up_bias,
    down_weight,
    first_gain,
    first_shift,
    second_gain,
    second_shift,
    output_bias,
    down_bias,
    cotangent,
):
    tok_rows = tokens.shape[0]
    series = lengths.shape[0]
    count = tok_rows // series
    heads_here = query_weight.shape[1] // DH
    groups = lax.axis_size("tensor")
    share = tok_rows // groups
    begin = lax.axis_index("tensor") * share
    scale_factor = 1.0 / math.sqrt(DH)
    allowed = allowed_mask(lengths, count)[:, None]

    def share_rows(array):
        return lax.dynamic_slice_in_dim(array, begin, share, 0)

    def to_heads(array):
        return array.reshape(series, count, heads_here, DH)

    def masked_scores(query_four, key_four):
        raw = (
            jnp.einsum("sqhd,skhd->shqk", query_four, key_four, preferred_element_type=jnp.float32)
            * scale_factor
        )
        return jnp.where(allowed, raw, -1e30)

    inputs = tokens.astype(jnp.float32)
    gain_one = first_gain.astype(jnp.float32)
    gain_two = second_gain.astype(jnp.float32)
    first_normed, first_scaled, first_inverse = norm_parts(
        inputs, gain_one, first_shift.astype(jnp.float32)
    )
    first_low = first_normed.astype(jnp.bfloat16)
    queries = jnp.dot(first_low, query_weight, preferred_element_type=jnp.float32).astype(
        jnp.bfloat16
    )
    key_rows = jnp.dot(first_low, key_weight, preferred_element_type=jnp.float32).astype(
        jnp.bfloat16
    )
    value_rows = jnp.dot(first_low, value_weight, preferred_element_type=jnp.float32).astype(
        jnp.bfloat16
    )
    query_four = to_heads(queries)
    key_four = to_heads(key_rows)
    value_four = to_heads(value_rows)
    scores = masked_scores(query_four, key_four)
    row_max = jnp.max(scores, axis=-1, keepdims=True)
    numerator = jnp.exp(scores - row_max)
    row_total = jnp.sum(numerator, axis=-1, keepdims=True)
    log_total = row_max + jnp.log(row_total)
    probs_low = (numerator / row_total).astype(jnp.bfloat16)
    heads_out = jnp.einsum(
        "shqk,skhd->sqhd", probs_low, value_four, preferred_element_type=jnp.float32
    )
    heads_low = heads_out.astype(jnp.bfloat16).reshape(tok_rows, heads_here * DH)
    attn_part = jnp.dot(heads_low, output_weight, preferred_element_type=jnp.float32)
    bias_attn = output_bias.astype(jnp.float32)
    bias_down = down_bias.astype(jnp.float32)
    grad_output = cotangent.astype(jnp.float32)
    attn_share = lax.psum_scatter(attn_part, "tensor", scatter_dimension=0, tiled=True)
    residual_share = share_rows(inputs) + attn_share + bias_attn
    second_share, second_scaled, second_inverse = norm_parts(
        residual_share, gain_two, second_shift.astype(jnp.float32)
    )
    second_low = lax.all_gather(second_share.astype(jnp.bfloat16), "tensor", axis=0, tiled=True)
    up_pre = jnp.dot(second_low, up_weight, preferred_element_type=jnp.float32) + up_bias.astype(
        jnp.float32
    )
    activated, gelu_pull = jax.vjp(gelu_exact, up_pre)
    activated = activated.astype(jnp.bfloat16)
    down_part = jnp.dot(activated, down_weight, preferred_element_type=jnp.float32)
    down_share = lax.psum_scatter(
        down_part.astype(jnp.bfloat16), "tensor", scatter_dimension=0, tiled=True
    ).astype(jnp.float32)
    out_share = (residual_share + down_share + bias_down).astype(jnp.bfloat16)
    block_out = lax.all_gather(out_share, "tensor", axis=0, tiled=True)
    down_bias_part = jnp.sum(share_rows(grad_output), axis=0)
    down_grad = jnp.einsum("tf,td->fd", activated, cotangent, preferred_element_type=jnp.float32)
    activated_grad = jnp.einsum(
        "td,fd->tf", cotangent, down_weight, preferred_element_type=jnp.float32
    )
    up_grad_pre = gelu_pull(activated_grad)[0].astype(jnp.bfloat16)
    up_bias_grad = jnp.sum(up_grad_pre.astype(jnp.float32), axis=0)
    up_grad = jnp.einsum("td,tf->df", second_low, up_grad_pre, preferred_element_type=jnp.float32)
    second_part = jnp.einsum(
        "tf,df->td", up_grad_pre, up_weight, preferred_element_type=jnp.float32
    )
    second_grad_share = lax.psum_scatter(second_part, "tensor", scatter_dimension=0, tiled=True)
    residual_share_grad = share_rows(grad_output) + norm_back(
        second_grad_share, second_scaled, second_inverse, gain_two
    )
    second_gain_part = jnp.sum(second_grad_share * second_scaled, axis=0)
    second_shift_part = jnp.sum(second_grad_share, axis=0)
    output_bias_part = jnp.sum(residual_share_grad, axis=0)
    residual_low = lax.all_gather(
        residual_share_grad.astype(jnp.bfloat16), "tensor", axis=0, tiled=True
    )
    output_grad = jnp.einsum(
        "tc,td->cd", heads_low, residual_low, preferred_element_type=jnp.float32
    )
    heads_grad = jnp.einsum(
        "td,cd->tc", residual_low, output_weight, preferred_element_type=jnp.float32
    )
    heads_grad_four = to_heads(heads_grad.astype(jnp.bfloat16))
    probs_again = jnp.exp(masked_scores(query_four, key_four) - log_total)
    value_rows_grad = jnp.einsum(
        "shqk,sqhd->skhd", probs_low, heads_grad_four, preferred_element_type=jnp.float32
    ).astype(jnp.bfloat16)
    probs_grad = jnp.einsum(
        "sqhd,skhd->shqk", heads_grad_four, value_four, preferred_element_type=jnp.float32
    )
    inner_sum = jnp.sum(probs_again * probs_grad, axis=-1, keepdims=True)
    scores_grad = (probs_again * (probs_grad - inner_sum)).astype(jnp.bfloat16)
    queries_grad = (
        (
            jnp.einsum("shqk,skhd->sqhd", scores_grad, key_four, preferred_element_type=jnp.float32)
            * scale_factor
        )
        .astype(jnp.bfloat16)
        .reshape(tok_rows, heads_here * DH)
    )
    key_rows_grad = (
        (
            jnp.einsum(
                "shqk,sqhd->skhd", scores_grad, query_four, preferred_element_type=jnp.float32
            )
            * scale_factor
        )
        .astype(jnp.bfloat16)
        .reshape(tok_rows, heads_here * DH)
    )
    value_rows_grad = value_rows_grad.reshape(tok_rows, heads_here * DH)
    query_grad = jnp.einsum(
        "td,tc->dc", first_low, queries_grad, preferred_element_type=jnp.float32
    )
    key_grad = jnp.einsum("td,tc->dc", first_low, key_rows_grad, preferred_element_type=jnp.float32)
    value_grad = jnp.einsum(
        "td,tc->dc", first_low, value_rows_grad, preferred_element_type=jnp.float32
    )
    first_part = (
        jnp.einsum("tc,dc->td", queries_grad, query_weight, preferred_element_type=jnp.float32)
        + jnp.einsum("tc,dc->td", key_rows_grad, key_weight, preferred_element_type=jnp.float32)
        + jnp.einsum("tc,dc->td", value_rows_grad, value_weight, preferred_element_type=jnp.float32)
    )
    first_grad_share = lax.psum_scatter(
        first_part.astype(jnp.bfloat16), "tensor", scatter_dimension=0, tiled=True
    ).astype(jnp.float32)
    scaled_share = share_rows(first_scaled)
    token_share = residual_share_grad + norm_back(
        first_grad_share, scaled_share, share_rows(first_inverse), gain_one
    )
    token_grad = lax.all_gather(token_share.astype(jnp.bfloat16), "tensor", axis=0, tiled=True)
    first_gain_part = jnp.sum(first_grad_share * scaled_share, axis=0)
    first_shift_part = jnp.sum(first_grad_share, axis=0)
    query_grad, key_grad, value_grad, output_grad, up_grad, up_bias_grad, down_grad = (
        lax.psum(query_grad.astype(jnp.bfloat16), "dp").astype(jnp.float32),
        lax.psum(key_grad.astype(jnp.bfloat16), "dp").astype(jnp.float32),
        lax.psum(value_grad.astype(jnp.bfloat16), "dp").astype(jnp.float32),
        lax.psum(output_grad.astype(jnp.bfloat16), "dp").astype(jnp.float32),
        lax.psum(up_grad.astype(jnp.bfloat16), "dp").astype(jnp.float32),
        lax.psum(up_bias_grad.astype(jnp.bfloat16), "dp").astype(jnp.float32),
        lax.psum(down_grad.astype(jnp.bfloat16), "dp").astype(jnp.float32),
    )
    (
        first_gain_grad,
        first_shift_grad,
        second_gain_grad,
        second_shift_grad,
        output_bias_grad,
        down_bias_grad,
    ) = lax.psum(
        (
            first_gain_part,
            first_shift_part,
            second_gain_part,
            second_shift_part,
            output_bias_part,
            down_bias_part,
        ),
        ("dp", "tensor"),
    )
    return (
        block_out,
        token_grad,
        query_grad,
        key_grad,
        value_grad,
        output_grad,
        up_grad,
        up_bias_grad,
        down_grad,
        first_gain_grad,
        first_shift_grad,
        second_gain_grad,
        second_shift_grad,
        output_bias_grad,
        down_bias_grad,
    )


F32 = jnp.float32
BF16 = jnp.bfloat16
MESH = pl.DeviceIdType.MESH
N_LOCAL = 19

TASKS = "DUOQSTVWFGBAXYZHKPE"
PARTS = (
    ("D", 0, 64, "a"), ("D", 64, 64, "d"), ("D", 128, 64, "a"), ("D", 192, 64, "a"),
    ("D", 256, 64, "d"), ("D", 320, 64, "a"), ("D", 384, 64, "a"), ("D", 448, 64, "a"),
    ("U", 0, 128, "a"), ("U", 128, 128, "d"), ("U", 256, 128, "d"), ("U", 384, 128, "a"),
    ("U", 512, 128, "a"), ("U", 640, 128, "a"), ("U", 768, 128, "b"), ("U", 896, 128, "a"),
    ("O", 0, 64, "a"), ("O", 64, 64, "b"), ("O", 128, 64, "a"), ("O", 192, 64, "d"),
    ("Q", 0, 64, "d"), ("Q", 64, 64, "a"), ("Q", 128, 64, "a"), ("Q", 192, 64, "a"),
    ("Q", 256, 64, "a"), ("Q", 320, 64, "a"), ("Q", 384, 64, "a"), ("Q", 448, 64, "d"),
    ("Q", 512, 64, "a"), ("Q", 576, 64, "a"), ("Q", 640, 64, "d"), ("Q", 704, 64, "d"),
    ("Q", 768, 64, "a"), ("Q", 832, 64, "a"), ("Q", 896, 64, "a"), ("Q", 960, 64, "d"),
)
ORDER = (
    1150, 1151, 1160, 1161, 1162, 1163, 1170, 1171, 1182, 1181, 1040, 1180, 1183, 1011, 1001, 1050,
    1061, 101, 1041, 1000, 41, 1010, 11, 111, 1051, 102, 91, 1060, 61, 51, 42, 1013, 112, 1012, 12,
    71, 21, 62, 92, 31, 52, 43, 113, 1100, 141, 63, 151, 53, 72, 1, 103, 22, 1110, 32, 142, 121,
    93, 73, 152, 23, 81, 2, 1070, 64, 33, 122, 114, 143, 1111, 104, 153, 3, 82, 1080, 44, 131, 105,
    13, 54, 94, 1101, 123, 45, 74, 1112, 132, 34, 14, 83, 144, 24, 1113, 95, 1031, 106, 1030, 15,
    46, 1090, 1032, 201, 1081, 133, 271, 1033, 251, 311, 16, 96, 351, 301, 272, 252, 1020, 312,
    202, 211, 171, 1091, 124, 352, 281, 4, 191, 212, 253, 241, 302, 282, 261, 172, 321, 242, 313,
    192, 262, 213, 283, 322, 331, 332, 221, 243, 181, 263, 222, 291, 341, 353, 203, 182, 323, 1071,
    292, 303, 214, 173, 231, 193, 342, 354, 223, 333, 183, 204, 273, 244, 1130, 314, 161, 293, 355,
    264, 205, 232, 174, 324, 1131, 194, 1140, 343, 284, 162, 206, 305, 356, 1120, 275, 304, 274,
    154, 1141, 233, 195, 334, 254, 134, 184, 315, 224, 294, 163, 276, 306, 84, 1142, 1121, 316,
    344, 164, 196, 234,
)

N_ROWS = {name: sum(p[2] for p in PARTS if p[0] == name) for name in "DUOQ"}
N_SENDS = len({(p[0], p[3], p[1] * 3 // N_ROWS[p[0]]) for p in PARTS}) + 11
N_RECVS = 3 * len(PARTS) + 38


def dot(a, b):
    return jnp.dot(a, b, preferred_element_type=F32)


def dot_nt(a, b):
    return lax.dot_general(a, b, (((1,), (1,)), ((), ())), preferred_element_type=F32)


def dot_tn(a, b):
    return lax.dot_general(a, b, (((0,), (0,)), ((), ())), preferred_element_type=F32)


def span(start, size):
    return pl.ds(pl.multiple_of(start, 16), size)


def lanes(start, size):
    return pl.ds(pl.multiple_of(start, 128), size)


class Links:
    def __init__(self, sends, recvs, anyone):
        self.sends, self.recvs, self.anyone = sends, recvs, anyone
        self.used = [0, 0]

    def group(self):
        self.used[0] += 1
        assert self.used[0] <= N_SENDS
        return self.used[0] - 1

    def take(self, count=1):
        first = self.used[1]
        self.used[1] += count
        assert self.used[1] <= N_RECVS
        return first

    def copy(self, src, dst, group, index, device):
        return pltpu.make_async_remote_copy(
            src_ref=src,
            dst_ref=dst,
            send_sem=self.sends.at[group],
            recv_sem=self.recvs.at[index],
            device_id=device,
            device_id_type=MESH,
        )

    def got(self, dst, index):
        self.copy(dst, dst, 0, index, self.anyone).wait_recv()

    def sent(self, like, group):
        self.copy(like, like, group, 0, self.anyone).wait_send()


def layer_kernel(
    count,
    tokens_hbm,
    lengths_hbm,
    query_hbm,
    key_hbm,
    value_hbm,
    output_hbm,
    up_hbm,
    up_bias_hbm,
    down_hbm,
    first_gain_hbm,
    first_shift_hbm,
    second_gain_hbm,
    second_shift_hbm,
    output_bias_hbm,
    down_bias_hbm,
    cotangent_hbm,
    block_out,
    token_grad,
    down_out,
    up_out,
    output_out,
    qkv_out,
    vec_out,
    lengths,
    up_bias,
    first_gain,
    first_shift,
    second_gain,
    second_shift,
    output_bias,
    down_bias,
    tokens,
    cotangent,
    query_weight,
    key_weight,
    value_weight,
    wo_all,
    up_weight,
    down_weight,
    first_low,
    queries,
    key_rows,
    value_rows,
    probs,
    heads_own,
    heads_full,
    residual,
    second_low,
    act,
    ugp,
    mail,
    residual_grad,
    residual_low,
    dqkv,
    g_down,
    g_up,
    g_output,
    g_qkv,
    rx_down,
    rx_up,
    rx_output,
    rx_qkv,
    rz_down,
    rz_up,
    rz_output,
    rz_qkv,
    rm_down,
    rm_up,
    rm_output,
    rm_qkv,
    vec,
    vec_sib,
    vec_parts,
    vec_sum,
    sends,
    recvs,
    local_sems,
):
    n_rows, width = tokens.shape
    half = n_rows // 2
    tile = 16 * count
    n_tiles = n_rows // tile
    half_tiles = n_tiles // 2
    heads_here = query_weight.shape[1] // DH
    cols = heads_here * DH
    hidden = up_weight.shape[1]
    scale_factor = 1.0 / math.sqrt(DH)

    dp = lax.axis_index("dp")
    t = lax.axis_index("tensor")
    x = dp % 2
    z = dp // 2
    c = t % 2
    t_sib = t + 1 - 2 * c
    t_opp = (t + 2) % 4
    t_diag = (t_sib + 2) % 4
    sib = (dp, t_sib)
    opp = (dp, t_opp)
    diag = (dp, t_diag)
    xp = (dp + 1 - 2 * x, t)
    adj = (dp + 2 - 4 * (z % 2), t)
    cross = (dp + 2 - 4 * (z % 2) + 1 - 2 * x, t)
    mid = ((3 - z) * 2 + x, t)
    is_mid = jnp.logical_or(z == 1, z == 2)
    is_end = jnp.logical_or(z == 0, z == 3)
    side = z // 2
    dp_peers = [((dp + k) % 8, t) for k in range(1, 8)]
    links = Links(sends, recvs, sib)

    barrier = pltpu.get_barrier_semaphore()
    peers = [sib, opp, diag, (adj[0], t_sib), (xp[0], t_sib)] + dp_peers
    for peer in peers:
        pl.semaphore_signal(barrier, inc=1, device_id=peer, device_id_type=MESH)

    other_rows = span((1 - c) * half, half)
    own_start = c * half
    sib_start = (1 - c) * half
    own_wo = span(t * cols, cols)

    def turn_rows(i):
        return span((i % 2) * half + (i // 2) * tile, tile)

    def token_load(i):
        rows = turn_rows(i)
        return pltpu.make_async_copy(tokens_hbm.at[rows, :], tokens.at[rows, :], local_sems.at[i])

    loads = [
        pltpu.make_async_copy(src, dst, local_sems.at[n_tiles + n])
        for n, (src, dst) in enumerate(
            (
                (query_hbm, query_weight),
                (key_hbm, key_weight),
                (value_hbm, value_weight),
                (lengths_hbm, lengths),
                (first_gain_hbm, first_gain),
                (first_shift_hbm, first_shift),
                (output_hbm, wo_all.at[own_wo, :]),
                (output_bias_hbm, output_bias),
                (second_gain_hbm, second_gain),
                (second_shift_hbm, second_shift),
                (up_bias_hbm, up_bias),
                (down_bias_hbm, down_bias),
                (up_hbm, up_weight),
                (down_hbm, down_weight),
                (cotangent_hbm, cotangent),
            )
        )
    ]
    token_load(0).start()
    early = 6
    for load in loads[:early]:
        load.start()
    for i in range(1, n_tiles):
        token_load(i).start()
    for load in loads[early:]:
        load.start()

    def row(ref):
        return ref[...].astype(F32).reshape(1, ref.shape[0])

    def norm_parts(v):
        e = v - jnp.mean(v, axis=-1, keepdims=True)
        r = lax.rsqrt(jnp.mean(e * e, axis=-1, keepdims=True) + EPS)
        return e * r, r

    piece = cols // 4
    quarter = x + 2 * (z % 2)

    def wo_piece(owner, number):
        return wo_all.at[span(owner * cols + number * piece, piece), :]

    i_wo = links.take(7)
    s_wo = links.group()
    by_y = links.copy(
        output_hbm.at[span(quarter * piece, piece), :], wo_piece(t, quarter), s_wo, i_wo, opp
    )
    whole_to_sib = links.copy(output_hbm, wo_all.at[own_wo, :], s_wo, i_wo + 1, sib)
    q_xp, q_adj = quarter + 1 - 2 * x, quarter + 2 - 4 * (z % 2)
    q_cross = q_adj + 1 - 2 * x
    mine = wo_piece(t_opp, quarter)
    to_x = links.copy(mine, mine, s_wo, i_wo + 2, xp)
    to_z = links.copy(mine, mine, s_wo, i_wo + 3, adj)

    def half_piece(number, which):
        return wo_all.at[span(t_opp * cols + number * piece + which * piece // 2, piece // 2), :]

    from_x, from_z = half_piece(q_xp, 0), half_piece(q_adj, 1)
    on_z = [links.copy(from_x, from_x, s_wo, i_wo + 4, (adj[0], v)) for v in (t, t_sib)]
    on_x = [links.copy(from_z, from_z, s_wo, i_wo + 5, (xp[0], v)) for v in (t, t_sib)]

    def relay(number):
        part = wo_piece(t_opp, number)
        links.copy(part, part, s_wo, i_wo + 6, sib).start()

    def share_first():
        links.got(mine, i_wo)
        to_x.start()
        to_z.start()
        relay(quarter)

    def share_next():
        links.got(wo_piece(t_opp, q_xp), i_wo + 2)
        for each in on_z:
            each.start()
        links.got(wo_piece(t_opp, q_adj), i_wo + 3)
        for each in on_x:
            each.start()
        relay(q_xp)
        relay(q_adj)

    def share_last():
        links.got(wo_piece(t_opp, q_cross), i_wo + 4)
        links.got(wo_piece(t_diag, q_cross), i_wo + 5)
        links.got(wo_all.at[span(t_diag * cols, 3 * piece), :], i_wo + 6)

    pl.semaphore_wait(barrier, len(peers))
    by_y.start()
    whole_to_sib.start()

    def allowed_of(number):
        def series_of(index):
            return jnp.floor((index + 0.5) * (1.0 / count))

        row_at = lax.broadcasted_iota(jnp.int32, (tile, 1), 0).astype(F32)
        col_at = lax.broadcasted_iota(jnp.int32, (1, tile), 1).astype(F32)
        row_series, col_series = series_of(row_at), series_of(col_at)
        n_series = lengths.shape[0]
        which = lax.broadcasted_iota(jnp.int32, (n_series, tile), 0).astype(F32)
        here = (which == col_series + (number * 16).astype(F32)).astype(BF16)
        all_lengths = jnp.broadcast_to(
            lengths[...].astype(F32).reshape(1, n_series), (8, n_series)
        ).astype(BF16)
        length = dot(all_lengths, here)[0:1, :]
        live = (col_at - count * col_series) >= (count - length)
        same = row_series == col_series
        seen = jnp.logical_and(live, col_at <= row_at)
        return jnp.logical_and(same, jnp.logical_or(seen, col_at == row_at))

    i_heads = links.take(2 * half_tiles + 1)
    i_near = i_heads + half_tiles + 1
    s_heads = links.group()

    def head_slot(j):
        return span(j * tile, tile)

    cut = tile // 32 * 16 + 16
    pieces = [[(0, tile)]] * (half_tiles - 1) + [[(0, cut), (cut, tile - cut)]]

    def attend(i, _):
        h, j = i % 2, i // 2
        number = h * half_tiles + j
        rows = turn_rows(i)
        token_load(i).wait()

        @pl.when(i == 0)
        def _():
            for load in loads[:early]:
                load.wait()

        xhat, _r = norm_parts(tokens[rows, :].astype(F32))
        first_low[rows, :] = (xhat * row(first_gain) + row(first_shift)).astype(BF16)

        normed = first_low[rows, :]
        q = dot(normed, query_weight[...]).astype(BF16)
        k = dot(normed, key_weight[...]).astype(BF16)
        v = dot(normed, value_weight[...]).astype(BF16)
        queries[rows, :] = q
        key_rows[rows, :] = k
        value_rows[rows, :] = v

        allowed = allowed_of(number)
        for head in range(heads_here):
            at = slice(head * DH, (head + 1) * DH)
            scores = jnp.where(allowed, dot_nt(q[:, at], k[:, at]) * scale_factor, -1e30)
            numerator = jnp.exp(scores - jnp.max(scores, axis=-1, keepdims=True))
            share = numerator / jnp.sum(numerator, axis=-1, keepdims=True)
            probs[number * heads_here + head] = share
            heads_own[rows, at] = dot(share.astype(BF16), v[:, at]).astype(BF16)
        mine = lanes(t * cols, cols)
        slot = heads_full.at[head_slot(j), mine]

        def over_y(device):
            @pl.when(j < half_tiles - 1)
            def _():
                links.copy(heads_own.at[rows, :], slot, s_heads, i_heads + j, device).start()

            @pl.when(j == half_tiles - 1)
            def _():
                for n, (start, size) in enumerate(pieces[-1]):
                    links.copy(
                        heads_own.at[span(h * half + j * tile + start, size), :],
                        heads_full.at[span(j * tile + start, size), mine],
                        s_heads,
                        i_heads + j + n,
                        device,
                    ).start()

        @pl.when(h == c)
        def _():
            heads_full[head_slot(j), mine] = heads_own[rows, :]
            over_y(opp)

        @pl.when(h != c)
        def _():
            links.copy(heads_own.at[rows, :], slot, s_heads, i_near + j, sib).start()
            over_y(diag)

        @pl.when(i == 1)
        def _():
            share_first()

        return 0

    lax.fori_loop(0, n_tiles, attend, 0)

    share_next()

    i_second = links.take(half_tiles + 1)
    s_second = links.group()
    vec[...] = jnp.zeros_like(vec)

    def in_turn(i):
        return jnp.where(i % 2 == 0, own_start, sib_start) + (i // 2) * tile

    chip = 2 * cols
    own_k, other_k = lanes((t // 2) * chip, chip), lanes((1 - t // 2) * chip, chip)

    def prepare(j):
        here = head_slot(j)
        if j == 0:
            for load in loads[early:]:
                load.wait()
            links.got(wo_all.at[span(t_sib * cols, cols), :], i_wo + 1)
        links.got(heads_full.at[here, lanes(t_sib * cols, cols)], i_near + j)
        residual[here, :] = dot(heads_full[here, own_k], wo_all[span((t // 2) * chip, chip), :])

    def down_slot(i):
        return residual_grad.at[head_slot(i // 2), (i % 2) * hidden : (i % 2 + 1) * hidden]

    def prepare_feed(i):
        down_slot(i)[...] = dot_nt(cotangent[span(in_turn(i), tile), :], down_weight[...])

    def feed(i):
        here = pieces[i // 2] if i % 2 == 1 else [(0, tile)]
        for n, (start, size) in enumerate(here):
            rows = span(in_turn(i) + start, size)
            if i % 2 == 1:
                links.got(second_low.at[rows, :], i_second + i // 2 + n)
            u = dot(second_low[rows, :], up_weight[...]) + row(up_bias)
            big = 0.5 * (1.0 + lax.erf(u * (1.0 / math.sqrt(2.0))))
            act[rows, :] = (u * big).astype(BF16)
            slope = big + u * (jnp.exp(-0.5 * u * u) * (1.0 / math.sqrt(2.0 * math.pi)))
            grad = (down_slot(i)[start : start + size, :] * slope).astype(BF16)
            ugp[rows, :] = grad
            vec[6:7, 0:hidden] += jnp.sum(grad.astype(F32), axis=0, keepdims=True)

    def project(j):
        if j == 0:
            share_last()
        for n, (start, size) in enumerate(pieces[j]):
            here = span(j * tile + start, size)
            links.got(heads_full.at[here, other_k], i_heads + j + n)
            rows = span(own_start + j * tile + start, size)
            other = dot(heads_full[here, other_k], wo_all[span((1 - t // 2) * chip, chip), :])
            v = tokens[rows, :].astype(F32) + (residual[here, :] + other) + row(output_bias)
            residual[here, :] = v
            xhat, _r = norm_parts(v)
            second_low[rows, :] = (xhat * row(second_gain) + row(second_shift)).astype(BF16)
            links.copy(
                second_low.at[rows, :], second_low.at[rows, :], s_second, i_second + j + n, sib
            ).start()

    class Tensor:
        def __init__(self, grads, rx, rz, rm, out, long):
            self.grads, self.rx, self.rz, self.rm, self.out = grads, rx, rz, rm, out
            self.long = long
            self.final = links.take()
            self.groups = {}

        def group_of(self, kind, start):
            key = kind, start * 3 // self.grads.shape[0]
            if key not in self.groups:
                self.groups[key] = links.group()
            return self.groups[key]

        def end(self, name):
            mine = [p for p in PARTS if p[0] == name]
            halves = {kind: sum(p[2] // 2 for p in mine if p[3] == kind) for kind in "abcdh"}
            for here, copies, came in (
                (is_mid, {"a": 4, "b": 5, "c": 4, "d": 4, "h": 4}, {"a": 1, "b": 0, "c": 1, "d": 0, "h": 1}),
                (is_end, {"a": 3, "b": 2, "c": 3, "d": 3, "h": 3}, {"a": 1, "b": 2, "c": 1, "d": 1, "h": 1}),
            ):

                @pl.when(here)
                def _(copies=copies, came=came):
                    rows = sum(came[kind] * halves[kind] for kind in "abcdh")
                    assert rows <= self.long.shape[0]
                    if rows > 0:
                        links.got(self.long.at[0:rows, :], self.final)
                    for (kind, which), group in self.groups.items():
                        rows = sum(
                            copies[kind] * p[2] // 2
                            for p in mine
                            if p[3] == kind and p[1] * 3 // self.grads.shape[0] == which
                        )
                        assert rows <= self.long.shape[0]
                        links.sent(self.long.at[0:rows, :], group)

    tensors = {
        "D": Tensor(g_down, rx_down, rz_down, rm_down, down_out, wo_all),
        "U": Tensor(g_up, rx_up, rz_up, rm_up, up_out, up_weight),
        "O": Tensor(g_output, rx_output, rz_output, rm_output, output_out, wo_all),
        "Q": Tensor(g_qkv, rx_qkv, rz_qkv, rm_qkv, qkv_out, dqkv),
    }

    class Part:
        def __init__(self, tensor, start, size, kind):
            self.size = size // 2
            self.start = start
            here = pl.ds(start // 2, self.size)
            self.grads, self.out = tensor.grads, tensor.out
            self.rx, self.rm = tensor.rx.at[here, :], tensor.rm.at[here, :]
            self.rz = tensor.rz.at[pl.ds(start, self.size), :]
            self.rz_whole = tensor.rz.at[pl.ds(start, size), :]
            self.index = links.take(3)
            self.final = tensor.final
            self.group = tensor.group_of(kind, start)

        def half_at(self, which):
            return span(self.start + which * self.size, self.size)

        def send(self, src, dst, message, device):
            links.copy(src, dst, self.group, self.index + message, device).start()

        def send_last(self, ref, device):
            links.copy(ref, ref, self.group, self.final, device).start()

        def got(self, dst, message):
            links.got(dst, self.index + message)

        def add(self, rows, came):
            return (self.grads[rows, :].astype(F32) + came[...].astype(F32)).astype(BF16)

    class PartX(Part):
        def begin(self):
            self.send(self.grads.at[self.half_at(1 - x), :], self.rx, 0, xp)

        def step(self, number):
            mine = self.half_at(x)
            grads, out = self.grads.at[mine, :], self.out.at[mine, :]
            if number == 1:
                self.got(self.rx, 0)
                self.grads[mine, :] = self.add(mine, self.rx)

                @pl.when(is_end)
                def _():
                    self.send(grads, self.rz, 1, adj)

            if number == 2:

                @pl.when(is_mid)
                def _():
                    self.got(self.rz, 1)
                    self.grads[mine, :] = self.add(mine, self.rz)
                    self.send(grads, self.rm, 2, mid)

            if number == 3:

                @pl.when(is_mid)
                def _():
                    self.got(self.rm, 2)
                    self.out[mine, :] = self.add(mine, self.rm)
                    self.send(out, out, 1, adj)
                    self.send_last(out, xp)

            if number == 4:

                @pl.when(is_end)
                def _():
                    self.got(out, 1)
                    self.send_last(out, xp)

    class PartE(Part):
        def begin(self):
            self.send(self.grads.at[self.half_at(1 - x), :], self.rx, 0, xp)

        def step(self, number):
            size = self.size // 2
            mine = self.half_at(x)
            near = span(self.start + x * self.size + side * size, size)
            far = span(self.start + x * self.size + (1 - side) * size, size)
            near_out, far_out = self.out.at[near, :], self.out.at[far, :]
            rz, rm = self.rz.at[0:size, :], self.rm.at[0:size, :]
            if number == 1:
                self.got(self.rx, 0)
                self.grads[mine, :] = self.add(mine, self.rx)

            @pl.when(is_end if number in (1, 4, 7) else is_mid)
            def _():
                if number == 1:
                    self.send(self.grads.at[far, :], rz, 1, adj)
                if number == 2:
                    self.got(rz, 1)
                    self.grads[far, :] = self.add(far, rz)
                    self.send(self.grads.at[far, :], rm, 2, mid)
                if number == 3:
                    self.got(rm, 2)
                    self.grads[near, :] = self.add(near, rm)
                    self.send(self.grads.at[near, :], rz, 1, adj)
                if number == 4:
                    self.got(rz, 1)
                    self.out[near, :] = self.add(near, rz)
                    self.send(near_out, near_out, 0, adj)
                    self.send_last(near_out, xp)
                if number == 5:
                    self.got(near_out, 0)
                    self.send(near_out, near_out, 1, mid)
                    self.send_last(near_out, xp)
                if number == 6:
                    self.got(far_out, 1)
                    self.send(far_out, far_out, 0, adj)
                    self.send_last(far_out, xp)
                if number == 7:
                    self.got(far_out, 0)
                    self.send_last(far_out, xp)

    class PartH(Part):
        def begin(self):
            @pl.when(is_end)
            def _():
                whole = self.grads.at[pl.ds(self.start, 2 * self.size), :]
                self.send(whole, self.rz_whole, 0, adj)

        def step(self, number):
            size = self.size // 2
            near, far = self.half_at(side), self.half_at(1 - side)
            near_at = self.start + side * self.size
            far_at = self.start + (1 - side) * self.size
            near_mine = span(near_at + x * size, size)
            near_other = span(near_at + (1 - x) * size, size)
            far_mine = span(far_at + x * size, size)
            near_out, far_out = self.out.at[near_mine, :], self.out.at[far_mine, :]
            rx = self.rx.at[0:size, :]

            @pl.when(is_end if number > 4 else is_mid)
            def _():
                if number == 1:
                    whole = pl.ds(self.start, 2 * self.size)
                    self.got(self.rz_whole, 0)
                    self.grads[whole, :] = self.add(whole, self.rz_whole)
                    self.send(self.grads.at[far, :], self.rm, 1, mid)
                if number == 2:
                    self.got(self.rm, 1)
                    self.grads[near, :] = self.add(near, self.rm)
                    self.send(self.grads.at[near_other, :], rx, 2, xp)
                if number == 3:
                    self.got(rx, 2)
                    self.out[near_mine, :] = self.add(near_mine, rx)
                    self.send(near_out, near_out, 0, adj)
                    self.send(near_out, near_out, 0, mid)
                    self.send_last(near_out, xp)
                if number == 4:
                    self.got(far_out, 0)
                    self.send(far_out, far_out, 1, adj)
                    self.send_last(far_out, xp)
                if number == 5:
                    self.got(near_out, 0)
                    self.send_last(near_out, xp)
                if number == 6:
                    self.got(far_out, 1)
                    self.send_last(far_out, xp)

    class PartZ(Part):
        def begin(self):
            far = self.grads.at[self.half_at(1 - side), :]

            @pl.when(is_end)
            def _():
                self.send(far, self.rz, 0, adj)

        def step(self, number):
            near, far = self.half_at(side), self.half_at(1 - side)
            near_out, far_out = self.out.at[near, :], self.out.at[far, :]

            @pl.when(is_end if number in (3, 4) else is_mid)
            def _():
                if number == 1:
                    self.got(self.rz, 0)
                    self.grads[far, :] = self.add(far, self.rz)
                    self.send(self.grads.at[far, :], self.rm, 1, mid)
                if number == 2:
                    self.got(self.rm, 1)
                    self.grads[near, :] = self.add(near, self.rm)
                    self.send(self.grads.at[near, :], self.rz, 0, adj)
                if number == 3:
                    self.got(self.rz, 0)
                    self.grads[near, :] = self.add(near, self.rz)
                    self.send(self.grads.at[near, :], self.rx, 1, xp)
                if number == 4:
                    self.got(self.rx, 1)
                    self.out[near, :] = self.add(near, self.rx)
                    self.send(near_out, near_out, 0, adj)
                if number == 5:
                    self.got(near_out, 0)
                    self.send(near_out, near_out, 2, mid)
                if number == 6:
                    self.got(far_out, 2)
                    self.send_last(far_out, adj)

    class PartM(Part):
        def begin(self):
            @pl.when(is_end)
            def _():
                whole = self.grads.at[pl.ds(self.start, 2 * self.size), :]
                self.send(whole, self.rz_whole, 0, adj)

        def step(self, number):
            near, far = self.half_at(side), self.half_at(1 - side)
            near_out, far_out = self.out.at[near, :], self.out.at[far, :]

            @pl.when(is_mid)
            def _():
                if number == 1:
                    whole = pl.ds(self.start, 2 * self.size)
                    self.got(self.rz_whole, 0)
                    self.grads[whole, :] = self.add(whole, self.rz_whole)
                    self.send(self.grads.at[far, :], self.rm, 1, mid)
                if number == 2:
                    self.got(self.rm, 1)
                    self.grads[near, :] = self.add(near, self.rm)
                    self.send(self.grads.at[near, :], self.rx, 2, xp)
                if number == 3:
                    self.got(self.rx, 2)
                    self.out[near, :] = self.add(near, self.rx)
                    self.send_last(near_out, adj)
                    self.send(near_out, near_out, 0, mid)
                if number == 4:
                    self.got(far_out, 0)
                    self.send_last(far_out, adj)

    parts = [
        {"a": PartX, "b": PartM, "c": PartE, "d": PartZ, "h": PartH}[kind](tensors[name], start, size, kind)
        for name, start, size, kind in PARTS
    ]

    def begin_parts(name, first, size):
        for (which, start, rows, _kind), part in zip(PARTS, parts, strict=True):
            if which == name and first < start + rows <= first + size:
                part.begin()

    block = 256

    def down_grads(i):
        at = slice(i * block, (i + 1) * block)
        g_down[at, :] = dot_tn(act[:, at], cotangent[...]).astype(BF16)
        begin_parts("D", i * block, block)

    def up_grads(i):
        at = slice(i * block, (i + 1) * block)
        g_up[at, :] = dot_tn(second_low[:, at], ugp[...]).astype(BF16)
        begin_parts("U", i * block, block)

    def output_grads(_i):
        g_output[...] = dot_tn(heads_own[...], residual_low[...]).astype(BF16)
        begin_parts("O", 0, cols)

    def qkv_grads(i):
        at = slice(i * block, (i + 1) * block)
        g_qkv[at, :] = dot_tn(first_low[:, at], dqkv[...]).astype(BF16)
        begin_parts("Q", i * block, block)

    class RowSum:
        def __init__(self, number, part, snd):
            self.snd = snd
            self.r1, self.cs, self.r2 = (mail.at[3 * number + n] for n in range(3))
            self.part = part
            self.index = links.take(2 * half_tiles)
            self.group = links.group()

        def far(self, j):
            here = head_slot(j)
            self.snd[here, :] = self.part(span(sib_start + j * tile, tile)).astype(BF16)
            links.copy(
                self.snd.at[here, :], self.r1.at[here, :], self.group, self.index + j, sib
            ).start()

        def near(self, j):
            here = head_slot(j)
            mine = self.part(span(own_start + j * tile, tile))
            links.got(self.r1.at[here, :], self.index + j)
            self.cs[here, :] = (mine + self.r1[here, :].astype(F32)).astype(BF16)
            links.copy(
                self.cs.at[here, :],
                self.r2.at[here, :],
                self.group,
                self.index + half_tiles + j,
                opp,
            ).start()

        def rows(self, j):
            here = head_slot(j)
            links.got(self.r2.at[here, :], self.index + half_tiles + j)
            return self.cs[here, :].astype(F32) + self.r2[here, :].astype(F32)

        def end(self):
            links.sent(first_low, self.group)

    second_sum = RowSum(0, lambda rows: dot_nt(ugp[rows, :], up_weight[...]), mail.at[9])
    out_sum = RowSum(1, lambda rows: dot(act[rows, :], down_weight[...]), mail.at[10])
    first_sum = RowSum(
        2,
        lambda rows: dot_nt(dqkv[rows, 0:cols], query_weight[...])
        + dot_nt(dqkv[rows, cols : 2 * cols], key_weight[...])
        + dot_nt(dqkv[rows, 2 * cols : 3 * cols], value_weight[...]),
        heads_full,
    )
    row_sums = (second_sum, out_sum, first_sum)

    i_back = links.take(half_tiles)
    s_back = links.group()

    def add_to(at, value):
        vec[at : at + 1, :] += jnp.sum(value, axis=0, keepdims=True)

    def norm_back(incoming, xhat, r, gain):
        weighted = incoming * gain
        return r * (
            weighted
            - jnp.mean(weighted, axis=-1, keepdims=True)
            - xhat * jnp.mean(weighted * xhat, axis=-1, keepdims=True)
        )

    def second_back(j):
        local = head_slot(j)
        rows = span(own_start + j * tile, tile)
        incoming = second_sum.rows(j)
        xhat, r = norm_parts(residual[local, :])
        given = cotangent[rows, :].astype(F32)
        grad = given + norm_back(incoming, xhat, r, row(second_gain))
        residual_grad[local, :] = grad
        residual_low[rows, :] = grad.astype(BF16)
        links.copy(
            residual_low.at[rows, :], residual_low.at[rows, :], s_back, i_back + j, sib
        ).start()
        add_to(2, incoming * xhat)
        add_to(3, incoming)
        add_to(4, grad)
        add_to(5, given)

    def attend_back(i):
        start = in_turn(i)
        rows = span(start, tile)
        number = start // tile
        if i % 2 == 1:
            links.got(residual_low.at[rows, :], i_back + i // 2)
        grads = dot_nt(residual_low[rows, :], wo_all[own_wo, :]).astype(BF16)
        for head in range(heads_here):
            at = slice(head * DH, (head + 1) * DH)
            share = probs[number * heads_here + head]
            q, k, v = queries[rows, at], key_rows[rows, at], value_rows[rows, at]
            share_grad = dot_nt(grads[:, at], v)
            inner = jnp.sum(share * share_grad, axis=-1, keepdims=True)
            scores_grad = (share * (share_grad - inner)).astype(BF16)
            dqkv[rows, head * DH : (head + 1) * DH] = (
                dot(scores_grad, k) * scale_factor
            ).astype(BF16)
            dqkv[rows, cols + head * DH : cols + (head + 1) * DH] = (
                dot_tn(scores_grad, q) * scale_factor
            ).astype(BF16)
            dqkv[rows, 2 * cols + head * DH : 2 * cols + (head + 1) * DH] = dot_tn(
                share.astype(BF16), grads[:, at]
            ).astype(BF16)

    i_out = links.take(2)
    s_out = links.group()

    def finished(j, number, out, values):
        rows = span(own_start + j * tile, tile)
        out[rows, :] = values.astype(BF16)
        links.copy(out.at[rows, :], out.at[rows, :], s_out, i_out + number, sib).start()

    def finish_out(j):
        local = head_slot(j)
        finished(j, 0, block_out, residual[local, :] + out_sum.rows(j) + row(down_bias))

    def first_back(j):
        local = head_slot(j)
        rows = span(own_start + j * tile, tile)
        incoming = first_sum.rows(j)
        xhat, r = norm_parts(tokens[rows, :].astype(F32))
        grad = residual_grad[local, :] + norm_back(incoming, xhat, r, row(first_gain))
        finished(j, 1, token_grad, grad)
        add_to(0, incoming * xhat)
        add_to(1, incoming)

    i_vec = links.take(3)
    s_vec = [links.group() for _ in range(3)]
    part = width // 8
    mine_at = lanes(dp * part, part)
    seven = vec_parts.at[0:7]

    def vectors(number):
        if number == 0:
            links.copy(vec, vec_sib, s_vec[0], i_vec, sib).start()
        if number == 1:
            links.got(vec_sib, i_vec)
            links.sent(vec, s_vec[0])
            at_row = lax.broadcasted_iota(jnp.int32, vec.shape, 0)
            vec[...] = vec[...] + jnp.where(at_row < 6, vec_sib[...], 0.0)
            vec_parts[dp] = vec[:, mine_at]
            for peer in dp_peers:
                links.copy(
                    vec.at[:, lanes(peer[0] * part, part)],
                    vec_parts.at[dp],
                    s_vec[1],
                    i_vec + 1,
                    peer,
                ).start()
        if number == 2:
            links.got(seven, i_vec + 1)
            total = vec_parts[0]
            for k in range(1, 8):
                total = total + vec_parts[k]
            vec_sum[...] = total
            vec_out[:, mine_at] = total
            for peer in dp_peers:
                links.copy(vec_sum, vec_out.at[:, mine_at], s_vec[2], i_vec + 2, peer).start()
        if number == 3:
            links.got(seven, i_vec + 2)

    tasks = {
        "D": down_grads,
        "U": up_grads,
        "O": output_grads,
        "Q": qkv_grads,
        "S": second_sum.far,
        "T": second_sum.near,
        "V": out_sum.far,
        "W": out_sum.near,
        "F": first_sum.far,
        "G": first_sum.near,
        "B": second_back,
        "A": attend_back,
        "X": finish_out,
        "Y": first_back,
        "Z": vectors,
        "H": prepare,
        "K": prepare_feed,
        "P": project,
        "E": feed,
    }
    for code in ORDER:
        if code < 1000:
            parts[code // 10].step(code % 10)
        else:
            tasks[TASKS[code // 10 - 100]](code % 10)

    vectors(3)

    for name, tensor in tensors.items():
        tensor.end(name)
    links.sent(wo_all.at[0 : 3 * cols, :], s_wo)
    links.sent(heads_full.at[:, 0 : 3 * cols], s_heads)
    links.sent(second_low.at[0:half, :], s_second)
    links.sent(residual_low.at[0:half, :], s_back)
    for each in row_sums:
        each.end()
    for number, out in enumerate((block_out, token_grad)):
        links.got(out.at[other_rows, :], i_out + number)
    links.sent(first_low, s_out)
    links.sent(seven, s_vec[1])
    links.sent(seven, s_vec[2])


def results_kernel(cols, hidden, *refs):
    qkv, down, up, output, block, token, vec = refs[:7]
    outs, wide, small, sems = refs[7:22], refs[22:28], refs[28:35], refs[35]
    writes = [
        pltpu.make_async_copy(src, dst, sems.at[n])
        for n, (src, dst) in enumerate(zip((block, token, *wide, *small), outs, strict=True))
    ]
    writes[0].start()
    writes[1].start()
    small[0][...] = vec[6, 0:hidden]
    for n, ref in enumerate(small[1:]):
        ref[...] = vec[n, :]
    for write in writes[8:]:
        write.start()
    for n in range(3):
        wide[n][...] = qkv[:, n * cols : (n + 1) * cols].astype(F32)
        writes[2 + n].start()
    for n, grads in enumerate((down, up, output)):
        wide[3 + n][...] = grads[...].astype(F32)
        writes[5 + n].start()
    for write in writes:
        write.wait()


def kernel_shards(*args):
    tokens, lengths = args[0], args[1]
    n_rows, width = tokens.shape
    count = n_rows // lengths.shape[0]
    tile = 16 * count
    half = n_rows // 2
    cols = args[2].shape[1]
    hidden = args[6].shape[1]
    vmem = pltpu.VMEM
    grads = ((hidden, width), (width, hidden), (cols, width), (width, 3 * cols))
    halves = [(r // 2, n) for r, n in grads]
    any_space = pl.BlockSpec(memory_space=pl.ANY)
    in_vmem = pl.BlockSpec(memory_space=pltpu.VMEM)
    scratch = [vmem(args[n].shape, args[n].dtype) for n in (1, 7, 9, 10, 11, 12, 13, 14)]
    scratch += [
        vmem((n_rows, width), BF16),
        vmem((n_rows, width), BF16),
        vmem((width, cols), BF16),
        vmem((width, cols), BF16),
        vmem((width, cols), BF16),
        vmem((width, width), BF16),
        vmem((width, hidden), BF16),
        vmem((hidden, width), BF16),
        vmem((n_rows, width), BF16),
        vmem((n_rows, cols), BF16),
        vmem((n_rows, cols), BF16),
        vmem((n_rows, cols), BF16),
        vmem((n_rows // tile * (cols // DH), tile, tile), F32),
        vmem((n_rows, cols), BF16),
        vmem((half, width), BF16),
        vmem((half, width), F32),
        vmem((n_rows, width), BF16),
        vmem((n_rows, hidden), BF16),
        vmem((n_rows, hidden), BF16),
        vmem((11, half, width), BF16),
        vmem((half, width), F32),
        vmem((n_rows, width), BF16),
        vmem((n_rows, 3 * cols), BF16),
    ]
    scratch += [vmem(s, BF16) for s in grads]
    for shapes in (halves, grads, halves):
        scratch += [vmem(s, BF16) for s in shapes]
    scratch += [
        vmem((8, width), F32),
        vmem((8, width), F32),
        vmem((8, 8, width // 8), F32),
        vmem((8, width // 8), F32),
        pltpu.SemaphoreType.DMA((N_SENDS,)),
        pltpu.SemaphoreType.DMA((N_RECVS,)),
        pltpu.SemaphoreType.DMA((N_LOCAL,)),
    ]
    block_out, token_grad, down, up, output, qkv, vec = pl.pallas_call(
        functools.partial(layer_kernel, count),
        out_shape=[
            vmem((n_rows, width), BF16),
            vmem((n_rows, width), BF16),
            *[vmem(s, BF16) for s in grads],
            vmem((8, width), F32),
        ],
        in_specs=[any_space] * len(args),
        out_specs=[in_vmem] * 7,
        scratch_shapes=scratch,
        compiler_params=pltpu.CompilerParams(
            collective_id=0, has_side_effects=True, vmem_limit_bytes=56 * 2**20
        ),
        name="layer",
    )(*args)

    split = (width, cols)
    f32_grads = [split] * 3 + list(grads[:3])
    vector = jax.ShapeDtypeStruct((width,), F32)
    rows = (n_rows, width)
    block_out, token_grad, query, key, value, down, up, output, up_bias, *vectors = pl.pallas_call(
        functools.partial(results_kernel, cols, hidden),
        out_shape=[jax.ShapeDtypeStruct(rows, BF16)] * 2
        + [jax.ShapeDtypeStruct(s, F32) for s in f32_grads]
        + [jax.ShapeDtypeStruct((hidden,), F32)]
        + [vector] * 6,
        in_specs=[in_vmem] * 7,
        out_specs=[any_space] * 15,
        scratch_shapes=[vmem(s, F32) for s in (*f32_grads, (hidden,), *[(width,)] * 6)]
        + [pltpu.SemaphoreType.DMA((15,))],
        compiler_params=pltpu.CompilerParams(vmem_limit_bytes=16 * 2**20),
        name="results",
    )(qkv, down, up, output, block_out, token_grad, vec)
    return (
        block_out,
        token_grad,
        query,
        key,
        value,
        output,
        up,
        up_bias,
        down,
        *vectors,
    )


def solution(mesh):
    fits = mesh.shape["dp"] == 8 and mesh.shape["tensor"] == 4
    return jax.shard_map(
        kernel_shards if fits else plain_shards,
        mesh=mesh,
        in_specs=(
            P("dp", None),
            P("dp"),
            P(None, "tensor"),
            P(None, "tensor"),
            P(None, "tensor"),
            P("tensor", None),
            P(None, "tensor"),
            P("tensor"),
            P("tensor", None),
            P(),
            P(),
            P(),
            P(),
            P(),
            P(),
            P("dp", None),
        ),
        out_specs=(
            P("dp", None),
            P("dp", None),
            P(None, "tensor"),
            P(None, "tensor"),
            P(None, "tensor"),
            P("tensor", None),
            P(None, "tensor"),
            P("tensor"),
            P("tensor", None),
            P(),
            P(),
            P(),
            P(),
            P(),
            P(),
        ),
        check_vma=False,
    )
```
